32 devices in a mesh: dp: 8 (over y, x, core), mp: 4 (over z).
Axes of the slice: x: 2, y: 2, z: 4, core: 2. Of those that a mesh axis runs over, the one named last changes fastest.
Arguments:
- block_in: bfloat16 [16384, 1536], P(('dp', 'mp')), may hold values from -12 to 12
- cotangent: bfloat16 [16384, 1536], P(('dp', 'mp')), may hold values from -6 to 6
- segment_ids: int32 [32, 512], P(('dp', 'mp')), may hold values from 0 to 3, never falling along the last dimension, each value on 1 to 256 neighbouring positions
- granularity: int32 [32], P('dp'), may hold values from 0 to 3, as said below
- w_qkv: bfloat16 [1536, 4608], P('dp'), may hold values from -0.15625 to 0.15625
- w_out: bfloat16 [1536, 1536], P('dp'), may hold values from -0.625 to 0.625
- w_up: bfloat16 [1536, 6144], P('dp', 'mp'), may hold values from -0.15625 to 0.15625
- w_down: bfloat16 [6144, 1536], P('mp', 'dp'), may hold values from -0.15625 to 0.15625
- norm1_gain: float32 [1536], replicated, may hold values from 0.1 to 1.9
- norm1_bias: float32 [1536], replicated, may hold values from -1.75 to 1.75
- norm2_gain: float32 [1536], replicated, may hold values from 0.1 to 1.9
- norm2_bias: float32 [1536], replicated, may hold values from -1.75 to 1.75
Outputs:
- block_out: bfloat16 [16384, 1536], P(('dp', 'mp'))
- grad_input: float32 [16384, 1536], P(('dp', 'mp'))
- grad_w_qkv: float32 [1536, 4608], P('dp')
- grad_w_out: float32 [1536, 1536], P('dp')
- grad_w_up: float32 [1536, 6144], P('dp', 'mp')
- grad_w_down: float32 [6144, 1536], P('mp', 'dp')
- grad_norm1_gain: float32 [1536], replicated
- grad_norm1_bias: float32 [1536], replicated
- grad_norm2_gain: float32 [1536], replicated
- grad_norm2_bias: float32 [1536], replicated
The draws below stay inside these ranges and needn't reach their ends.
Inputs may be any that keep to these rules, and one draw needn't show every extreme that they name: Each aligned run of the sequences of one index of dp holds at least one sequence of granularity 3.
All inputs are finite; a program needn't handle non-finite values.
Results may differ from the reference program's by a relative error of at most 0.019.
Values may be sent and summed in bfloat16 or wider, within the bound.
No kernel may reach another device: no remote copies, remote signals or barrier semaphores. Data moves between devices by JAX's collectives and lax.ppermute only.
A program may use at most 256 MiB of HBM per device.

```python
import math
import jax
import jax.numpy as jnp
import numpy as np
from jax import lax

D = 1536
HEADS = 12
HEAD_DIM = 128
FF = 6144
SEQ = 512
BLOCK = 768
NSEQ = 32
TOKENS = 16384
N_DP = 8
N_MP = 4


def draw_granularity(key, part):
    key = jax.random.fold_in(key, 7)
    first_key, second_key = jax.random.split(key)
    groups = NSEQ // N_MP
    levels = jax.random.randint(first_key, (groups, N_MP), 0, 4)
    chosen = jax.random.randint(second_key, (groups, 1), 0, N_MP)
    levels = jnp.where(jnp.arange(N_MP)[None, :] == chosen, 3, levels)
    return levels.reshape(NSEQ).astype(jnp.int32)


def raised(array, key, source, target, blocks, factor):
    owner, partner = [(jnp.arange(array.shape[dim]) // (array.shape[dim] // blocks)).reshape([-1 if axis == dim else 1 for axis in range(array.ndim)]) for dim in (source, target)]
    chosen = jax.random.permutation(key, blocks)[partner]
    strong = (owner == chosen) | (owner == (partner + blocks // 2) % blocks)
    return jnp.where(strong, factor * array, array)


def shard_levels(own_key, extent, shards, smallest, largest):
    gain, own = 1.0, jax.random.fold_in(own_key, 6)
    for position, shards_of in shards:
        steps = jnp.exp(jax.random.uniform(jax.random.fold_in(own, position), (shards_of,), jnp.float32, smallest / len(shards), largest / len(shards)))
        gain = gain * jnp.repeat(steps, extent[position] // shards_of).reshape([-1 if axis == position else 1 for axis in range(len(extent))])
    return gain


def length_profile(count, total, limit, slope):
    weights = [(1 << 20) // math.isqrt(rank ** slope) + 1 for rank in range(2, count + 1)]
    surplus, given = total - limit - (count - 1), [1] * (count - 1)
    while surplus > 0:
        free = [i for i in range(count - 1) if given[i] < limit]
        pool, remaining = sum([weights[i] for i in free]), surplus
        for i in free:
            extra = min(limit - given[i], max(1, remaining * weights[i] // pool), surplus)
            given[i] = given[i] + extra
            surplus = surplus - extra
    return np.array([limit] + given)


def ragged(own_key, number_of, total, reach, lean):
    if number_of == 2:
        one = jax.random.randint(own_key, (), max(1, total - reach), min(reach, total - 1) + 1)
        return jnp.stack([one, total - one])
    lengths = jnp.asarray(length_profile(number_of, total, reach, lean), jnp.int32)
    pairs = (number_of - 1) // 2
    donor, taker = lengths[1:1 + 2 * pairs:2], lengths[2:2 + 2 * pairs:2]
    margin = jnp.minimum(donor - 1, reach - taker)
    passed = jax.random.randint(jax.random.fold_in(own_key, 1), (pairs,), 0, 1 << 20) % (margin + 1)
    lengths = lengths.at[1:1 + 2 * pairs:2].set(donor - passed).at[2:2 + 2 * pairs:2].set(taker + passed)
    return lengths[jax.random.permutation(jax.random.fold_in(own_key, 2), number_of)]


def gaussian(rng, shape, deviation, reach, shards=(), kind=jnp.bfloat16):
    values = jax.random.normal(rng, shape, jnp.float32) * deviation
    if len(shards) > 0:
        values = shard_levels(rng, shape, shards, -0.22, 0.18) * values
    return jnp.clip(values, min=-reach, max=reach).astype(kind)


def noise_with(key, extent, width, bound, shards, heavy, held_as=jnp.bfloat16):
    entries = width * jax.random.normal(key, extent, jnp.float32)
    if shards:
        entries = entries * shard_levels(key, extent, shards, -0.22, 0.18)
    return jnp.clip(raised(entries, jax.random.fold_in(key, 3), *heavy), -bound, bound).astype(held_as)


def setup_inputs(seed: int = 0) -> dict:
    streams_of = jax.random.split(jax.random.key(seed), 13)
    block_in = noise_with(streams_of[0], (TOKENS, D), 1.0, 12.0, ((0, 32),), (0, 1, 32, 2.75))
    cotangent = gaussian(streams_of[1], (TOKENS, D), 1.0, 6.0, ((0, 32),))
    segment_ids = jax.vmap(lambda own: jnp.searchsorted(jnp.cumsum(ragged(own, 4, SEQ, SEQ // 2, 2)), jnp.arange(SEQ), side="right"))(jax.random.split(streams_of[2], NSEQ)).reshape((NSEQ, SEQ)).astype(jnp.int32)
    granularity = draw_granularity(jax.random.fold_in(streams_of[12], 71), 0)
    w_qkv = gaussian(streams_of[4], (D, 3 * D), D ** -0.5, 0.15625, ((0, 8),))
    w_out = gaussian(streams_of[5], (D, D), (D // 16) ** -0.5, 0.625, ((0, 8),))
    w_up = gaussian(streams_of[6], (D, FF), D ** -0.5, 0.15625, ((0, 8), (1, 4)))
    w_down = gaussian(streams_of[7], (FF, D), (FF // 4) ** -0.5, 0.15625, ((0, 4), (1, 8)))
    norm1_gain = jnp.clip(1.0 + 0.18 * jax.random.normal(streams_of[8], (D,), jnp.float32), 0.1, 1.9)
    norm1_bias = gaussian(streams_of[9], (D,), 0.3, 1.75, (), jnp.float32)
    norm2_gain = jnp.clip(1.0 + 0.18 * jax.random.normal(streams_of[10], (D,), jnp.float32), 0.1, 1.9)
    norm2_bias = gaussian(streams_of[11], (D,), 0.3, 1.75, (), jnp.float32)
    return {"block_in": block_in, "cotangent": cotangent, "segment_ids": segment_ids, "granularity": granularity, "w_qkv": w_qkv, "w_out": w_out, "w_up": w_up, "w_down": w_down, "norm1_gain": norm1_gain, "norm1_bias": norm1_bias, "norm2_gain": norm2_gain, "norm2_bias": norm2_bias}


epsilon = 1e-05
theta_base = 10000.0
highest = lax.Precision.HIGHEST

@jax.custom_vjp
def low(v):
    return lax.optimization_barrier(v.astype(jnp.bfloat16)).astype(jnp.float32)

@jax.custom_vjp
def low_back(v):
    return v

def low_keep(v):
    return (low(v), None)

def low_pass(kept, grad):
    return (grad,)

def back_keep(v):
    return (v, None)

def back_low(kept, grad):
    return (low(grad),)
low.defvjp(low_keep, low_pass)
low_back.defvjp(back_keep, back_low)

def layer_norm(values, norm_gain, norm_shift):
    average = lax.optimization_barrier(jnp.mean(values, axis=-1, keepdims=True))
    centred = values - average
    variance = lax.optimization_barrier(jnp.mean(centred * centred, axis=-1, keepdims=True))
    return centred * lax.rsqrt(variance + epsilon) * norm_gain + norm_shift

def rotary_tables(length, head_width):
    halfway = head_width // 2
    frequency = theta_base ** (-2.0 * jnp.arange(halfway, dtype=jnp.float32) / head_width)
    angles = jnp.arange(length, dtype=jnp.float32)[:, None] * frequency[None, :]
    angles = jnp.concatenate([angles, angles], axis=1)
    return (jnp.cos(angles), jnp.sin(angles))

def rotate(values, cosine_table, sine_table):
    halfway = values.shape[-1] // 2
    turned = jnp.concatenate([-values[..., halfway:], values[..., :halfway]], axis=-1)
    return values * cosine_table[:, None, :] + turned * sine_table[:, None, :]

def attend(operands):
    queries, key_part, value_part, segment = operands
    raw_scores = jnp.einsum('shd,thd->hst', queries, key_part, precision=highest)
    scores = low_back(raw_scores) * HEAD_DIM ** (-0.5)
    places = jnp.arange(SEQ)
    allowed = (places[:, None] >= places[None, :]) & (segment[:, None] == segment[None, :])
    scores = jnp.where(allowed[None], scores, -1000000000.0)
    weights = low(jax.nn.softmax(scores, axis=-1))
    return jnp.einsum('hst,thd->shd', weights, value_part, precision=highest)

def layer(inputs, segments, granular, w_qkv, w_out, w_up, w_down, norm1_gain, norm1_bias, norm2_gain, norm2_bias):
    normed1 = low(layer_norm(inputs, norm1_gain, norm1_bias))
    joined_qkv = low_back(jnp.dot(normed1, w_qkv, precision=highest))
    pieces = joined_qkv.reshape(N_MP, SEQ, 3, HEADS, HEAD_DIM)
    cosine_table, sine_table = rotary_tables(SEQ, HEAD_DIM)
    queries = low(rotate(pieces[:, :, 0], cosine_table, sine_table))
    key_part = low(rotate(pieces[:, :, 1], cosine_table, sine_table))
    value_part = low(pieces[:, :, 2])
    context = lax.map(jax.checkpoint(attend), (queries, key_part, value_part, segments))
    context = low(low_back(context.reshape(N_MP * SEQ, D)))
    hidden1 = inputs + low_back(jnp.dot(context, w_out, precision=highest))
    normed2 = low(layer_norm(hidden1, norm2_gain, norm2_bias))
    preact = low_back(jnp.dot(normed2, w_up, precision=highest))
    limits = jnp.repeat(BLOCK * jnp.power(2, granular), SEQ)
    usable = (jnp.arange(FF)[None, :] < limits[:, None]).astype(jnp.float32)
    active = low(jax.nn.gelu(preact, approximate=False) * usable)
    return hidden1 + jnp.dot(active, w_down, precision=highest)

def reference(block_in, cotangent, segment_ids, granularity, w_qkv, w_out, w_up, w_down, norm1_gain, norm1_bias, norm2_gain, norm2_bias):
    group_rows = N_MP * SEQ
    inputs = block_in.astype(jnp.float32).reshape(N_DP, group_rows, D)
    upstream = cotangent.astype(jnp.float32).reshape(N_DP, group_rows, D)
    segments = segment_ids.reshape(N_DP, N_MP, SEQ)
    granular = granularity.reshape(N_DP, N_MP)
    params = (w_qkv.astype(jnp.float32), w_out.astype(jnp.float32), w_up.astype(jnp.float32), w_down.astype(jnp.float32), norm1_gain, norm1_bias, norm2_gain, norm2_bias)

    def advance(totals, operands):
        group_in, group_up, group_seg, group_gran = operands

        def forward(group_x, *weights):
            return layer(group_x, group_seg, group_gran, *weights)
        result, backward = jax.vjp(forward, group_in, *params)
        gradients = backward(group_up)
        summed = tuple((carried + gradient for carried, gradient in zip(totals, gradients[1:])))
        return (summed, (result.astype(jnp.bfloat16), gradients[0]))
    starting = tuple((jnp.zeros_like(weight) for weight in params))
    totals, (outputs, grad_rows) = lax.scan(advance, starting, (inputs, upstream, segments, granular))
    return (outputs.reshape(TOKENS, D), grad_rows.reshape(TOKENS, D), totals[0], totals[1], totals[2], totals[3], totals[4], totals[5], totals[6], totals[7])
```

```python
import functools

import jax
import jax.numpy as jnp
from jax import lax
from jax.experimental import pallas as pl
from jax.experimental.pallas import tpu as pltpu
from jax.sharding import PartitionSpec as P

HEADS = 12
HEAD_DIM = 128
BLOCK = 768
AXES = ("dp", "mp")
PAIR = 2

epsilon = 1e-05
theta_base = 10000.0
score_scale = HEAD_DIM ** (-0.5)
contract_rows = (((0,), (0,)), ((), ()))
contract_cols = (((1,), (1,)), ((), ()))
f32 = jnp.float32
bf16 = jnp.bfloat16
VMEM_LIMIT = 56 * 1024 * 1024


def layer_norm_stats(values):
    average = jnp.mean(values, axis=-1, keepdims=True)
    centred = values - average
    variance = jnp.mean(centred * centred, axis=-1, keepdims=True)
    inverse = lax.rsqrt(variance + epsilon)
    return average, inverse


def layer_norm_back(q, normal, inverse, gain):
    c = q * gain
    mean_c = jnp.mean(c, axis=-1, keepdims=True)
    mean_cn = jnp.mean(c * normal, axis=-1, keepdims=True)
    return (c - mean_c - normal * mean_cn) * inverse


def rotary_tables(length, head_width):
    halfway = head_width // 2
    frequency = theta_base ** (-2.0 * jnp.arange(halfway, dtype=f32) / head_width)
    angles = jnp.arange(length, dtype=f32)[:, None] * frequency[None, :]
    angles = jnp.concatenate([angles, angles], axis=1)
    return (jnp.cos(angles), jnp.sin(angles))


def turn(values):
    halfway = values.shape[-1] // 2
    return jnp.concatenate([-values[:, halfway:], values[:, :halfway]], axis=-1)


def turn_back(values):
    halfway = values.shape[-1] // 2
    return jnp.concatenate([values[:, halfway:], -values[:, :halfway]], axis=-1)


def allowed_block(seg_col, seg_row, row_start, block, extent):
    row_place = row_start + lax.broadcasted_iota(jnp.int32, (block, extent), 0)
    col_place = lax.broadcasted_iota(jnp.int32, (block, extent), 1)
    return (row_place >= col_place) & (seg_col == seg_row)


def attend_kernel(chips, seq_len, offs_ref, norm_ref, cos_ref, sin_ref, segc_ref, segr_ref, *refs):
    pieces = refs[:chips]
    wide_ref, qkv_ref, ctx_ref, lse_ref = refs[chips:]
    span = pieces[0].shape[0]
    for j in range(chips):
        wide_ref[pl.ds(pl.multiple_of(offs_ref[j], span), span), :] = pieces[j][...]
    hd = HEAD_DIM
    block = seq_len // 2

    def project(i, carry):
        start = pl.multiple_of(i * block, block)
        rows = pl.ds(start, block)
        joined = jnp.dot(norm_ref[rows, :], wide_ref[...], preferred_element_type=f32)
        table = pl.ds(pl.multiple_of((i % 2) * block, block), block)
        cosine, sine = cos_ref[table, :], sin_ref[table, :]
        for h in range(2 * PAIR):
            part = joined[:, h * hd : (h + 1) * hd]
            qkv_ref[rows, h * hd : (h + 1) * hd] = (part * cosine + turn(part) * sine).astype(bf16)
        qkv_ref[rows, 2 * PAIR * hd :] = joined[:, 2 * PAIR * hd :].astype(bf16)
        return carry

    lax.fori_loop(0, 4, project, 0)

    lane = lax.broadcasted_iota(jnp.int32, (block, hd), 1)

    def sequence(s, carry):
        base = s * seq_len
        for r in range(2):
            extent = (r + 1) * block
            rows = pl.ds(pl.multiple_of(base + r * block, block), block)
            cols = pl.ds(pl.multiple_of(base, block), extent)
            allowed = allowed_block(
                segc_ref[s, r * block : (r + 1) * block, :],
                segr_ref[s, :, :extent],
                r * block,
                block,
                extent,
            )
            logs = jnp.zeros((block, hd), f32)
            for h in range(PAIR):
                query = qkv_ref[rows, h * hd : (h + 1) * hd]
                key = qkv_ref[cols, (PAIR + h) * hd : (PAIR + h + 1) * hd]
                value = qkv_ref[cols, (2 * PAIR + h) * hd : (2 * PAIR + h + 1) * hd]
                scores = lax.dot_general(query, key, contract_cols, preferred_element_type=f32)
                scores = jnp.where(allowed, scores * score_scale, -1000000000.0)
                top = jnp.max(scores, axis=-1, keepdims=True)
                weight = jnp.exp(scores - top)
                total = jnp.sum(weight, axis=-1, keepdims=True)
                probs = (weight * (1.0 / total)).astype(bf16)
                ctx_ref[rows, h * hd : (h + 1) * hd] = jnp.dot(
                    probs, value, preferred_element_type=f32
                ).astype(bf16)
                logs = jnp.where(lane == h, top + jnp.log(total), logs)
            lse_ref[rows, :] = logs
        return carry

    lax.fori_loop(0, 2, sequence, 0)


def attend_back_kernel(seq_len, qkv_ref, lse_ref, grad_ref, cos_ref, sin_ref, segc_ref, segr_ref, out_ref, gq, gk, gv):
    hd = HEAD_DIM
    block = seq_len // 2

    def sequence(s, carry):
        base = s * seq_len
        for h in range(PAIR):
            for r in (1, 0):
                extent = (r + 1) * block
                rows = pl.ds(pl.multiple_of(base + r * block, block), block)
                cols = pl.ds(pl.multiple_of(base, block), extent)
                allowed = allowed_block(
                    segc_ref[s, r * block : (r + 1) * block, :],
                    segr_ref[s, :, :extent],
                    r * block,
                    block,
                    extent,
                )
                query = qkv_ref[rows, h * hd : (h + 1) * hd]
                key = qkv_ref[cols, (PAIR + h) * hd : (PAIR + h + 1) * hd]
                value = qkv_ref[cols, (2 * PAIR + h) * hd : (2 * PAIR + h + 1) * hd]
                grad = grad_ref[rows, h * hd : (h + 1) * hd]
                scores = lax.dot_general(query, key, contract_cols, preferred_element_type=f32)
                scores = jnp.where(allowed, scores * score_scale, -1000000000.0)
                probs = jnp.exp(scores - lse_ref[rows, h : h + 1])
                grad_probs = lax.dot_general(grad, value, contract_cols, preferred_element_type=f32)
                weighted = jnp.sum(probs * grad_probs, axis=-1, keepdims=True)
                grad_scores = (probs * (grad_probs - weighted) * score_scale).astype(bf16)
                probs = probs.astype(bf16)
                gq[r * block : (r + 1) * block, :] = jnp.dot(grad_scores, key, preferred_element_type=f32)
                grad_key = lax.dot_general(grad_scores, query, contract_rows, preferred_element_type=f32)
                grad_value = lax.dot_general(probs, grad, contract_rows, preferred_element_type=f32)
                if r == 1:
                    gk[...] = grad_key
                    gv[...] = grad_value
                else:
                    gk[:block, :] = gk[:block, :] + grad_key
                    gv[:block, :] = gv[:block, :] + grad_value
            sine, cosine = sin_ref[...], cos_ref[...]
            rows = pl.ds(pl.multiple_of(base, seq_len), seq_len)
            grad_query, grad_key = gq[...], gk[...]
            out_ref[rows, h * hd : (h + 1) * hd] = (
                grad_query * cosine + turn_back(grad_query * sine)
            ).astype(bf16)
            out_ref[rows, (PAIR + h) * hd : (PAIR + h + 1) * hd] = (
                grad_key * cosine + turn_back(grad_key * sine)
            ).astype(bf16)
            out_ref[rows, (2 * PAIR + h) * hd : (2 * PAIR + h + 1) * hd] = gv[...].astype(bf16)
        return carry

    lax.fori_loop(0, 2, sequence, 0)


SMEM_SPEC = pl.BlockSpec(memory_space=pltpu.SMEM)
VMEM_SPEC = pl.BlockSpec(memory_space=pltpu.VMEM)


def attend(offsets, normed, cosine, sine, seg_col, seg_row, pieces):
    chips = len(pieces)
    rows, width = normed.shape
    cols = pieces[0].shape[1]
    return pl.pallas_call(
        functools.partial(attend_kernel, chips, rows // 2),
        out_shape=(
            jax.ShapeDtypeStruct((width, cols), bf16),
            jax.ShapeDtypeStruct((rows, cols), bf16),
            jax.ShapeDtypeStruct((rows, PAIR * HEAD_DIM), bf16),
            jax.ShapeDtypeStruct((rows, HEAD_DIM), f32),
        ),
        in_specs=[SMEM_SPEC] + [VMEM_SPEC] * (5 + chips),
        out_specs=(VMEM_SPEC,) * 4,
        compiler_params=pltpu.CompilerParams(vmem_limit_bytes=VMEM_LIMIT),
        name="attend",
    )(offsets, normed, cosine, sine, seg_col, seg_row, *pieces)


def attend_back(qkv, lse, grad, cosine, sine, seg_col, seg_row):
    rows, cols = qkv.shape
    seq_len = rows // 2
    return pl.pallas_call(
        functools.partial(attend_back_kernel, seq_len),
        out_shape=jax.ShapeDtypeStruct((rows, cols), bf16),
        in_specs=[VMEM_SPEC] * 7,
        out_specs=VMEM_SPEC,
        scratch_shapes=[pltpu.VMEM((seq_len, HEAD_DIM), f32)] * 3,
        compiler_params=pltpu.CompilerParams(vmem_limit_bytes=VMEM_LIMIT),
        name="attend_back",
    )(qkv, lse, grad, cosine, sine, seg_col, seg_row)


def tie(value, *others):
    return lax.optimization_barrier((value, *others))[0]


def build(dp_size, mp_size):
    total = dp_size * mp_size
    chip_bits = []
    bit = 2 * mp_size
    while bit < total:
        chip_bits.append(bit)
        bit *= 2
    core_bit = mp_size
    near_bit = 1
    far_bits = []
    bit = 2
    while bit < mp_size:
        far_bits.append(bit)
        bit *= 2
    chips = dp_size // 2

    def flip(value, bit):
        return lax.ppermute(value, AXES, [(i, i ^ bit) for i in range(total)])

    def gather_chips(piece, way):
        if len(chip_bits) == 2:
            first, second = chip_bits
            from_x = flip(piece, first)
            from_y = flip(piece, second)
            corner = flip(from_x, second) if way == 0 else flip(from_y, first)
            return [piece, from_x, from_y, corner]
        held = [piece]
        for bit in chip_bits:
            held = held + [flip(value, bit) for value in held]
        return held

    def add(a, b):
        return a.astype(f32) + b.astype(f32)

    def scatter_chips(pieces, way):
        if len(chip_bits) == 2:
            first, second = chip_bits
            own, to_x, to_y, corner = pieces
            if way == 0:
                to_y = add(to_y, flip(corner, first)).astype(bf16)
            else:
                to_x = add(to_x, flip(corner, second)).astype(bf16)
            return own.astype(f32) + flip(to_x, first).astype(f32) + flip(to_y, second).astype(f32)
        held = list(pieces)
        for bit in reversed(chip_bits):
            middle = len(held) // 2
            low, high = held[:middle], held[middle:]
            held = [add(a, flip(b.astype(bf16), bit)) for a, b in zip(low, high)]
        return held[0].astype(f32)

    def on_device(
        block_in,
        cotangent,
        segment_ids,
        granularity,
        w_qkv,
        w_out,
        w_up,
        w_down,
        norm1_gain,
        norm1_bias,
        norm2_gain,
        norm2_bias,
    ):
        seq_len, width = block_in.shape
        rows = width // dp_size
        units = w_up.shape[1]
        half_units = units // 2
        dp = lax.axis_index("dp")
        mp = lax.axis_index("mp")
        core = dp % 2
        chip = dp // 2
        span = 2 * rows
        offsets = jnp.stack([(chip ^ j) * span for j in range(chips)]).astype(jnp.int32)
        core_heads = HEADS // 2
        chunks = core_heads // PAIR
        chunk_cols = 3 * PAIR * HEAD_DIM

        def chip_order(value):
            return jnp.concatenate(
                [lax.dynamic_slice_in_dim(value, offsets[j], span, axis=1) for j in range(chips)],
                axis=1,
            )

        def by_core(own, other):
            return jnp.where(core == 0, own, other), jnp.where(core == 0, other, own)

        def both_rows(own, other):
            return jnp.concatenate(list(by_core(own, other)), axis=0)

        shard = w_qkv.reshape(rows, 3, 2, chunks, PAIR * HEAD_DIM)
        keep, send = by_core(shard[:, :, 0], shard[:, :, 1])
        other_in = flip(block_in, core_bit)
        got = flip(send, core_bit)
        qkv_pieces = []
        for p in range(chunks):
            own_p = both_rows(keep[:, :, p], got[:, :, p]).reshape(span, chunk_cols)
            qkv_pieces.append(gather_chips(own_p, p % 2))

        small = jnp.concatenate([segment_ids, jnp.broadcast_to(granularity[:, None], (mp_size, seq_len))])
        small_other = flip(small, core_bit)
        segments = jnp.stack([small[0], small_other[0]])
        levels = jnp.concatenate([small[1:, 0], small_other[1:, 0]])
        seg_col = segments[:, :, None]
        seg_row = segments[:, None, :]
        cosine, sine = rotary_tables(seq_len, HEAD_DIM)

        out_pieces = gather_chips(w_out, 1)
        out_others = [flip(v, core_bit) for v in out_pieces]
        wide_out = jnp.concatenate([both_rows(a, b) for a, b in zip(out_pieces, out_others)], axis=0)

        pair = jnp.stack([w_up, w_down.T])
        keep, send = by_core(pair[:, :, :half_units], pair[:, :, half_units:])
        got = flip(send, core_bit)
        mine = jnp.concatenate(list(by_core(keep, got)), axis=1).reshape(2 * span, half_units)
        slices = [mine]
        for bit in far_bits:
            slices = slices + [flip(v, bit) for v in slices]
        cot_z = flip(cotangent, near_bit)
        cot_rows = [cotangent, flip(cotangent, core_bit), cot_z, flip(cot_z, core_bit)]
        cot_rows = chip_order(jnp.concatenate(cot_rows, axis=0))
        up_blocks, down_blocks = [], []
        for k, v in enumerate(slices):
            got = gather_chips(v, k % 2)
            up_blocks.append(jnp.concatenate([g[:span] for g in got], axis=0))
            down_blocks.append(jnp.concatenate([g[span:] for g in got], axis=0))

        inputs = block_in.astype(f32)
        average1, inverse1 = layer_norm_stats(inputs)
        normal1 = (inputs - average1) * inverse1
        other_inputs = other_in.astype(f32)
        other_average, other_inverse = layer_norm_stats(other_inputs)
        other_normal = (other_inputs - other_average) * other_inverse
        normed1 = jnp.concatenate(
            [
                (normal1 * norm1_gain + norm1_bias).astype(bf16),
                (other_normal * norm1_gain + norm1_bias).astype(bf16),
            ]
        )
        qkv_wide, qkv_low, contexts, logs = [], [], [], []
        for p in range(chunks):
            a, b, c, d = attend(offsets, normed1, cosine, sine, seg_col, seg_row, qkv_pieces[p])
            qkv_wide.append(a)
            qkv_low.append(b)
            contexts.append(c)
            logs.append(d)
        context_mine = jnp.concatenate(contexts, axis=1)
        context_got = flip(context_mine[seq_len:], core_bit)
        context_low = jnp.concatenate(list(by_core(context_mine[:seq_len], context_got)), axis=1)
        hidden1 = inputs + jnp.dot(chip_order(context_low), wide_out, preferred_element_type=f32)
        average2, inverse2 = layer_norm_stats(hidden1)
        normal2 = (hidden1 - average2) * inverse2
        normed2_low = chip_order((normal2 * norm2_gain + norm2_bias).astype(bf16))

        norm_z = flip(normed2_low, near_bit)
        norm_rows = [normed2_low, flip(normed2_low, core_bit), norm_z, flip(norm_z, core_bit)]
        norm_rows = jnp.concatenate(norm_rows, axis=0)

        own_level = lax.dynamic_index_in_dim(levels, mp, keepdims=False)
        core_level = lax.dynamic_index_in_dim(levels, mp_size + mp, keepdims=False)
        near_level = lax.dynamic_index_in_dim(levels, mp ^ 1, keepdims=False)
        both_level = lax.dynamic_index_in_dim(levels, mp_size + (mp ^ 1), keepdims=False)
        limits = jnp.stack([own_level, core_level, near_level, both_level])
        limits = jnp.repeat(BLOCK * jnp.power(2, limits), seq_len)

        out_part = 0.0
        back_part = 0.0
        shares = []
        for k, (up_k, down_k) in enumerate(zip(up_blocks, down_blocks)):
            start = (mp ^ (2 * k)) * units + core * half_units
            unit_ids = start + jnp.arange(half_units)
            mask = (unit_ids[None, :] < limits[:, None]).astype(f32)
            preact = jnp.dot(norm_rows, up_k, preferred_element_type=f32)
            grad_active = jnp.dot(cot_rows, down_k, preferred_element_type=f32)
            cdf = 0.5 * (1.0 + lax.erf(preact * 0.7071067811865476))
            active = (preact * cdf * mask).astype(bf16)
            slope = cdf + preact * jnp.exp(-0.5 * preact * preact) * 0.3989422804014327
            grad_preact = (grad_active * mask * slope).astype(bf16)
            back_part = back_part + lax.dot_general(
                grad_preact, up_k, contract_cols, preferred_element_type=f32
            )
            out_part = out_part + lax.dot_general(
                active, down_k, contract_cols, preferred_element_type=f32
            )
            grad_up = lax.dot_general(
                norm_rows, grad_preact, contract_rows, preferred_element_type=f32
            ).astype(bf16)
            grad_down = lax.dot_general(
                cot_rows, active, contract_rows, preferred_element_type=f32
            ).astype(bf16)
            shares.append(
                scatter_chips(
                    [
                        jnp.concatenate([g[j * span : (j + 1) * span] for g in (grad_up, grad_down)])
                        for j in range(chips)
                    ],
                    k % 2,
                )
            )

        def group_sum(part):
            own, beside, near, both = [part[i * seq_len : (i + 1) * seq_len] for i in range(4)]
            near = add(near, flip(both.astype(bf16), core_bit)).astype(bf16)
            own = own + flip(beside.astype(bf16), core_bit).astype(f32)
            return chip_order(own + flip(near, near_bit).astype(f32))

        grad_normed2 = group_sum(back_part)
        block_out = (hidden1 + group_sum(out_part)).astype(bf16)

        held = shares
        for bit in reversed(far_bits):
            middle = len(held) // 2
            held = [add(a, flip(b.astype(bf16), bit)) for a, b in zip(held[:middle], held[middle:])]
        summed = held[0].reshape(2, 2, rows, half_units)
        keep, send = by_core(summed[:, 0], summed[:, 1])
        got = flip(send.astype(bf16), core_bit)
        pair = jnp.concatenate(list(by_core(keep, got.astype(f32))), axis=2)
        grad_w_up = pair[0]
        grad_w_down = pair[1].T

        grad_gain2 = jnp.sum(grad_normed2 * normal2, axis=0)
        grad_bias2 = jnp.sum(grad_normed2, axis=0)
        grad_hidden1 = cotangent.astype(f32) + layer_norm_back(
            grad_normed2, normal2, inverse2, norm2_gain
        )
        grad_attn_low = grad_hidden1.astype(bf16)

        def over_mp(share):
            low = share.astype(bf16)
            bits = [near_bit] + far_bits
            held = low
            for bit in bits:
                size = held.shape[0] // 2
                upper = (mp // bit) % 2 == 1
                keep = jnp.where(upper, held[size:], held[:size])
                send = jnp.where(upper, held[:size], held[size:])
                held = add(keep, flip(send, bit)).astype(bf16)
            for bit in reversed(bits):
                got = flip(held, bit)
                upper = (mp // bit) % 2 == 1
                held = jnp.concatenate(
                    [jnp.where(upper, got, held), jnp.where(upper, held, got)], axis=0
                )
            return held

        grad_context = lax.dot_general(
            grad_attn_low, wide_out, contract_cols, preferred_element_type=f32
        ).astype(bf16)
        grad_context = chip_order(grad_context)
        half = width // 2
        keep, send = by_core(grad_context[:, :half], grad_context[:, half:])
        grad_context = jnp.concatenate([keep, flip(send, core_bit)])

        ordered = chip_order(context_low).reshape(seq_len, chips, 2, rows)
        keep, send = by_core(ordered[:, :, 0], ordered[:, :, 1])
        other = lax.dot_general(send.reshape(seq_len, half), grad_attn_low, contract_rows, preferred_element_type=f32)
        own = lax.dot_general(keep.reshape(seq_len, half), grad_attn_low, contract_rows, preferred_element_type=f32)
        chip_sum = add(own, flip(other.astype(bf16), core_bit)).astype(bf16)
        grad_w_out = over_mp(
            scatter_chips([chip_sum[j * rows : (j + 1) * rows] for j in range(chips)], 1)
        ).astype(f32)

        normed1_rel = chip_order(normed1)
        grad_low, qkv_shares = [], []
        for p in range(chunks):
            cols = slice(p * PAIR * HEAD_DIM, (p + 1) * PAIR * HEAD_DIM)
            low = attend_back(
                qkv_low[p], logs[p], grad_context[:, cols], cosine, sine, seg_col, seg_row
            )
            grad_low.append(low)
            parts = [
                lax.dot_general(
                    normed1_rel[:, j * span : (j + 1) * span],
                    low,
                    contract_rows,
                    preferred_element_type=f32,
                ).astype(bf16)
                for j in range(chips)
            ]
            share = scatter_chips(parts, p % 2)
            qkv_shares.append(over_mp(share))
        back = 0.0
        for p in range(chunks):
            back = back + lax.dot_general(
                grad_low[p], qkv_wide[p], contract_cols, preferred_element_type=f32
            )
        grad_normed1 = back[:seq_len] + flip(back[seq_len:].astype(bf16), core_bit).astype(f32)
        grad_gain1 = jnp.sum(grad_normed1 * normal1, axis=0)
        grad_bias1 = jnp.sum(grad_normed1, axis=0)
        grad_input = grad_hidden1 + layer_norm_back(grad_normed1, normal1, inverse1, norm1_gain)

        shares = jnp.stack(qkv_shares, axis=1).reshape(2, rows, chunks, 3, PAIR * HEAD_DIM)
        keep, send = by_core(shares[0], shares[1])
        got = flip(send, core_bit)
        sides = jnp.stack(list(by_core(keep, got)), axis=1)
        grad_w_qkv = sides.transpose(0, 3, 1, 2, 4).reshape(rows, 3 * width).astype(f32)

        def sum_all(value):
            bit = 1
            while bit < total:
                value = value + flip(value, bit)
                bit *= 2
            return value

        sums2 = sum_all(jnp.stack([grad_gain2, grad_bias2]))
        sums1 = sum_all(jnp.stack([grad_gain1, grad_bias1]))
        return (
            block_out,
            grad_input,
            grad_w_qkv,
            grad_w_out,
            grad_w_up,
            grad_w_down,
            sums1[0],
            sums1[1],
            sums2[0],
            sums2[1],
        )

    return on_device


def solution(mesh):
    return jax.shard_map(
        build(mesh.shape["dp"], mesh.shape["mp"]),
        mesh=mesh,
        in_specs=(
            P(("dp", "mp"), None),
            P(("dp", "mp"), None),
            P(("dp", "mp"), None),
            P("dp"),
            P("dp", None),
            P("dp", None),
            P("dp", "mp"),
            P("mp", "dp"),
            P(),
            P(),
            P(),
            P(),
        ),
        out_specs=(
            P(("dp", "mp"), None),
            P(("dp", "mp"), None),
            P("dp", None),
            P("dp", None),
            P("dp", "mp"),
            P("mp", "dp"),
            P(),
            P(),
            P(),
            P(),
        ),
        check_vma=False,
    )
```

```python
import functools

import jax
import jax.numpy as jnp
from jax import lax
from jax.experimental import pallas as pl
from jax.experimental.pallas import tpu as pltpu
from jax.sharding import PartitionSpec as P

HEADS = 12
HEAD_DIM = 128
BLOCK = 768
AXES = ("dp", "mp")
PAIR = 2
LANES = PAIR * HEAD_DIM

epsilon = 1e-05
theta_base = 10000.0
score_scale = HEAD_DIM ** (-0.5)
contract_rows = (((0,), (0,)), ((), ()))
contract_cols = (((1,), (1,)), ((), ()))
f32 = jnp.float32
bf16 = jnp.bfloat16
VMEM_LIMIT = 56 * 1024 * 1024
SMEM_SPEC = pl.BlockSpec(memory_space=pltpu.SMEM)
VMEM_SPEC = pl.BlockSpec(memory_space=pltpu.VMEM)


def rotary_tables(length, head_width):
    halfway = head_width // 2
    frequency = theta_base ** (-2.0 * jnp.arange(halfway, dtype=f32) / head_width)
    angles = jnp.arange(length, dtype=f32)[:, None] * frequency[None, :]
    angles = jnp.concatenate([angles, angles], axis=1)
    return (jnp.cos(angles), jnp.sin(angles))


def turn(values):
    halfway = values.shape[-1] // 2
    return jnp.concatenate([-values[:, halfway:], values[:, :halfway]], axis=-1)


def turn_back(values):
    halfway = values.shape[-1] // 2
    return jnp.concatenate([values[:, halfway:], -values[:, :halfway]], axis=-1)


def at(start, size):
    return pl.ds(pl.multiple_of(start, size), size)


def lanes(start, size):
    return pl.ds(pl.multiple_of(start, 128), size)


def normal_of(values):
    average = jnp.mean(values, axis=-1, keepdims=True)
    centred = values - average
    variance = jnp.mean(centred * centred, axis=-1, keepdims=True)
    inverse = lax.rsqrt(variance + epsilon)
    return centred * inverse, inverse


def norm_back(grad, normal, inverse, gain):
    scaled = grad * gain
    mean = jnp.mean(scaled, axis=-1, keepdims=True)
    mean_normal = jnp.mean(scaled * normal, axis=-1, keepdims=True)
    return (scaled - mean - normal * mean_normal) * inverse


COST = pl.CostEstimate(flops=1000000, bytes_accessed=0, transcendentals=0)


def run(name, kernel, outs, scalars, *args, scratch=()):
    many = isinstance(outs, (tuple, list))
    return pl.pallas_call(
        kernel,
        out_shape=outs,
        in_specs=[SMEM_SPEC] * len(scalars) + [VMEM_SPEC] * len(args),
        out_specs=[VMEM_SPEC] * len(outs) if many else VMEM_SPEC,
        scratch_shapes=list(scratch),
        cost_estimate=COST,
        compiler_params=pltpu.CompilerParams(vmem_limit_bytes=VMEM_LIMIT),
        name=name,
    )(*scalars, *args)


def shape(dims, kind=bf16):
    return jax.ShapeDtypeStruct(tuple(dims), kind)


def cut_attention_kernel(place, own_qkv, got_qkv, *outs):
    core = place[0]
    rows, width = own_qkv.shape
    width = width // 3
    half = width // 2
    mine, theirs = at(core * rows, rows), at((1 - core) * rows, rows)
    for p, out in enumerate(outs):
        for part in range(3):
            cols = lanes(core * half + (part * width + p * LANES), LANES)
            here = slice(part * LANES, (part + 1) * LANES)
            out[mine, here] = own_qkv[:, cols]
            out[theirs, here] = got_qkv[:, cols]


def cut_rest_kernel(place, own_out, own_up, own_down, got, out_piece, out_piece_got, ff_piece):
    core = place[0]
    rows, width = own_out.shape
    half = width // 2
    for out, part in ((out_piece, core), (out_piece_got, 1 - core)):
        cols = lanes(part * half, half)
        out[at(core * rows, rows), :] = own_out[:, cols]
        out[at((1 - core) * rows, rows), :] = got[:rows, cols]
    half = own_up.shape[1] // 2
    cols = lanes(core * half, half)
    units = own_up.shape[1]
    for i, own in enumerate((own_up, own_down)):
        ff_piece[at(core * rows + i * 2 * rows, rows), :] = own[:, cols]
        if units == width:
            ff_piece[at((1 - core) * rows + i * 2 * rows, rows), :] = got[(1 + i) * rows : (2 + i) * rows, cols]
        else:
            cols_got = lanes(core * half + i * units, half)
            ff_piece[at((1 - core) * rows + i * 2 * rows, rows), :] = got[rows:, cols_got]


def join(place, chips, pieces, outs):
    parts = len(outs)
    span = pieces[0].shape[0] // parts
    for j in range(min(chips, len(pieces))):
        for i, out in enumerate(outs):
            rows = at(place[1 + j], span)
            if len(pieces) == chips or j < chips - 1:
                out[rows, :] = pieces[j][i * span : (i + 1) * span, :]
            elif parts == 1:
                half = span // 2
                out[pl.ds(pl.multiple_of(place[1 + j], half), half), :] = pieces[j][...]
                out[pl.ds(pl.multiple_of(place[1 + j] + half, half), half), :] = pieces[j + 1][...]
            else:
                out[rows, :] = pieces[j + i][...]


def join_kernel(chips, many, place, *refs):
    *pieces, mine, got = refs
    join(place, chips, pieces[:many], [mine])
    join(place, chips, pieces[many:], [got])


def norm_kernel(own, other, gain, bias, out):
    seq_len = own.shape[0]
    block = 128

    def step(i, carry):
        rows = at(i * block, block)
        for k, ref in enumerate((own, other)):
            normal, _ = normal_of(ref[rows, :].astype(f32))
            out[at(k * seq_len + i * block, block), :] = (normal * gain[...] + bias[...]).astype(bf16)
        return carry

    lax.fori_loop(0, seq_len // block, step, 0)


def allowed_block(seg_col, seg_row, row_start, block, extent):
    row_place = row_start + lax.broadcasted_iota(jnp.int32, (block, extent), 0)
    col_place = lax.broadcasted_iota(jnp.int32, (block, extent), 1)
    return (row_place >= col_place) & (seg_col == seg_row)


def attend_kernel(chips, seq_len, place, norm_ref, cos_ref, sin_ref, segc_ref, segr_ref, *refs):
    *pieces, wide_ref, qkv_ref, ctx_ref, lse_ref = refs
    join(place, chips, pieces, [wide_ref])
    hd = HEAD_DIM
    block = seq_len // 2

    def project(i, carry):
        rows = at(i * block, block)
        joined = jnp.dot(norm_ref[rows, :], wide_ref[...], preferred_element_type=f32)
        table = at((i % 2) * block, block)
        cosine, sine = cos_ref[table, :], sin_ref[table, :]
        for h in range(2 * PAIR):
            part = joined[:, h * hd : (h + 1) * hd]
            qkv_ref[rows, h * hd : (h + 1) * hd] = (part * cosine + turn(part) * sine).astype(bf16)
        qkv_ref[rows, 2 * PAIR * hd :] = joined[:, 2 * PAIR * hd :].astype(bf16)
        return carry

    lax.fori_loop(0, 4, project, 0)

    lane = lax.broadcasted_iota(jnp.int32, (block, hd), 1)

    def sequence(s, carry):
        base = s * seq_len
        for r in range(2):
            extent = (r + 1) * block
            rows = at(base + r * block, block)
            cols = pl.ds(pl.multiple_of(base, block), extent)
            allowed = allowed_block(
                segc_ref[s, r * block : (r + 1) * block, :],
                segr_ref[s, :, :extent],
                r * block,
                block,
                extent,
            )
            logs = jnp.zeros((block, hd), f32)
            for h in range(PAIR):
                query = qkv_ref[rows, h * hd : (h + 1) * hd]
                key = qkv_ref[cols, (PAIR + h) * hd : (PAIR + h + 1) * hd]
                value = qkv_ref[cols, (2 * PAIR + h) * hd : (2 * PAIR + h + 1) * hd]
                scores = lax.dot_general(query, key, contract_cols, preferred_element_type=f32)
                scores = jnp.where(allowed, scores * score_scale, -1000000000.0)
                top = jnp.max(scores, axis=-1, keepdims=True)
                weight = jnp.exp(scores - top)
                total = jnp.sum(weight, axis=-1, keepdims=True)
                probs = (weight * (1.0 / total)).astype(bf16)
                ctx_ref[s, r * block : (r + 1) * block, h * hd : (h + 1) * hd] = jnp.dot(
                    probs, value, preferred_element_type=f32
                ).astype(bf16)
                logs = jnp.where(lane == h, top + jnp.log(total), logs)
            lse_ref[rows, :] = logs
        return carry

    lax.fori_loop(0, 2, sequence, 0)


def out_kernel(chunks, place, x_ref, *refs):
    mine, got = refs[:chunks], refs[chunks : 2 * chunks]
    w_mine, w_got, gain, bias, hidden, norm, ctx = refs[2 * chunks :]
    core = place[0]
    seq_len, width = x_ref.shape
    half = width // 2
    own_cols, got_cols = lanes(core * half, half), lanes((1 - core) * half, half)
    for p in range(chunks):
        here = lanes(core * half + p * LANES, LANES)
        there = lanes((1 - core) * half + p * LANES, LANES)
        ctx[:, here] = mine[p][...]
        ctx[:, there] = got[p][...]
    block = 128

    def step(i, carry):
        rows = at(i * block, block)
        hidden[rows, own_cols] = jnp.dot(ctx[rows, :], w_mine[...], preferred_element_type=f32)
        hidden[rows, got_cols] = jnp.dot(ctx[rows, :], w_got[...], preferred_element_type=f32)
        values = hidden[rows, :] + x_ref[rows, :].astype(f32)
        hidden[rows, :] = values
        normal, _ = normal_of(values)
        norm[rows, :] = (normal * gain[...] + bias[...]).astype(bf16)
        return carry

    lax.fori_loop(0, seq_len // block, step, 0)


def out_back_kernel(place, grad, w_mine, w_got, keep, send, grad_send):
    core = place[0]
    seq_len, width = grad.shape
    half = width // 2
    own_cols, got_cols = lanes(core * half, half), lanes((1 - core) * half, half)
    grad_send[...] = grad[:, got_cols]
    for out, part in ((send, 1 - core), (keep, core)):
        rows = at(part * half, half)

        def step(i, carry):
            here = at(i * 256, 256)
            out[here, :] = (
                lax.dot_general(grad[here, own_cols], w_mine[rows, :], contract_cols, preferred_element_type=f32)
                + lax.dot_general(grad[here, got_cols], w_got[rows, :], contract_cols, preferred_element_type=f32)
            ).astype(bf16)
            return carry

        lax.fori_loop(0, seq_len // 256, step, 0)


def spread(place, outs, product):
    if len(outs) > 1:
        span = outs[0].shape[0]
        for j, out in enumerate(outs[:3]):
            out[...] = product(lanes(place[1 + j], span)).astype(bf16)
        corner = product(lanes(place[4], span)).astype(bf16)
        outs[3][...] = corner[: span // 2, :]
        outs[4][...] = corner[span // 2 :, :]
    else:
        for start in range(0, outs[0].shape[0], 256):
            here = slice(start, start + 256)
            outs[0][here, :] = product(here).astype(bf16)


def out_weight_kernel(chunks, place, ctx, grad, grad_got, *refs):
    mine, got, outs, other = refs[:chunks], refs[chunks : 2 * chunks], refs[2 * chunks : -1], refs[-1]
    core = place[0]
    seq_len, width = grad.shape
    half = width // 2
    cols = lanes(core * half, half)
    for p in range(chunks):
        other[:, lanes(core * half + p * LANES, LANES)] = mine[p][...]
        other[:, lanes((1 - core) * half + p * LANES, LANES)] = got[p][...]

    def product(here):
        return lax.dot_general(
            ctx[:, here], grad[:, cols], contract_rows, preferred_element_type=f32
        ) + lax.dot_general(other[:, here], grad_got[...], contract_rows, preferred_element_type=f32)

    spread(place, outs, product)


def attend_back_kernel(
    chunk, place, qkv_ref, lse_ref, keep, got, norm, cos_ref, sin_ref, segc_ref, segr_ref, out_ref, *refs
):
    *pieces, gq, gk, gv = refs
    hd = HEAD_DIM
    seq_len = keep.shape[0]
    block = seq_len // 2
    for s, grad_ref in enumerate((keep, got)):
        base = s * seq_len
        for h in range(PAIR):
            lane = slice(chunk * LANES + h * hd, chunk * LANES + (h + 1) * hd)
            for r in (1, 0):
                extent = (r + 1) * block
                rows = slice(base + r * block, base + (r + 1) * block)
                cols = slice(base, base + extent)
                allowed = allowed_block(
                    segc_ref[s, r * block : (r + 1) * block, :],
                    segr_ref[s, :, :extent],
                    r * block,
                    block,
                    extent,
                )
                query = qkv_ref[rows, h * hd : (h + 1) * hd]
                key = qkv_ref[cols, (PAIR + h) * hd : (PAIR + h + 1) * hd]
                value = qkv_ref[cols, (2 * PAIR + h) * hd : (2 * PAIR + h + 1) * hd]
                grad = grad_ref[r * block : (r + 1) * block, lane]
                scores = lax.dot_general(query, key, contract_cols, preferred_element_type=f32)
                scores = jnp.where(allowed, scores * score_scale, -1000000000.0)
                probs = jnp.exp(scores - lse_ref[rows, h : h + 1])
                grad_probs = lax.dot_general(grad, value, contract_cols, preferred_element_type=f32)
                weighted = jnp.sum(probs * grad_probs, axis=-1, keepdims=True)
                grad_scores = (probs * (grad_probs - weighted) * score_scale).astype(bf16)
                probs = probs.astype(bf16)
                gq[r * block : (r + 1) * block, :] = jnp.dot(grad_scores, key, preferred_element_type=f32)
                grad_key = lax.dot_general(grad_scores, query, contract_rows, preferred_element_type=f32)
                grad_value = lax.dot_general(probs, grad, contract_rows, preferred_element_type=f32)
                if r == 1:
                    gk[...] = grad_key
                    gv[...] = grad_value
                else:
                    gk[:block, :] = gk[:block, :] + grad_key
                    gv[:block, :] = gv[:block, :] + grad_value
            sine, cosine = sin_ref[...], cos_ref[...]
            rows = slice(base, base + seq_len)
            grad_query, grad_key = gq[...], gk[...]
            out_ref[rows, h * hd : (h + 1) * hd] = (
                grad_query * cosine + turn_back(grad_query * sine)
            ).astype(bf16)
            out_ref[rows, (PAIR + h) * hd : (PAIR + h + 1) * hd] = (
                grad_key * cosine + turn_back(grad_key * sine)
            ).astype(bf16)
            out_ref[rows, (2 * PAIR + h) * hd : (2 * PAIR + h + 1) * hd] = gv[...].astype(bf16)

    def product(here):
        return lax.dot_general(norm[:, here], out_ref[...], contract_rows, preferred_element_type=f32)

    spread(place, pieces, product)


def ff_act_kernel(chips, place, limits, norm_a, norm_b, cot_a, cot_b, *refs):
    if chips:
        *pieces, act_a, act_b, grad_a, grad_b, up, down = refs
        join(place, chips, pieces, [up, down])
    else:
        up, down, act_a, act_b, grad_a, grad_b = refs
    seq_len = norm_a.shape[0]
    units = up.shape[1]
    block, tile = 256, 256 if units % 256 == 0 else 128
    for s, (norm, cot, act, grad) in enumerate(((norm_a, cot_a, act_a, grad_a), (norm_b, cot_b, act_b, grad_b))):
        limit = limits[s]

        def step(i, carry):
            rows = at(i * block, block)
            for n in range(0, units, tile):
                cols = slice(n, n + tile)
                preact = jnp.dot(norm[rows, :], up[:, cols], preferred_element_type=f32)
                grad_active = jnp.dot(cot[rows, :], down[:, cols], preferred_element_type=f32)
                mask = n + lax.broadcasted_iota(jnp.int32, (block, tile), 1) < limit
                cdf = 0.5 * (1.0 + lax.erf(preact * 0.7071067811865476))
                slope = cdf + preact * jnp.exp(-0.5 * preact * preact) * 0.3989422804014327
                act[rows, cols] = jnp.where(mask, preact * cdf, 0.0).astype(bf16)
                grad[rows, cols] = jnp.where(mask, grad_active * slope, 0.0).astype(bf16)
            return carry

        lax.fori_loop(0, seq_len // block, step, 0)


def rows_back_kernel(count, base, *refs):
    grads, weights, outs = refs[:count], refs[count : 2 * count], refs[2 * count :]
    total = outs[0].shape[0]
    for k, out in enumerate(outs):

        def step(i, carry):
            rows = at(base + k * total + i * 256, 256)
            acc = 0.0
            for g, w in zip(grads, weights):
                acc = acc + lax.dot_general(g[rows, :], w[...], contract_cols, preferred_element_type=f32)
            out[at(i * 256, 256), :] = acc.astype(out.dtype)
            return carry

        lax.fori_loop(0, total // 256, step, 0)


def ff_weight_kernel(count, place, *refs):
    norms, cots = refs[:count], refs[count : 2 * count]
    acts, grads, outs = refs[2 * count : 3 * count], refs[3 * count : 4 * count], refs[4 * count :]
    span = norms[0].shape[1]
    corner = len(outs) == 5
    for j in range(4 if corner else len(outs)):

        @pl.when(pl.program_id(0) == j)
        def _():
            for i, (lefts, rights) in enumerate(((norms, grads), (cots, acts))):
                acc = 0.0
                for left, right in zip(lefts, rights):
                    acc = acc + lax.dot_general(
                        left[...], right[...], contract_rows, preferred_element_type=f32
                    )
                if corner and j == 3:
                    outs[3 + i][...] = acc.astype(bf16)
                else:
                    outs[j][i * span : (i + 1) * span, :] = acc.astype(bf16)


def ff_weight(order, chips, norms, cots, acts, grads):
    seq_len, width = norms[0].shape
    units = acts[0].shape[1]
    span = width // chips
    count = len(norms)
    outs = [(2 * span, units)] * chips
    if chips == 4:
        outs = [(2 * span, units)] * 3 + [(span, units)] * 2
    wide = pl.BlockSpec((seq_len, span), lambda j, order: (0, order[j]))
    whole = pl.BlockSpec((seq_len, units), lambda j, order: (0, 0))
    return pl.pallas_call(
        functools.partial(ff_weight_kernel, count),
        out_shape=[shape(v) for v in outs],
        grid_spec=pltpu.PrefetchScalarGridSpec(
            num_scalar_prefetch=1,
            grid=(chips,),
            in_specs=[wide] * (2 * count) + [whole] * (2 * count),
            out_specs=[pl.BlockSpec(v, lambda j, order: (0, 0)) for v in outs],
        ),
        cost_estimate=COST,
        compiler_params=pltpu.CompilerParams(vmem_limit_bytes=VMEM_LIMIT),
        name="ff_weight",
    )(order, *norms, *cots, *acts, *grads)


def second_back_kernel(own, beside_a, beside_b, near, hidden, cot, gain, grad_hidden, grad_low, sums):
    seq_len, width = own.shape
    block = 64
    sums[...] = jnp.zeros_like(sums)

    def step(i, carry, first, beside):
        rows = at(first + i * block, block)
        grad = own[rows, :] + beside[at(i * block, block), :].astype(f32) + near[rows, :].astype(f32)
        normal, inverse = normal_of(hidden[rows, :])
        sums[0:1, :] += jnp.sum(grad * normal, axis=0, keepdims=True)
        sums[1:2, :] += jnp.sum(grad, axis=0, keepdims=True)
        back = cot[rows, :].astype(f32) + norm_back(grad, normal, inverse, gain[...])
        grad_hidden[rows, :] = back
        grad_low[rows, :] = back.astype(bf16)
        return carry

    for k, ref in enumerate((beside_a, beside_b)):
        part = functools.partial(step, first=k * seq_len // 2, beside=ref)
        lax.fori_loop(0, seq_len // 2 // block, part, 0)


def first_back_kernel(own, beside_a, beside_b, x_ref, grad_hidden, gain, out, sums):
    seq_len, width = own.shape
    block = 64
    sums[...] = jnp.zeros_like(sums)

    def step(i, carry, first, beside):
        rows = at(first + i * block, block)
        grad = own[rows, :] + beside[at(i * block, block), :].astype(f32)
        normal, inverse = normal_of(x_ref[rows, :].astype(f32))
        sums[0:1, :] += jnp.sum(grad * normal, axis=0, keepdims=True)
        sums[1:2, :] += jnp.sum(grad, axis=0, keepdims=True)
        out[rows, :] = grad_hidden[rows, :] + norm_back(grad, normal, inverse, gain[...])
        return carry

    for k, ref in enumerate((beside_a, beside_b)):
        part = functools.partial(step, first=k * seq_len // 2, beside=ref)
        lax.fori_loop(0, seq_len // 2 // block, part, 0)


def place_attention_kernel(count, place, *refs):
    mine, got, out = refs[:count], refs[count : 2 * count], refs[2 * count]
    core = place[0]
    rows = out.shape[0]
    width = out.shape[1] // 3
    half = width // 2
    here = at(core * rows, rows)
    for p in range(count):
        for part in range(3):
            cols = slice(part * LANES, (part + 1) * LANES)
            base = part * width + p * LANES
            out[:, lanes(core * half + base, LANES)] = mine[p][here, cols].astype(f32)
            out[:, lanes((1 - core) * half + base, LANES)] = got[p][here, cols].astype(f32)


def place_halves_kernel(place, *refs):
    mine, got, outs = refs[0], refs[1], refs[2:]
    core = place[0]
    rows = outs[0].shape[0]
    half = outs[0].shape[1] // 2
    for i, out in enumerate(outs):
        here = at(core * rows + i * 2 * rows, rows)
        out[:, lanes(core * half, half)] = mine[here, :].astype(f32)
        out[:, lanes((1 - core) * half, half)] = got[here, :].astype(f32)


def tie(value, *others):
    return lax.optimization_barrier((value, *others))[0]


def build(dp_size, mp_size):
    total = dp_size * mp_size
    chip_bits = []
    bit = 2 * mp_size
    while bit < total:
        chip_bits.append(bit)
        bit *= 2
    core_bit = mp_size
    near_bit = 1
    far_bits = []
    bit = 2
    while bit < mp_size:
        far_bits.append(bit)
        bit *= 2
    chips = dp_size // 2

    def flip(value, bit):
        return lax.ppermute(value, AXES, [(i, i ^ bit) for i in range(total)])

    def add(a, b):
        return a.astype(f32) + b.astype(f32)

    def add_low(a, b):
        return add(a, b).astype(bf16)

    class Line:
        def __init__(self):
            self.last = []
            self.open = {}

        def end(self, *values):
            for v in values:
                self.open.pop(id(v), None)

        def after(self, value, *waits):
            self.end(value, *waits)
            waits = list(waits) + self.last
            return tie(value, *waits) if waits else value

        def wait(self, *transfers):
            self.end(*transfers)
            self.last = self.last + list(transfers)

        def send(self, value, bit):
            result = flip(self.after(value), bit)
            self.open[id(result)] = (result, bit)
            return result

        def kernel(self, name, kernel, outs, scalars, *args, wait=(), scratch=()):
            self.end(*args)
            args = (self.after(args[0], *wait),) + args[1:]
            result = run(name, kernel, outs, scalars, *args, scratch=scratch)
            self.last = [result[0] if isinstance(result, (tuple, list)) else result]
            return result

        def op(self, function, *args):
            self.end(*args)
            result = function(self.after(args[0]), *args[1:])
            self.last = [result[0] if isinstance(result, (tuple, list)) else result]
            return result

    two = len(chip_bits) == 2

    class Gather:
        def __init__(self, line, piece):
            self.line, self.piece = line, piece
            if two:
                self.x = line.send(piece, chip_bits[0])
                self.y = line.send(piece, chip_bits[1])
            else:
                held = [line.after(piece)]
                for bit in chip_bits:
                    held = held + [flip(value, bit) for value in held]
                self.all = held

        def turn(self):
            if two:
                half = self.piece.shape[0] // 2
                self.line.wait(self.x, self.y)
                low = self.line.op(lambda v: v[:half], self.x)
                self.low = self.line.send(low, chip_bits[1])
                high = self.line.op(lambda v: v[half:], self.y)
                self.high = self.line.send(high, chip_bits[0])

        def wait(self):
            if two:
                self.line.wait(self.low, self.high)

        def send_first(self, bit):
            if two:
                return [self.line.send(v, bit) for v in (self.x, self.y)]
            return [flip(v, bit) for v in self.all[1:]]

        def send_last(self, bit):
            if two:
                corner = self.line.op(lambda a, b: jnp.concatenate([a, b]), self.low, self.high)
                return [self.line.send(corner, bit)]
            return []

        def pieces(self):
            return [self.piece, self.x, self.y, self.low, self.high] if two else self.all

    class Scatter:
        def __init__(self, line, parts):
            self.line, self.parts = line, parts
            if two:
                self.low = line.send(parts[3], chip_bits[0])
                self.high = line.send(parts[4], chip_bits[1])

        def turn(self):
            if two:
                _, to_x, to_y, low, high = self.parts
                half = low.shape[0]
                self.line.wait(self.low, self.high)
                to_y = self.line.op(lambda v, g: v.at[:half].set(add_low(v[:half], g)), to_y, self.low)
                self.y = self.line.send(to_y, chip_bits[1])
                to_x = self.line.op(lambda v, g: v.at[half:].set(add_low(v[half:], g)), to_x, self.high)
                self.x = self.line.send(to_x, chip_bits[0])

        def close(self):
            if two:
                return self.line.op(
                    lambda own, a, b: (add(own, a) + b.astype(f32)).astype(bf16),
                    self.parts[0],
                    self.x,
                    self.y,
                )
            held = list(self.parts)
            for bit in reversed(chip_bits):
                middle = len(held) // 2
                held = [add_low(a, flip(b, bit)) for a, b in zip(held[:middle], held[middle:])]
            return held[0]

    class OverMp:
        def __init__(self, line, share):
            self.line = line
            size = share.shape[0] // 2
            self.upper = lax.axis_index("mp") % 2
            send = line.op(lambda v: lax.dynamic_slice_in_dim(v, (1 - self.upper) * size, size, axis=0), share)
            self.keep = lax.dynamic_slice_in_dim(share, self.upper * size, size, axis=0)
            self.got = line.send(send, near_bit)

        def turn(self):
            value = self.line.op(add_low, self.keep, self.got)
            for bit in far_bits[:-1]:
                value = add_low(value, flip(value, bit))
            self.keep = value
            self.got = self.line.send(value, far_bits[-1])

        def back(self):
            self.keep = self.line.op(add_low, self.keep, self.got)
            self.got = self.line.send(self.keep, near_bit)

        def close(self):
            def joined(keep, got):
                low = jnp.where(self.upper == 0, keep, got)
                return jnp.concatenate([low, jnp.where(self.upper == 0, got, keep)])

            return self.line.op(joined, self.keep, self.got)

    class SumAll:
        def __init__(self, line, value):
            self.line, self.value, self.bit = line, value, 1
            self.got = line.send(value, 1)

        def turn(self):
            if self.bit < total:
                self.value = self.line.op(jnp.add, self.value, self.got)
                self.bit *= 2
                if self.bit < total:
                    self.got = self.line.send(self.value, self.bit)

        def close(self):
            while self.bit < total:
                self.turn()
            return self.value

    def on_device(
        block_in,
        cotangent,
        segment_ids,
        granularity,
        w_qkv,
        w_out,
        w_up,
        w_down,
        norm1_gain,
        norm1_bias,
        norm2_gain,
        norm2_bias,
    ):
        seq_len, width = block_in.shape
        rows = width // dp_size
        units = w_up.shape[1]
        half_units = units // 2
        half = width // 2
        dp = lax.axis_index("dp")
        mp = lax.axis_index("mp")
        core = dp % 2
        chip = dp // 2
        span = 2 * rows
        order = jnp.stack([chip ^ j for j in range(chips)]).astype(jnp.int32)
        place = jnp.concatenate([core[None].astype(jnp.int32), order * span])
        chunks = HEADS // 2 // PAIR
        chunk_cols = 3 * LANES
        gain1, bias1 = norm1_gain[None], norm1_bias[None]
        gain2, bias2 = norm2_gain[None], norm2_bias[None]
        line = Line()

        def parts_shapes(cols):
            if span % 128 == 0 and chips == 4:
                return [shape((span, cols))] * 3 + [shape((rows, cols))] * 2
            return [shape((width, cols))]

        def by_chip(parts):
            if len(parts) > 1:
                return parts
            return [lax.dynamic_slice_in_dim(parts[0], place[1 + j], span, axis=0) for j in range(chips)]

        def ff_parts(*groups):
            if span % 128 == 0 and chips == 4:
                return ff_weight(order, chips, *groups)
            blocks = width // 256
            parts = ff_weight(jnp.arange(blocks, dtype=jnp.int32), blocks, *groups)
            sides = [
                by_chip([jnp.concatenate([v[i * 256 : (i + 1) * 256] for v in parts])]) for i in range(2)
            ]
            return [jnp.concatenate(v) for v in zip(*sides)]

        w_down_t = w_down.T
        qkv_other = line.send(w_qkv, core_bit)
        tokens = jnp.concatenate([block_in, cotangent])
        tokens_other = line.send(tokens, core_bit)
        if units == width:
            rest = jnp.concatenate([w_out, w_up, w_down_t])
        else:
            rest = jnp.concatenate([w_out, jnp.concatenate([w_up, w_down_t], axis=1)])
        rest_other = line.send(rest, core_bit)
        small = jnp.concatenate([segment_ids, jnp.broadcast_to(granularity[:, None], (mp_size, seq_len))])
        small_other = line.send(small, core_bit)

        qkv_pieces = line.kernel(
            "cut_attention",
            cut_attention_kernel,
            [shape((span, chunk_cols))] * chunks,
            [place],
            w_qkv,
            qkv_other,
        )
        heads = [Gather(line, qkv_pieces[0])]
        normed1 = line.kernel(
            "norm",
            norm_kernel,
            shape((2 * seq_len, width)),
            [],
            block_in,
            tokens_other,
            gain1,
            bias1,
        )
        out_piece, out_piece_got, ff_piece = line.kernel(
            "cut_rest",
            cut_rest_kernel,
            [shape((span, half))] * 2 + [shape((2 * span, half_units))],
            [place],
            w_out,
            w_up,
            w_down_t,
            rest_other,
            wait=(small_other,),
        )
        heads.append(Gather(line, qkv_pieces[1]))
        small_other = line.after(small_other)
        segments = jnp.stack([small[0], small_other[0]])
        seg_col = segments[:, :, None]
        seg_row = segments[:, None, :]
        cosine, sine = rotary_tables(seq_len, HEAD_DIM)
        levels = jnp.stack([small[1:, 0], small_other[1:, 0]])
        limits = BLOCK * jnp.power(2, levels)
        limits = jnp.stack([limits[0, mp], limits[1, mp], limits[0, mp ^ 1], limits[1, mp ^ 1]])
        starts = [(mp ^ (2 * k)) * units + core * half_units for k in range(mp_size // 2)]
        limits = [(limits - start).astype(jnp.int32) for start in starts]
        last = mp_size // 2 - 1

        qkv_wide, qkv_low, contexts, logs = [], [], [], []

        def attend(p):
            a, b, c, d = line.kernel(
                "attend",
                functools.partial(attend_kernel, chips, seq_len),
                [
                    shape((width, chunk_cols)),
                    shape((2 * seq_len, chunk_cols)),
                    shape((2, seq_len, LANES)),
                    shape((2 * seq_len, HEAD_DIM), f32),
                ],
                [place],
                normed1,
                cosine,
                sine,
                seg_col,
                seg_row,
                *heads[p].pieces(),
            )
            qkv_wide.append(a)
            qkv_low.append(b)
            contexts.append(c)
            logs.append(d)

        heads[0].turn()
        slices = [ff_piece]
        for bit in far_bits:
            slices = slices + [line.send(v, bit) for v in slices]
        heads[1].turn()
        heads[0].wait()
        heads.append(Gather(line, qkv_pieces[2]))
        attend(0)
        heads[1].wait()
        heads[2].turn()
        outs = Gather(line, out_piece)
        attend(1)
        heads[2].wait()
        ctx_near = [line.send(c[1], core_bit) for c in contexts]
        outs.turn()
        line.wait(*ctx_near)
        outs_other = [out_piece_got] + outs.send_first(core_bit)
        line.wait(*outs_other[1:], *slices[1:])
        ffs = {last: Gather(line, slices[last])}
        cot_near = line.send(cotangent, near_bit)
        attend(2)
        outs.wait()
        ctx_near.append(line.send(contexts[2][1], core_bit))
        outs_other += outs.send_last(core_bit)
        out_mine, out_got = line.kernel(
            "join",
            functools.partial(join_kernel, chips, len(outs.pieces())),
            [shape((width, half))] * 2,
            [place],
            *outs.pieces(),
            *outs_other,
        )
        line.wait(ctx_near[2])
        ffs[last].turn()
        hidden1, normed2, context = line.kernel(
            "out",
            functools.partial(out_kernel, chunks),
            [shape((seq_len, width), f32), shape((seq_len, width)), shape((seq_len, width))],
            [place],
            block_in,
            *[c[0] for c in contexts],
            *ctx_near,
            out_mine,
            out_got,
            gain2,
            bias2,
        )

        norm_near = line.send(normed2, near_bit)
        norm_core = line.send(normed2, core_bit)
        ffs[last].wait()
        line.wait(norm_core, cot_near)
        for k in range(last - 1, -1, -1):
            ffs[k] = Gather(line, slices[k])
        cot_both = line.send(cot_near, core_bit)
        cot_core = line.after(tokens_other)[seq_len:]
        cot_rows = [cotangent, cot_core, cot_near, cot_both]
        outs_ff = [shape((seq_len, half_units))] * 4
        wide_ff = [shape((width, half_units))] * 2
        acts, grads, ups, downs = {}, {}, {}, {}

        def ff_own(k):
            act_a, act_b, grad_a, grad_b, up, down = line.kernel(
                "ff_own",
                functools.partial(ff_act_kernel, chips),
                outs_ff + wide_ff,
                [place, limits[k][:2]],
                normed2,
                norm_core,
                *cot_rows[:2],
                *ffs[k].pieces(),
            )
            acts[k] = [act_a, act_b]
            grads[k] = [grad_a, grad_b]
            ups[k] = up
            downs[k] = down

        def ff_near(k):
            act_a, act_b, grad_a, grad_b = line.kernel(
                "ff_near",
                functools.partial(ff_act_kernel, 0),
                outs_ff,
                [place, limits[k][2:]],
                norm_near,
                norm_both,
                *cot_rows[2:],
                ups[k],
                downs[k],
            )
            acts[k] += [act_a, act_b]
            grads[k] += [grad_a, grad_b]

        def ff_grads(k):
            lefts = [line.after(normed2), norm_core, norm_near, norm_both]
            parts = ff_parts(lefts, cot_rows, acts[k], grads[k])
            line.last = [parts[0]]
            return Scatter(line, parts)

        def rows_back(name, lefts, i, weights, kind):
            outs = [shape((seq_len, width), kind)] if kind == f32 else [shape((seq_len // 2, width))] * 2
            result = line.kernel(
                name,
                functools.partial(rows_back_kernel, len(weights), 0),
                outs,
                [],
                *[v[i] for v in lefts.values()],
                *weights.values(),
            )
            return result[0] if kind == f32 else result

        def add_halves(a, low, high):
            middle = a.shape[0] // 2
            return jnp.concatenate([add_low(a[:middle], low), add_low(a[middle:], high)])

        ff_own(last)
        line.wait(cot_both)
        for k in range(last - 1, -1, -1):
            ffs[k].turn()
        line.wait(norm_near)
        norm_both = line.send(norm_near, core_bit)
        ctx_far = [line.send(c[0], core_bit) for c in contexts[:2]]
        ff_near(last)
        ctx_far.append(line.send(contexts[2][0], core_bit))
        line.wait(*ctx_far)
        scatters = {last: ff_grads(last)}
        for k in range(last - 1, -1, -1):
            ff_own(k)
            if k == last - 1:
                scatters[last].turn()
            ff_near(k)
        back_both = rows_back("ff_back", grads, 3, ups, bf16)
        back_both = [line.send(v, core_bit) for v in back_both]
        back_near = rows_back("ff_back", grads, 2, ups, f32)
        back_near = line.op(add_halves, back_near, *back_both)
        back_near = line.send(back_near, near_bit)
        held = {last: scatters[last].close()}
        for k in range(last - 1, -1, -1):
            scatters[k] = ff_grads(k)
        back_beside = rows_back("ff_back", grads, 1, ups, bf16)
        for k in range(last - 1, -1, -1):
            scatters[k].turn()
        back_beside = [line.send(v, core_bit) for v in back_beside]
        back_own = rows_back("ff_back", grads, 0, ups, f32)

        grad_hidden1, grad_attn, sums2 = line.kernel(
            "second_back",
            second_back_kernel,
            [shape((seq_len, width), f32), shape((seq_len, width)), shape((8, width), f32)],
            [],
            back_own,
            *back_beside,
            back_near,
            hidden1,
            cotangent,
            gain2,
        )
        far_got = line.send(held[last], far_bits[0]) if len(far_bits) == 1 else None
        keep, send, grad_send = line.kernel(
            "out_back",
            out_back_kernel,
            [shape((seq_len, half))] * 3,
            [place],
            grad_attn,
            out_mine,
            out_got,
        )
        context_got = line.send(send, core_bit)
        grad_got = line.send(grad_send, core_bit)
        fore_both = rows_back("ff_fore", acts, 3, downs, bf16)
        line.wait(context_got, grad_got)
        grad_low, qkv_scatters = [], []

        def attend_back(p):
            low, *parts = line.kernel(
                "attend_back",
                functools.partial(attend_back_kernel, p),
                [shape((2 * seq_len, chunk_cols))] + parts_shapes(chunk_cols),
                [place],
                qkv_low[p],
                logs[p],
                keep,
                context_got,
                normed1,
                cosine,
                sine,
                seg_col,
                seg_row,
                scratch=[pltpu.VMEM((seq_len, HEAD_DIM), f32)] * 3,
            )
            grad_low.append(low)
            return by_chip(parts)

        parts = attend_back(0)
        if len(far_bits) == 1:
            own_sum = scatters[0].close()
        else:
            for k in range(last - 1, -1, -1):
                held[k] = scatters[k].close()
        qkv_scatters.append(Scatter(line, parts))
        fore_both = [line.send(v, core_bit) for v in fore_both]
        fore_near = rows_back("ff_fore", acts, 2, downs, f32)
        fore_near = line.op(add_halves, fore_near, *fore_both)
        qkv_scatters[0].turn()
        fore_near = line.send(fore_near, near_bit)
        parts = attend_back(1)
        if len(far_bits) == 1:
            ff_share = line.op(add_low, own_sum, far_got)
        else:
            held = [held[k] for k in range(len(slices))]
            for bit in reversed(far_bits):
                middle = len(held) // 2
                held = [add_low(a, flip(c, bit)) for a, c in zip(held[:middle], held[middle:])]
            ff_share = held[0]
        qkv_scatters.append(Scatter(line, parts))
        out_parts = line.kernel(
            "out_weight",
            functools.partial(out_weight_kernel, chunks),
            parts_shapes(half),
            [place],
            context,
            grad_attn,
            grad_got,
            *[c[1] for c in contexts],
            *ctx_far,
            scratch=[pltpu.VMEM((seq_len, width), bf16)],
        )
        qkv_z = [OverMp(line, qkv_scatters[0].close())]
        qkv_scatters[1].turn()
        parts = attend_back(2)
        line.wait(fore_near)
        qkv_scatters.append(Scatter(line, parts))
        qkv_z[0].turn()
        qkv_z.append(OverMp(line, qkv_scatters[1].close()))
        qkv_scatters[2].turn()
        back_other = line.kernel(
            "qkv_back",
            functools.partial(rows_back_kernel, chunks, seq_len),
            [shape((seq_len // 2, width))] * 2,
            [],
            *grad_low,
            *qkv_wide,
        )
        qkv_z[0].back()
        qkv_z[1].turn()
        shares = [qkv_z[0].close()]
        out_scatter = Scatter(line, by_chip(out_parts))
        qkv_z.append(OverMp(line, qkv_scatters[2].close()))
        out_scatter.turn()
        qkv_z[1].back()
        back_mine = line.kernel(
            "qkv_back",
            functools.partial(rows_back_kernel, chunks, 0),
            [shape((seq_len, width), f32)],
            [],
            *grad_low,
            *qkv_wide,
        )[0]
        qkv_z[2].turn()
        shares.append(qkv_z[1].close())
        back_other_got = [line.send(v, core_bit) for v in back_other]
        out_z = OverMp(line, out_scatter.close())
        grad_input, sums1 = line.kernel(
            "first_back",
            first_back_kernel,
            [shape((seq_len, width), f32), shape((8, width), f32)],
            [],
            back_mine,
            *back_other_got,
            block_in,
            grad_hidden1,
            gain1,
        )
        qkv_z[2].back()
        out_z.turn()
        sums = SumAll(line, jnp.concatenate([sums1[:2], sums2[:2]]))
        fore_beside = rows_back("ff_fore", acts, 1, downs, bf16)
        shares.append(qkv_z[2].close())
        out_z.back()
        sums.turn()
        shares_got = [line.send(v, core_bit) for v in shares]
        fore_own = rows_back("ff_fore", acts, 0, downs, f32)
        line.wait(*shares_got)
        sums.turn()
        out_share = out_z.close()
        ff_share_got = line.send(ff_share, core_bit)
        out_share_got = line.send(out_share, core_bit)
        fore_beside = [line.send(v, core_bit) for v in fore_beside]
        grad_w_qkv = line.kernel(
            "place_qkv",
            functools.partial(place_attention_kernel, chunks),
            shape((rows, 3 * width), f32),
            [place],
            *shares,
            *shares_got,
        )
        sums.turn()
        grad_w_up, grad_w_down = line.kernel(
            "place_ff",
            place_halves_kernel,
            [shape((rows, units), f32)] * 2,
            [place],
            ff_share,
            ff_share_got,
        )
        grad_w_down = grad_w_down.T
        sums.turn()
        grad_w_out = line.kernel(
            "place_out",
            place_halves_kernel,
            [shape((rows, width), f32)],
            [place],
            out_share,
            out_share_got,
        )[0]
        sums = sums.close()

        def finish(base, own, near, low, high):
            middle = own.shape[0] // 2
            total_rows = base + own + near.astype(f32)
            return jnp.concatenate(
                [total_rows[:middle] + low.astype(f32), total_rows[middle:] + high.astype(f32)]
            ).astype(bf16)

        block_out = line.op(finish, hidden1, fore_own, fore_near, *fore_beside)
        return (
            block_out,
            grad_input,
            grad_w_qkv,
            grad_w_out,
            grad_w_up,
            grad_w_down,
            sums[0],
            sums[1],
            sums[2],
            sums[3],
        )

    return on_device


def solution(mesh):
    return jax.shard_map(
        build(mesh.shape["dp"], mesh.shape["mp"]),
        mesh=mesh,
        in_specs=(
            P(("dp", "mp"), None),
            P(("dp", "mp"), None),
            P(("dp", "mp"), None),
            P("dp"),
            P("dp", None),
            P("dp", None),
            P("dp", "mp"),
            P("mp", "dp"),
            P(),
            P(),
            P(),
            P(),
        ),
        out_specs=(
            P(("dp", "mp"), None),
            P(("dp", "mp"), None),
            P("dp", None),
            P("dp", None),
            P("dp", "mp"),
            P("mp", "dp"),
            P(),
            P(),
            P(),
            P(),
        ),
        check_vma=False,
    )
```

```python
import functools
import math

import jax
import jax.numpy as jnp
import numpy as np
from jax import lax
from jax.experimental import pallas as pl
from jax.experimental.pallas import tpu as pltpu
from jax.sharding import PartitionSpec as P

HEADS = 12
HEAD_DIM = 128
BLOCK = 768
AXES = ("dp", "mp")
PAIR = 2
LANES = PAIR * HEAD_DIM

epsilon = 1e-05
theta_base = 10000.0
score_scale = HEAD_DIM ** (-0.5)
contract_rows = (((0,), (0,)), ((), ()))
contract_cols = (((1,), (1,)), ((), ()))
f32 = jnp.float32
bf16 = jnp.bfloat16
SMEM_SPEC = pl.BlockSpec(memory_space=pltpu.SMEM)
VMEM_SPEC = pl.BlockSpec(memory_space=pltpu.VMEM)


def rotary_tables(length, head_width):
    halfway = head_width // 2
    frequency = np.float32(theta_base) ** (np.float32(-2.0) * np.arange(halfway, dtype=np.float32) / head_width)
    angles = np.arange(length, dtype=np.float32)[:, None] * frequency.astype(np.float32)[None, :]
    angles = np.concatenate([angles, angles], axis=1).astype(np.float64)
    return jnp.asarray(np.cos(angles), f32), jnp.asarray(np.sin(angles), f32)


def turn(values):
    halfway = values.shape[-1] // 2
    return jnp.concatenate([-values[:, halfway:], values[:, :halfway]], axis=-1)


def turn_back(values):
    halfway = values.shape[-1] // 2
    return jnp.concatenate([values[:, halfway:], -values[:, :halfway]], axis=-1)


def at(start, size):
    return pl.ds(pl.multiple_of(start, size), size)


def lanes(start, size):
    return pl.ds(pl.multiple_of(start, 128), size)


def normal_of(values):
    average = jnp.mean(values, axis=-1, keepdims=True)
    centred = values - average
    variance = jnp.mean(centred * centred, axis=-1, keepdims=True)
    inverse = lax.rsqrt(variance + epsilon)
    return centred * inverse, inverse


def norm_back(grad, normal, inverse, gain):
    scaled = grad * gain
    mean = jnp.mean(scaled, axis=-1, keepdims=True)
    mean_normal = jnp.mean(scaled * normal, axis=-1, keepdims=True)
    return (scaled - mean - normal * mean_normal) * inverse


COST = pl.CostEstimate(flops=1000000, bytes_accessed=0, transcendentals=0)


EXTRA = 6 * 1024 * 1024


def room(value):
    return math.prod(value.shape) * jnp.dtype(value.dtype).itemsize


def run(name, kernel, outs, scalars, *args, scratch=()):
    many = isinstance(outs, (tuple, list))
    held = sum(room(v) for v in args) + sum(room(v) for v in (outs if many else [outs]))
    held += sum(room(v) for v in scratch)
    return pl.pallas_call(
        kernel,
        out_shape=outs,
        in_specs=[SMEM_SPEC] * len(scalars) + [VMEM_SPEC] * len(args),
        out_specs=[VMEM_SPEC] * len(outs) if many else VMEM_SPEC,
        scratch_shapes=list(scratch),
        cost_estimate=COST,
        compiler_params=pltpu.CompilerParams(vmem_limit_bytes=held + EXTRA),
        name=name,
    )(*scalars, *args)


def shape(dims, kind=bf16):
    return jax.ShapeDtypeStruct(tuple(dims), kind)


def cut_attention_kernel(place, own_qkv, got_qkv, *outs):
    core = place[0]
    rows, width = own_qkv.shape
    width = width // 3
    half = width // 2
    mine, theirs = at(core * rows, rows), at((1 - core) * rows, rows)
    for p, out in enumerate(outs):
        for part in range(3):
            cols = lanes(core * half + (part * width + p * LANES), LANES)
            here = slice(part * LANES, (part + 1) * LANES)
            out[mine, here] = own_qkv[:, cols]
            out[theirs, here] = got_qkv[:, cols]


def cut_rest_kernel(place, own_out, own_up, own_down, got, out_piece, out_piece_got, ff_piece):
    core = place[0]
    rows, width = own_out.shape
    half = width // 2
    for out, part in ((out_piece, core), (out_piece_got, 1 - core)):
        cols = lanes(part * half, half)
        out[at(core * rows, rows), :] = own_out[:, cols]
        out[at((1 - core) * rows, rows), :] = got[:rows, cols]
    half = own_up.shape[1] // 2
    cols = lanes(core * half, half)
    units = own_up.shape[1]
    for i, own in enumerate((own_up, own_down)):
        ff_piece[at(core * rows + i * 2 * rows, rows), :] = own[:, cols]
        if units == width:
            ff_piece[at((1 - core) * rows + i * 2 * rows, rows), :] = got[(1 + i) * rows : (2 + i) * rows, cols]
        else:
            cols_got = lanes(core * half + i * units, half)
            ff_piece[at((1 - core) * rows + i * 2 * rows, rows), :] = got[rows:, cols_got]


def join(place, chips, pieces, outs):
    parts = len(outs)
    span = pieces[0].shape[0] // parts
    for j in range(min(chips, len(pieces))):
        for i, out in enumerate(outs):
            rows = at(place[1 + j], span)
            if len(pieces) == chips or j < chips - 1:
                out[rows, :] = pieces[j][i * span : (i + 1) * span, :]
            elif parts == 1:
                half = span // 2
                out[pl.ds(pl.multiple_of(place[1 + j], half), half), :] = pieces[j][...]
                out[pl.ds(pl.multiple_of(place[1 + j] + half, half), half), :] = pieces[j + 1][...]
            else:
                out[rows, :] = pieces[j + i][...]


def join_kernel(chips, many, place, *refs):
    *pieces, mine, got = refs
    join(place, chips, pieces[:many], [mine])
    join(place, chips, pieces[many:], [got])


def norm_kernel(own, other, gain, bias, out):
    seq_len = own.shape[0]
    block = 128

    def step(i, carry):
        rows = at(i * block, block)
        for k, ref in enumerate((own, other)):
            normal, _ = normal_of(ref[rows, :].astype(f32))
            out[at(k * seq_len + i * block, block), :] = (normal * gain[...] + bias[...]).astype(bf16)
        return carry

    lax.fori_loop(0, seq_len // block, step, 0)


def allowed_block(seg_col, seg_row, row_start, block, extent):
    row_place = row_start + lax.broadcasted_iota(jnp.int32, (block, extent), 0)
    col_place = lax.broadcasted_iota(jnp.int32, (block, extent), 1)
    return (row_place >= col_place) & (seg_col == seg_row)


def attend_kernel(chips, seq_len, place, norm_ref, cos_ref, sin_ref, segc_ref, segr_ref, *refs):
    *pieces, wide_ref, qkv_ref, ctx_ref, lse_ref = refs
    join(place, chips, pieces, [wide_ref])
    hd = HEAD_DIM
    block = seq_len // 2

    def project(i, carry):
        rows = at(i * block, block)
        joined = jnp.dot(norm_ref[rows, :], wide_ref[...], preferred_element_type=f32)
        table = at((i % 2) * block, block)
        cosine, sine = cos_ref[table, :], sin_ref[table, :]
        for h in range(2 * PAIR):
            part = joined[:, h * hd : (h + 1) * hd]
            qkv_ref[rows, h * hd : (h + 1) * hd] = (part * cosine + turn(part) * sine).astype(bf16)
        qkv_ref[rows, 2 * PAIR * hd :] = joined[:, 2 * PAIR * hd :].astype(bf16)
        return carry

    lax.fori_loop(0, 4, project, 0)

    lane = lax.broadcasted_iota(jnp.int32, (block, hd), 1)

    def sequence(s, carry):
        base = s * seq_len
        for r in range(2):
            extent = (r + 1) * block
            rows = at(base + r * block, block)
            cols = pl.ds(pl.multiple_of(base, block), extent)
            allowed = allowed_block(
                segc_ref[s, r * block : (r + 1) * block, :],
                segr_ref[s, :, :extent],
                r * block,
                block,
                extent,
            )
            logs = jnp.zeros((block, hd), f32)
            for h in range(PAIR):
                query = qkv_ref[rows, h * hd : (h + 1) * hd]
                key = qkv_ref[cols, (PAIR + h) * hd : (PAIR + h + 1) * hd]
                value = qkv_ref[cols, (2 * PAIR + h) * hd : (2 * PAIR + h + 1) * hd]
                scores = lax.dot_general(query, key, contract_cols, preferred_element_type=f32)
                scores = jnp.where(allowed, scores * score_scale, -1000000000.0)
                top = jnp.max(scores, axis=-1, keepdims=True)
                weight = jnp.exp(scores - top)
                total = jnp.sum(weight, axis=-1, keepdims=True)
                probs = (weight * (1.0 / total)).astype(bf16)
                ctx_ref[s, r * block : (r + 1) * block, h * hd : (h + 1) * hd] = jnp.dot(
                    probs, value, preferred_element_type=f32
                ).astype(bf16)
                logs = jnp.where(lane == h, top + jnp.log(total), logs)
            lse_ref[rows, :] = logs
        return carry

    lax.fori_loop(0, 2, sequence, 0)


def out_kernel(chunks, place, x_ref, *refs):
    mine, got = refs[:chunks], refs[chunks : 2 * chunks]
    w_mine, w_got, gain, bias, hidden, norm, ctx = refs[2 * chunks :]
    core = place[0]
    seq_len, width = x_ref.shape
    half = width // 2
    own_cols, got_cols = lanes(core * half, half), lanes((1 - core) * half, half)
    for p in range(chunks):
        here = lanes(core * half + p * LANES, LANES)
        there = lanes((1 - core) * half + p * LANES, LANES)
        ctx[:, here] = mine[p][...]
        ctx[:, there] = got[p][...]
    block = 128

    def step(i, carry):
        rows = at(i * block, block)
        hidden[rows, own_cols] = jnp.dot(ctx[rows, :], w_mine[...], preferred_element_type=f32)
        hidden[rows, got_cols] = jnp.dot(ctx[rows, :], w_got[...], preferred_element_type=f32)
        values = hidden[rows, :] + x_ref[rows, :].astype(f32)
        hidden[rows, :] = values
        normal, _ = normal_of(values)
        norm[rows, :] = (normal * gain[...] + bias[...]).astype(bf16)
        return carry

    lax.fori_loop(0, seq_len // block, step, 0)


def out_back_kernel(place, grad, w_mine, w_got, keep, send, grad_send):
    core = place[0]
    seq_len, width = grad.shape
    half = width // 2
    own_cols, got_cols = lanes(core * half, half), lanes((1 - core) * half, half)
    grad_send[...] = grad[:, got_cols]
    for out, part in ((send, 1 - core), (keep, core)):
        rows = at(part * half, half)

        def step(i, carry):
            here = at(i * 256, 256)
            out[here, :] = (
                lax.dot_general(grad[here, own_cols], w_mine[rows, :], contract_cols, preferred_element_type=f32)
                + lax.dot_general(grad[here, got_cols], w_got[rows, :], contract_cols, preferred_element_type=f32)
            ).astype(bf16)
            return carry

        lax.fori_loop(0, seq_len // 256, step, 0)


def spread(place, outs, product):
    if len(outs) > 1:
        span = outs[0].shape[0]
        for j, out in enumerate(outs[:3]):
            out[...] = product(lanes(place[1 + j], span)).astype(bf16)
        corner = product(lanes(place[4], span)).astype(bf16)
        outs[3][...] = corner[: span // 2, :]
        outs[4][...] = corner[span // 2 :, :]
    else:
        for start in range(0, outs[0].shape[0], 256):
            here = slice(start, start + 256)
            outs[0][here, :] = product(here).astype(bf16)


def out_weight_kernel(chunks, place, ctx, grad, grad_got, *refs):
    mine, got, outs, other = refs[:chunks], refs[chunks : 2 * chunks], refs[2 * chunks : -1], refs[-1]
    core = place[0]
    seq_len, width = grad.shape
    half = width // 2
    cols = lanes(core * half, half)
    for p in range(chunks):
        other[:, lanes(core * half + p * LANES, LANES)] = mine[p][...]
        other[:, lanes((1 - core) * half + p * LANES, LANES)] = got[p][...]

    def product(here):
        return lax.dot_general(
            ctx[:, here], grad[:, cols], contract_rows, preferred_element_type=f32
        ) + lax.dot_general(other[:, here], grad_got[...], contract_rows, preferred_element_type=f32)

    spread(place, outs, product)


def attend_back_kernel(
    chunk, place, qkv_ref, lse_ref, keep, got, norm, cos_ref, sin_ref, segc_ref, segr_ref, out_ref, *refs
):
    *pieces, gq, gk, gv = refs
    hd = HEAD_DIM
    seq_len = keep.shape[0]
    block = seq_len // 2
    for s, grad_ref in enumerate((keep, got)):
        base = s * seq_len
        for h in range(PAIR):
            lane = slice(chunk * LANES + h * hd, chunk * LANES + (h + 1) * hd)
            for r in (1, 0):
                extent = (r + 1) * block
                rows = slice(base + r * block, base + (r + 1) * block)
                cols = slice(base, base + extent)
                allowed = allowed_block(
                    segc_ref[s, r * block : (r + 1) * block, :],
                    segr_ref[s, :, :extent],
                    r * block,
                    block,
                    extent,
                )
                query = qkv_ref[rows, h * hd : (h + 1) * hd]
                key = qkv_ref[cols, (PAIR + h) * hd : (PAIR + h + 1) * hd]
                value = qkv_ref[cols, (2 * PAIR + h) * hd : (2 * PAIR + h + 1) * hd]
                grad = grad_ref[r * block : (r + 1) * block, lane]
                scores = lax.dot_general(query, key, contract_cols, preferred_element_type=f32)
                scores = jnp.where(allowed, scores * score_scale, -1000000000.0)
                probs = jnp.exp(scores - lse_ref[rows, h : h + 1])
                grad_probs = lax.dot_general(grad, value, contract_cols, preferred_element_type=f32)
                weighted = jnp.sum(probs * grad_probs, axis=-1, keepdims=True)
                grad_scores = (probs * (grad_probs - weighted) * score_scale).astype(bf16)
                probs = probs.astype(bf16)
                gq[r * block : (r + 1) * block, :] = jnp.dot(grad_scores, key, preferred_element_type=f32)
                grad_key = lax.dot_general(grad_scores, query, contract_rows, preferred_element_type=f32)
                grad_value = lax.dot_general(probs, grad, contract_rows, preferred_element_type=f32)
                if r == 1:
                    gk[...] = grad_key
                    gv[...] = grad_value
                else:
                    gk[:block, :] = gk[:block, :] + grad_key
                    gv[:block, :] = gv[:block, :] + grad_value
            sine, cosine = sin_ref[...], cos_ref[...]
            rows = slice(base, base + seq_len)
            grad_query, grad_key = gq[...], gk[...]
            out_ref[rows, h * hd : (h + 1) * hd] = (
                grad_query * cosine + turn_back(grad_query * sine)
            ).astype(bf16)
            out_ref[rows, (PAIR + h) * hd : (PAIR + h + 1) * hd] = (
                grad_key * cosine + turn_back(grad_key * sine)
            ).astype(bf16)
            out_ref[rows, (2 * PAIR + h) * hd : (2 * PAIR + h + 1) * hd] = gv[...].astype(bf16)

    def product(here):
        return lax.dot_general(norm[:, here], out_ref[...], contract_rows, preferred_element_type=f32)

    spread(place, pieces, product)


def ff_act_kernel(chips, index, place, limits, *refs):
    if chips:
        norm_a, norm_b, cot_a, cot_b, *pieces, act_a, act_b, grad_a, grad_b, up, down = refs
        join(place, chips, pieces, [up, down])
        norms = ([norm_a], [norm_b])
        first = 0
    else:
        norm_a, norm_low, norm_high, cot_a, cot_b, up, down, act_a, act_b, grad_a, grad_b = refs
        norms = ([norm_a], [norm_low, norm_high])
        first = 2
    sides = zip(norms, (cot_a, cot_b), (act_a, act_b), (grad_a, grad_b))
    units = up.shape[1]
    block, tile = 256, 256 if units % 256 == 0 else 128
    for s, (norm_parts, cot, act, grad) in enumerate(sides):
        limit = limits[index, first + s]
        for k, norm in enumerate(norm_parts):
            length = norm.shape[0]

            def step(i, carry):
                here = at(i * block, block)
                rows = at(k * length + i * block, block)
                for n in range(0, units, tile):
                    cols = slice(n, n + tile)
                    preact = jnp.dot(norm[here, :], up[:, cols], preferred_element_type=f32)
                    grad_active = jnp.dot(cot[rows, :], down[:, cols], preferred_element_type=f32)
                    mask = n + lax.broadcasted_iota(jnp.int32, (block, tile), 1) < limit
                    cdf = 0.5 * (1.0 + lax.erf(preact * 0.7071067811865476))
                    slope = cdf + preact * jnp.exp(-0.5 * preact * preact) * 0.3989422804014327
                    act[rows, cols] = jnp.where(mask, preact * cdf, 0.0).astype(bf16)
                    grad[rows, cols] = jnp.where(mask, grad_active * slope, 0.0).astype(bf16)
                return carry

            lax.fori_loop(0, length // block, step, 0)


def rows_back_kernel(count, base, *refs):
    grads, weights, outs = refs[:count], refs[count : 2 * count], refs[2 * count :]
    total = outs[0].shape[0]
    for k, out in enumerate(outs):

        def step(i, carry):
            rows = at(base + k * total + i * 256, 256)
            acc = 0.0
            for g, w in zip(grads, weights):
                acc = acc + lax.dot_general(g[rows, :], w[...], contract_cols, preferred_element_type=f32)
            out[at(i * 256, 256), :] = acc.astype(out.dtype)
            return carry

        lax.fori_loop(0, total // 256, step, 0)


def ff_weight_kernel(count, place, *refs):
    norms, cots = refs[:count], refs[count : 2 * count]
    acts, grads, outs = refs[2 * count : 3 * count], refs[3 * count : 4 * count], refs[4 * count :]
    span = norms[0].shape[1]
    corner = len(outs) == 5
    for j in range(4 if corner else len(outs)):

        @pl.when(pl.program_id(0) == j)
        def _():
            for i, (lefts, rights) in enumerate(((norms, grads), (cots, acts))):
                acc = 0.0
                for left, right in zip(lefts, rights):
                    acc = acc + lax.dot_general(
                        left[...], right[...], contract_rows, preferred_element_type=f32
                    )
                if corner and j == 3:
                    outs[3 + i][...] = acc.astype(bf16)
                else:
                    outs[j][i * span : (i + 1) * span, :] = acc.astype(bf16)


def ff_weight(order, chips, norms, cots, acts, grads):
    seq_len, width = norms[0].shape
    units = acts[0].shape[1]
    span = width // chips
    count = len(norms)
    outs = [(2 * span, units)] * chips
    if chips == 4:
        outs = [(2 * span, units)] * 3 + [(span, units)] * 2
    wide = pl.BlockSpec((seq_len, span), lambda j, order: (0, order[j]))
    whole = pl.BlockSpec((seq_len, units), lambda j, order: (0, 0))
    return pl.pallas_call(
        functools.partial(ff_weight_kernel, count),
        out_shape=[shape(v) for v in outs],
        grid_spec=pltpu.PrefetchScalarGridSpec(
            num_scalar_prefetch=1,
            grid=(chips,),
            in_specs=[wide] * (2 * count) + [whole] * (2 * count),
            out_specs=[pl.BlockSpec(v, lambda j, order: (0, 0)) for v in outs],
        ),
        cost_estimate=COST,
        compiler_params=pltpu.CompilerParams(vmem_limit_bytes=40 * 1024 * 1024),
        name="ff_weight",
    )(order, *norms, *cots, *acts, *grads)


def second_back_kernel(own, beside_a, beside_b, near, hidden, cot, gain, grad_hidden, grad_low, sums):
    seq_len, width = own.shape
    block = 64
    sums[...] = jnp.zeros_like(sums)

    def step(i, carry, first, beside):
        rows = at(first + i * block, block)
        grad = own[rows, :] + beside[at(i * block, block), :].astype(f32) + near[rows, :].astype(f32)
        normal, inverse = normal_of(hidden[rows, :])
        sums[0:1, :] += jnp.sum(grad * normal, axis=0, keepdims=True)
        sums[1:2, :] += jnp.sum(grad, axis=0, keepdims=True)
        back = cot[rows, :].astype(f32) + norm_back(grad, normal, inverse, gain[...])
        grad_hidden[rows, :] = back
        grad_low[rows, :] = back.astype(bf16)
        return carry

    for k, ref in enumerate((beside_a, beside_b)):
        part = functools.partial(step, first=k * seq_len // 2, beside=ref)
        lax.fori_loop(0, seq_len // 2 // block, part, 0)


def first_back_kernel(own, beside_a, beside_b, x_ref, grad_hidden, gain, out, sums):
    seq_len, width = own.shape
    block = 64
    sums[...] = jnp.zeros_like(sums)

    def step(i, carry, first, beside):
        rows = at(first + i * block, block)
        grad = own[rows, :] + beside[at(i * block, block), :].astype(f32)
        normal, inverse = normal_of(x_ref[rows, :].astype(f32))
        sums[0:1, :] += jnp.sum(grad * normal, axis=0, keepdims=True)
        sums[1:2, :] += jnp.sum(grad, axis=0, keepdims=True)
        out[rows, :] = grad_hidden[rows, :] + norm_back(grad, normal, inverse, gain[...])
        return carry

    for k, ref in enumerate((beside_a, beside_b)):
        part = functools.partial(step, first=k * seq_len // 2, beside=ref)
        lax.fori_loop(0, seq_len // 2 // block, part, 0)


def place_attention_kernel(count, place, *refs):
    mine, got, out = refs[:count], refs[count : 2 * count], refs[2 * count]
    core = place[0]
    rows = out.shape[0]
    width = out.shape[1] // 3
    half = width // 2
    here = at(core * rows, rows)
    for p in range(count):
        for part in range(3):
            cols = slice(part * LANES, (part + 1) * LANES)
            base = part * width + p * LANES
            out[:, lanes(core * half + base, LANES)] = mine[p][here, cols].astype(f32)
            out[:, lanes((1 - core) * half + base, LANES)] = got[p][here, cols].astype(f32)


def place_halves_kernel(place, *refs):
    mine, got, outs = refs[0], refs[1], refs[2:]
    core = place[0]
    rows = outs[0].shape[0]
    half = outs[0].shape[1] // 2
    for i, out in enumerate(outs):
        here = at(core * rows + i * 2 * rows, rows)
        out[:, lanes(core * half, half)] = mine[here, :].astype(f32)
        out[:, lanes((1 - core) * half, half)] = got[here, :].astype(f32)


def tie(value, *others):
    return lax.optimization_barrier((value, *others))[0]


def build(dp_size, mp_size):
    total = dp_size * mp_size
    chip_bits = []
    bit = 2 * mp_size
    while bit < total:
        chip_bits.append(bit)
        bit *= 2
    core_bit = mp_size
    near_bit = 1
    far_bits = []
    bit = 2
    while bit < mp_size:
        far_bits.append(bit)
        bit *= 2
    chips = dp_size // 2

    def flip(value, bit):
        return lax.ppermute(value, AXES, [(i, i ^ bit) for i in range(total)])

    def add(a, b):
        return a.astype(f32) + b.astype(f32)

    def add_low(a, b):
        return add(a, b).astype(bf16)

    class Line:
        def __init__(self):
            self.last = []
            self.open = {}

        def end(self, *values):
            for v in values:
                self.open.pop(id(v), None)

        def after(self, value, *waits):
            self.end(value, *waits)
            waits = list(waits) + self.last
            return tie(value, *waits) if waits else value

        def wait(self, *transfers):
            self.end(*transfers)
            self.last = self.last + list(transfers)

        def send(self, value, bit):
            result = flip(self.after(value), bit)
            self.open[id(result)] = (result, bit)
            return result

        def kernel(self, name, kernel, outs, scalars, *args, wait=(), scratch=()):
            self.end(*args)
            args = (self.after(args[0], *wait),) + args[1:]
            result = run(name, kernel, outs, scalars, *args, scratch=scratch)
            self.last = [result[0] if isinstance(result, (tuple, list)) else result]
            return result

        def op(self, function, *args):
            self.end(*args)
            result = function(self.after(args[0]), *args[1:])
            self.last = [result[0] if isinstance(result, (tuple, list)) else result]
            return result

    two = len(chip_bits) == 2

    class Gather:
        def __init__(self, line, piece):
            self.line, self.piece = line, piece
            if two:
                self.x = line.send(piece, chip_bits[0])
                self.y = line.send(piece, chip_bits[1])
            else:
                held = [line.after(piece)]
                for bit in chip_bits:
                    held = held + [flip(value, bit) for value in held]
                self.all = held

        def turn(self):
            if two:
                half = self.piece.shape[0] // 2
                self.line.wait(self.x, self.y)
                low = self.line.op(lambda v: v[:half], self.x)
                self.low = self.line.send(low, chip_bits[1])
                high = self.line.op(lambda v: v[half:], self.y)
                self.high = self.line.send(high, chip_bits[0])

        def wait(self):
            if two:
                self.line.wait(self.low, self.high)

        def send_first(self, bit):
            if two:
                return [self.line.send(v, bit) for v in (self.x, self.y)]
            return [flip(v, bit) for v in self.all[1:]]

        def send_last(self, bit):
            if two:
                corner = self.line.op(lambda a, b: jnp.concatenate([a, b]), self.low, self.high)
                return [self.line.send(corner, bit)]
            return []

        def pieces(self):
            return [self.piece, self.x, self.y, self.low, self.high] if two else self.all

    class Scatter:
        def __init__(self, line, parts):
            self.line, self.parts = line, parts
            if two:
                self.low = line.send(parts[3], chip_bits[0])
                self.high = line.send(parts[4], chip_bits[1])

        def turn(self):
            if two:
                _, to_x, to_y, low, high = self.parts
                half = low.shape[0]
                self.line.wait(self.low, self.high)
                to_y = self.line.op(lambda v, g: v.at[:half].set(add_low(v[:half], g)), to_y, self.low)
                self.y = self.line.send(to_y, chip_bits[1])
                to_x = self.line.op(lambda v, g: v.at[half:].set(add_low(v[half:], g)), to_x, self.high)
                self.x = self.line.send(to_x, chip_bits[0])

        def close(self):
            if two:
                return self.line.op(
                    lambda own, a, b: (add(own, a) + b.astype(f32)).astype(bf16),
                    self.parts[0],
                    self.x,
                    self.y,
                )
            held = list(self.parts)
            for bit in reversed(chip_bits):
                middle = len(held) // 2
                held = [add_low(a, flip(b, bit)) for a, b in zip(held[:middle], held[middle:])]
            return held[0]

    class OverMp:
        def __init__(self, line, share):
            self.line = line
            size = share.shape[0] // 2
            self.upper = lax.axis_index("mp") % 2
            send = line.op(lambda v: lax.dynamic_slice_in_dim(v, (1 - self.upper) * size, size, axis=0), share)
            self.keep = lax.dynamic_slice_in_dim(share, self.upper * size, size, axis=0)
            self.got = line.send(send, near_bit)

        def turn(self):
            value = self.line.op(add_low, self.keep, self.got)
            for bit in far_bits[:-1]:
                value = add_low(value, flip(value, bit))
            self.keep = value
            self.got = self.line.send(value, far_bits[-1])

        def back(self):
            self.keep = self.line.op(add_low, self.keep, self.got)
            self.got = self.line.send(self.keep, near_bit)

        def close(self):
            def joined(keep, got):
                low = jnp.where(self.upper == 0, keep, got)
                return jnp.concatenate([low, jnp.where(self.upper == 0, got, keep)])

            return self.line.op(joined, self.keep, self.got)

    class SumAll:
        def __init__(self, line, value):
            self.line, self.value, self.bit = line, value, 1
            self.got = line.send(value, 1)

        def turn(self):
            if self.bit < total:
                self.value = self.line.op(jnp.add, self.value, self.got)
                self.bit *= 2
                if self.bit < total:
                    self.got = self.line.send(self.value, self.bit)

        def close(self):
            while self.bit < total:
                self.turn()
            return self.value

    def on_device(
        block_in,
        cotangent,
        segment_ids,
        granularity,
        w_qkv,
        w_out,
        w_up,
        w_down,
        norm1_gain,
        norm1_bias,
        norm2_gain,
        norm2_bias,
    ):
        seq_len, width = block_in.shape
        rows = width // dp_size
        units = w_up.shape[1]
        half_units = units // 2
        half = width // 2
        dp = lax.axis_index("dp")
        mp = lax.axis_index("mp")
        core = dp % 2
        chip = dp // 2
        span = 2 * rows
        order = jnp.stack([chip ^ j for j in range(chips)]).astype(jnp.int32)
        place = jnp.concatenate([core[None].astype(jnp.int32), order * span])
        chunks = HEADS // 2 // PAIR
        chunk_cols = 3 * LANES
        gain1, bias1 = norm1_gain[None], norm1_bias[None]
        gain2, bias2 = norm2_gain[None], norm2_bias[None]
        line = Line()

        def parts_shapes(cols):
            if span % 128 == 0 and chips == 4:
                return [shape((span, cols))] * 3 + [shape((rows, cols))] * 2
            return [shape((width, cols))]

        def by_chip(parts):
            if len(parts) > 1:
                return parts
            return [lax.dynamic_slice_in_dim(parts[0], place[1 + j], span, axis=0) for j in range(chips)]

        def ff_parts(*groups):
            if span % 128 == 0 and chips == 4:
                return ff_weight(order, chips, *groups)
            blocks = width // 256
            parts = ff_weight(jnp.arange(blocks, dtype=jnp.int32), blocks, *groups)
            sides = [
                by_chip([jnp.concatenate([v[i * 256 : (i + 1) * 256] for v in parts])]) for i in range(2)
            ]
            return [jnp.concatenate(v) for v in zip(*sides)]

        w_down_t = w_down.T
        qkv_other = line.send(w_qkv, core_bit)
        small = jnp.concatenate([segment_ids, jnp.broadcast_to(granularity[:, None], (mp_size, seq_len))])
        small_other = line.send(small, core_bit)
        x_other = line.send(block_in, core_bit)
        if units == width:
            rest = jnp.concatenate([w_out, w_up, w_down_t])
        else:
            rest = jnp.concatenate([w_out, jnp.concatenate([w_up, w_down_t], axis=1)])
        rest_other = line.send(rest, core_bit)

        qkv_pieces = line.kernel(
            "cut_attention",
            cut_attention_kernel,
            [shape((span, chunk_cols))] * chunks,
            [place],
            w_qkv,
            qkv_other,
            wait=(small_other,),
        )
        heads = [Gather(line, qkv_pieces[0])]
        cot_near = line.send(cotangent, near_bit)
        normed1 = line.kernel(
            "norm",
            norm_kernel,
            shape((2 * seq_len, width)),
            [],
            block_in,
            x_other,
            gain1,
            bias1,
        )
        out_piece, out_piece_got, ff_piece = line.kernel(
            "cut_rest",
            cut_rest_kernel,
            [shape((span, half))] * 2 + [shape((2 * span, half_units))],
            [place],
            w_out,
            w_up,
            w_down_t,
            rest_other,
        )
        heads.append(Gather(line, qkv_pieces[1]))
        cosine, sine = rotary_tables(seq_len, HEAD_DIM)
        last = mp_size // 2 - 1

        qkv_wide, qkv_low, contexts, logs = [], [], [], []

        def attend(p):
            a, b, c, d = line.kernel(
                "attend",
                functools.partial(attend_kernel, chips, seq_len),
                [
                    shape((width, chunk_cols)),
                    shape((2 * seq_len, chunk_cols)),
                    shape((2, seq_len, LANES)),
                    shape((2 * seq_len, HEAD_DIM), f32),
                ],
                [place],
                normed1,
                cosine,
                sine,
                seg_col,
                seg_row,
                *heads[p].pieces(),
            )
            qkv_wide.append(a)
            qkv_low.append(b)
            contexts.append(c)
            logs.append(d)

        heads[0].turn()

        def from_small(own, other):
            segments = jnp.stack([own[0], other[0]])
            levels = jnp.stack([own[1:, 0], other[1:, 0]])
            ends = BLOCK * jnp.power(2, levels)
            ends = jnp.stack([ends[0, mp], ends[1, mp], ends[0, mp ^ 1], ends[1, mp ^ 1]])
            starts = [(mp ^ (2 * k)) * units + core * half_units for k in range(mp_size // 2)]
            limits = (ends[None, :] - jnp.stack(starts)[:, None]).astype(jnp.int32)
            return limits, segments[:, :, None], segments[:, None, :]

        limits, seg_col, seg_row = line.op(from_small, small, small_other)
        heads[1].turn()
        heads[0].wait()
        line.wait(cot_near)
        slices = [ff_piece]
        for bit in far_bits:
            slices = slices + [line.send(v, bit) for v in slices]
        heads.append(Gather(line, qkv_pieces[2]))
        attend(0)
        heads[1].wait()
        heads[2].turn()
        outs = Gather(line, out_piece)
        attend(1)
        heads[2].wait()
        ctx_near = [line.send(c[1], core_bit) for c in contexts]
        outs.turn()
        line.wait(*ctx_near)
        outs_other = [out_piece_got] + outs.send_first(core_bit)
        attend(2)
        outs.wait()
        line.wait(*outs_other[1:], *slices[1:])
        ffs = {0: Gather(line, slices[0])}
        ctx_near.append(line.send(contexts[2][1], core_bit))
        outs_other += outs.send_last(core_bit)
        out_mine, out_got = line.kernel(
            "join",
            functools.partial(join_kernel, chips, len(outs.pieces())),
            [shape((width, half))] * 2,
            [place],
            *outs.pieces(),
            *outs_other,
            wait=(ctx_near[2],),
        )
        cot_both = line.send(cot_near, core_bit)
        cot_core = line.send(cotangent, core_bit)
        hidden1, normed2, context = line.kernel(
            "out",
            functools.partial(out_kernel, chunks),
            [shape((seq_len, width), f32), shape((seq_len, width)), shape((seq_len, width))],
            [place],
            block_in,
            *[c[0] for c in contexts],
            *ctx_near,
            out_mine,
            out_got,
            gain2,
            bias2,
        )

        line.wait(cot_both, cot_core)
        norm_near = line.send(normed2, near_bit)
        norm_core = line.send(normed2, core_bit)
        ffs[0].turn()
        ffs[0].wait()
        line.wait(norm_core)
        for k in range(1, last + 1):
            ffs[k] = Gather(line, slices[k])
        cot_rows = [cotangent, cot_core, cot_near, cot_both]
        outs_ff = [shape((seq_len, half_units))] * 4
        wide_ff = [shape((width, half_units))] * 2
        acts, grads, ups, downs = {}, {}, {}, {}

        def ff_own(k):
            act_a, act_b, grad_a, grad_b, up, down = line.kernel(
                "ff_own",
                functools.partial(ff_act_kernel, chips, k),
                outs_ff + wide_ff,
                [place, limits],
                normed2,
                norm_core,
                *cot_rows[:2],
                *ffs[k].pieces(),
            )
            acts[k] = [act_a, act_b]
            grads[k] = [grad_a, grad_b]
            ups[k] = up
            downs[k] = down

        def ff_near(k):
            act_a, act_b, grad_a, grad_b = line.kernel(
                "ff_near",
                functools.partial(ff_act_kernel, 0, k),
                outs_ff,
                [place, limits],
                norm_near,
                *norm_both,
                *cot_rows[2:],
                ups[k],
                downs[k],
            )
            acts[k] += [act_a, act_b]
            grads[k] += [grad_a, grad_b]

        def ff_grads(k):
            lefts = [line.after(normed2), norm_core, norm_near, norm_joined]
            parts = ff_parts(lefts, cot_rows, acts[k], grads[k])
            line.last = [parts[0]]
            return parts

        def rows_back(name, lefts, i, weights, kind, count=1):
            outs = [shape((seq_len // count, width), kind)] * count
            result = line.kernel(
                name,
                functools.partial(rows_back_kernel, len(weights), 0),
                outs,
                [],
                *[v[i] for v in lefts.values()],
                *weights.values(),
            )
            return result[0] if count == 1 else result

        def add_halves(a, low, high):
            middle = a.shape[0] // 2
            return jnp.concatenate([add_low(a[:middle], low), add_low(a[middle:], high)])

        ff_own(0)
        line.wait(norm_near)
        arrived = line.after(norm_near)
        middle = seq_len // 2
        norm_both = [line.send(v, core_bit) for v in (arrived[:middle], arrived[middle:])]
        line.wait(*norm_both)
        ff_near(0)
        norm_joined = line.op(lambda a, c: jnp.concatenate([a, c]), *norm_both)
        for k in range(1, last + 1):
            ffs[k].turn()
        ctx_far = [line.send(c[0], core_bit) for c in contexts]
        parts = ff_grads(0)
        line.wait(*ctx_far)
        scatters = {0: Scatter(line, parts)}
        for k in range(1, last + 1):
            ff_own(k)
            if k == 1:
                scatters[0].turn()
            ff_near(k)
        back_both = rows_back("ff_back", grads, 3, ups, bf16, 2)
        back_both = [line.send(v, core_bit) for v in back_both]
        back_near = rows_back("ff_back", grads, 2, ups, f32)
        held = {0: scatters[0].close()}
        back_near = line.op(add_halves, back_near, *back_both)
        back_near = line.send(back_near, near_bit)
        for k in range(1, last + 1):
            scatters[k] = Scatter(line, ff_grads(k))
        back_beside = rows_back("ff_back", grads, 1, ups, bf16, 2)
        back_beside = [line.send(v, core_bit) for v in back_beside]
        for k in range(1, last + 1):
            scatters[k].turn()
        back_own = rows_back("ff_back", grads, 0, ups, f32)

        grad_hidden1, grad_attn, sums2 = line.kernel(
            "second_back",
            second_back_kernel,
            [shape((seq_len, width), f32), shape((seq_len, width)), shape((8, width), f32)],
            [],
            back_own,
            *back_beside,
            back_near,
            hidden1,
            cotangent,
            gain2,
        )
        keep, send, grad_send = line.kernel(
            "out_back",
            out_back_kernel,
            [shape((seq_len, half))] * 3,
            [place],
            grad_attn,
            out_mine,
            out_got,
        )
        context_got = line.send(send, core_bit)
        grad_got = line.send(grad_send, core_bit)
        fore_both = rows_back("ff_fore", acts, 3, downs, bf16, 2)
        line.wait(context_got, grad_got)
        grad_low, qkv_scatters = [], []

        def attend_back(p):
            low, *parts = line.kernel(
                "attend_back",
                functools.partial(attend_back_kernel, p),
                [shape((2 * seq_len, chunk_cols))] + parts_shapes(chunk_cols),
                [place],
                qkv_low[p],
                logs[p],
                keep,
                context_got,
                normed1,
                cosine,
                sine,
                seg_col,
                seg_row,
                scratch=[pltpu.VMEM((seq_len, HEAD_DIM), f32)] * 3,
            )
            grad_low.append(low)
            return by_chip(parts)

        parts = attend_back(0)
        for k in range(1, last + 1):
            held[k] = scatters[k].close()
        far_got = line.send(held[last], far_bits[0]) if len(far_bits) == 1 else None
        qkv_scatters.append(Scatter(line, parts))
        fore_both = [line.send(v, core_bit) for v in fore_both]
        fore_near = rows_back("ff_fore", acts, 2, downs, f32)
        fore_near = line.op(add_halves, fore_near, *fore_both)
        qkv_scatters[0].turn()
        fore_near = line.send(fore_near, near_bit)
        parts = attend_back(1)
        qkv_scatters.append(Scatter(line, parts))
        out_parts = line.kernel(
            "out_weight",
            functools.partial(out_weight_kernel, chunks),
            parts_shapes(half),
            [place],
            context,
            grad_attn,
            grad_got,
            *[c[1] for c in contexts],
            *ctx_far,
            scratch=[pltpu.VMEM((seq_len, width), bf16)],
        )
        qkv_z = [OverMp(line, qkv_scatters[0].close())]
        qkv_scatters[1].turn()
        parts = attend_back(2)
        line.wait(fore_near)
        if len(far_bits) == 1:
            ff_share = line.op(add_low, held[0], far_got)
        else:
            held = [held[k] for k in range(len(slices))]
            for bit in reversed(far_bits):
                middle = len(held) // 2
                held = [add_low(a, flip(c, bit)) for a, c in zip(held[:middle], held[middle:])]
            ff_share = held[0]
        qkv_scatters.append(Scatter(line, parts))
        qkv_z[0].turn()
        qkv_z.append(OverMp(line, qkv_scatters[1].close()))
        qkv_scatters[2].turn()
        back_other = line.kernel(
            "qkv_back",
            functools.partial(rows_back_kernel, chunks, seq_len),
            [shape((seq_len // 2, width))] * 2,
            [],
            *grad_low,
            *qkv_wide,
        )
        qkv_z[0].back()
        qkv_z[1].turn()
        shares = [qkv_z[0].close()]
        out_scatter = Scatter(line, by_chip(out_parts))
        qkv_z.append(OverMp(line, qkv_scatters[2].close()))
        out_scatter.turn()
        qkv_z[1].back()
        back_mine = line.kernel(
            "qkv_back",
            functools.partial(rows_back_kernel, chunks, 0),
            [shape((seq_len, width), f32)],
            [],
            *grad_low,
            *qkv_wide,
        )[0]
        qkv_z[2].turn()
        shares.append(qkv_z[1].close())
        back_other_got = [line.send(v, core_bit) for v in back_other]
        out_z = OverMp(line, out_scatter.close())
        grad_input, sums1 = line.kernel(
            "first_back",
            first_back_kernel,
            [shape((seq_len, width), f32), shape((8, width), f32)],
            [],
            back_mine,
            *back_other_got,
            block_in,
            grad_hidden1,
            gain1,
        )
        qkv_z[2].back()
        out_z.turn()
        sums = SumAll(line, jnp.concatenate([sums1[:2], sums2[:2]]))
        fore_beside = rows_back("ff_fore", acts, 1, downs, bf16, 2)
        shares.append(qkv_z[2].close())
        out_z.back()
        sums.turn()
        shares_got = [line.send(v, core_bit) for v in shares]
        fore_own = rows_back("ff_fore", acts, 0, downs, f32)
        line.wait(*shares_got)
        sums.turn()
        out_share = out_z.close()
        ff_share_got = line.send(ff_share, core_bit)
        out_share_got = line.send(out_share, core_bit)
        fore_beside = [line.send(v, core_bit) for v in fore_beside]
        grad_w_qkv = line.kernel(
            "place_qkv",
            functools.partial(place_attention_kernel, chunks),
            shape((rows, 3 * width), f32),
            [place],
            *shares,
            *shares_got,
        )
        sums.turn()
        grad_w_up, grad_w_down = line.kernel(
            "place_ff",
            place_halves_kernel,
            [shape((rows, units), f32)] * 2,
            [place],
            ff_share,
            ff_share_got,
        )
        grad_w_down = grad_w_down.T
        sums.turn()
        grad_w_out = line.kernel(
            "place_out",
            place_halves_kernel,
            [shape((rows, width), f32)],
            [place],
            out_share,
            out_share_got,
        )[0]
        sums = sums.close()

        def finish(base, own, near, low, high):
            middle = own.shape[0] // 2
            total_rows = base + own + near.astype(f32)
            return jnp.concatenate(
                [total_rows[:middle] + low.astype(f32), total_rows[middle:] + high.astype(f32)]
            ).astype(bf16)

        block_out = line.op(finish, hidden1, fore_own, fore_near, *fore_beside)
        return (
            block_out,
            grad_input,
            grad_w_qkv,
            grad_w_out,
            grad_w_up,
            grad_w_down,
            sums[0],
            sums[1],
            sums[2],
            sums[3],
        )

    return on_device


def solution(mesh):
    return jax.shard_map(
        build(mesh.shape["dp"], mesh.shape["mp"]),
        mesh=mesh,
        in_specs=(
            P(("dp", "mp"), None),
            P(("dp", "mp"), None),
            P(("dp", "mp"), None),
            P("dp"),
            P("dp", None),
            P("dp", None),
            P("dp", "mp"),
            P("mp", "dp"),
            P(),
            P(),
            P(),
            P(),
        ),
        out_specs=(
            P(("dp", "mp"), None),
            P(("dp", "mp"), None),
            P("dp", None),
            P("dp", None),
            P("dp", "mp"),
            P("mp", "dp"),
            P(),
            P(),
            P(),
            P(),
        ),
        check_vma=False,
    )
```

```python
import functools
import math

import jax
import jax.numpy as jnp
import numpy as np
from jax import lax
from jax.experimental import pallas as pl
from jax.experimental.pallas import tpu as pltpu
from jax.sharding import PartitionSpec as P

HEADS = 12
HEAD_DIM = 128
BLOCK = 768
AXES = ("dp", "mp")
PAIR = 2
LANES = PAIR * HEAD_DIM

epsilon = 1e-05
theta_base = 10000.0
score_scale = HEAD_DIM ** (-0.5)
contract_rows = (((0,), (0,)), ((), ()))
contract_cols = (((1,), (1,)), ((), ()))
f32 = jnp.float32
bf16 = jnp.bfloat16
SMEM_SPEC = pl.BlockSpec(memory_space=pltpu.SMEM)
VMEM_SPEC = pl.BlockSpec(memory_space=pltpu.VMEM)


def rotary_tables(length, head_width):
    halfway = head_width // 2
    frequency = np.float32(theta_base) ** (np.float32(-2.0) * np.arange(halfway, dtype=np.float32) / head_width)
    angles = np.arange(length, dtype=np.float32)[:, None] * frequency.astype(np.float32)[None, :]
    angles = np.concatenate([angles, angles], axis=1).astype(np.float64)
    return jnp.asarray(np.cos(angles), f32), jnp.asarray(np.sin(angles), f32)


def turn(values):
    halfway = values.shape[-1] // 2
    return jnp.concatenate([-values[:, halfway:], values[:, :halfway]], axis=-1)


def turn_back(values):
    halfway = values.shape[-1] // 2
    return jnp.concatenate([values[:, halfway:], -values[:, :halfway]], axis=-1)


def at(start, size):
    return pl.ds(pl.multiple_of(start, size), size)


def lanes(start, size):
    return pl.ds(pl.multiple_of(start, 128), size)


def normal_of(values):
    average = jnp.mean(values, axis=-1, keepdims=True)
    centred = values - average
    variance = jnp.mean(centred * centred, axis=-1, keepdims=True)
    inverse = lax.rsqrt(variance + epsilon)
    return centred * inverse, inverse


def norm_back(grad, normal, inverse, gain):
    scaled = grad * gain
    mean = jnp.mean(scaled, axis=-1, keepdims=True)
    mean_normal = jnp.mean(scaled * normal, axis=-1, keepdims=True)
    return (scaled - mean - normal * mean_normal) * inverse


COST = pl.CostEstimate(flops=1000000, bytes_accessed=0, transcendentals=0)


EXTRA = 6 * 1024 * 1024


def room(value):
    return math.prod(value.shape) * jnp.dtype(value.dtype).itemsize


def run(name, kernel, outs, scalars, *args, scratch=()):
    many = isinstance(outs, (tuple, list))
    held = sum(room(v) for v in args) + sum(room(v) for v in (outs if many else [outs]))
    held += sum(room(v) for v in scratch)
    return pl.pallas_call(
        kernel,
        out_shape=outs,
        in_specs=[SMEM_SPEC] * len(scalars) + [VMEM_SPEC] * len(args),
        out_specs=[VMEM_SPEC] * len(outs) if many else VMEM_SPEC,
        scratch_shapes=list(scratch),
        cost_estimate=COST,
        compiler_params=pltpu.CompilerParams(vmem_limit_bytes=held + EXTRA),
        name=name,
    )(*scalars, *args)


def shape(dims, kind=bf16):
    return jax.ShapeDtypeStruct(tuple(dims), kind)


def cut_attention_kernel(place, own_qkv, got_qkv, *outs):
    core = place[0]
    rows, width = own_qkv.shape
    width = width // 3
    half = width // 2
    mine, theirs = at(core * rows, rows), at((1 - core) * rows, rows)
    for p, out in enumerate(outs):
        for part in range(3):
            cols = lanes(core * half + (part * width + p * LANES), LANES)
            here = slice(part * LANES, (part + 1) * LANES)
            out[mine, here] = own_qkv[:, cols]
            out[theirs, here] = got_qkv[:, cols]


def cut_rest_kernel(place, own_out, own_up, own_down, got, out_piece, out_piece_got, ff_piece):
    core = place[0]
    rows, width = own_out.shape
    half = width // 2
    for out, part in ((out_piece, core), (out_piece_got, 1 - core)):
        cols = lanes(part * half, half)
        out[at(core * rows, rows), :] = own_out[:, cols]
        out[at((1 - core) * rows, rows), :] = got[:rows, cols]
    half = own_up.shape[1] // 2
    cols = lanes(core * half, half)
    units = own_up.shape[1]
    for i, own in enumerate((own_up, own_down)):
        ff_piece[at(core * rows + i * 2 * rows, rows), :] = own[:, cols]
        if units == width:
            ff_piece[at((1 - core) * rows + i * 2 * rows, rows), :] = got[(1 + i) * rows : (2 + i) * rows, cols]
        else:
            cols_got = lanes(core * half + i * units, half)
            ff_piece[at((1 - core) * rows + i * 2 * rows, rows), :] = got[rows:, cols_got]


def join(place, chips, pieces, outs):
    parts = len(outs)
    span = pieces[0].shape[0] // parts
    for j in range(min(chips, len(pieces))):
        for i, out in enumerate(outs):
            rows = at(place[1 + j], span)
            if len(pieces) == chips or j < chips - 1:
                out[rows, :] = pieces[j][i * span : (i + 1) * span, :]
            elif parts == 1:
                half = span // 2
                out[pl.ds(pl.multiple_of(place[1 + j], half), half), :] = pieces[j][...]
                out[pl.ds(pl.multiple_of(place[1 + j] + half, half), half), :] = pieces[j + 1][...]
            else:
                out[rows, :] = pieces[j + i][...]


def join_kernel(chips, many, place, *refs):
    *pieces, mine, got = refs
    join(place, chips, pieces[:many], [mine])
    join(place, chips, pieces[many:], [got])


def norm_kernel(own, other, gain, bias, out):
    seq_len = own.shape[0]
    block = 128

    def step(i, carry):
        rows = at(i * block, block)
        for k, ref in enumerate((own, other)):
            normal, _ = normal_of(ref[rows, :].astype(f32))
            out[at(k * seq_len + i * block, block), :] = (normal * gain[...] + bias[...]).astype(bf16)
        return carry

    lax.fori_loop(0, seq_len // block, step, 0)


def allowed_block(seg_col, seg_row, row_start, block, extent):
    row_place = row_start + lax.broadcasted_iota(jnp.int32, (block, extent), 0)
    col_place = lax.broadcasted_iota(jnp.int32, (block, extent), 1)
    return (row_place >= col_place) & (seg_col == seg_row)


def attend_kernel(chips, seq_len, place, norm_ref, cos_ref, sin_ref, segc_ref, segr_ref, *refs):
    *pieces, wide_ref, qkv_ref, ctx_ref, lse_ref = refs
    join(place, chips, pieces, [wide_ref])
    hd = HEAD_DIM
    block = seq_len // 2

    def project(i, carry):
        rows = at(i * block, block)
        joined = jnp.dot(norm_ref[rows, :], wide_ref[...], preferred_element_type=f32)
        table = at((i % 2) * block, block)
        cosine, sine = cos_ref[table, :], sin_ref[table, :]
        for h in range(2 * PAIR):
            part = joined[:, h * hd : (h + 1) * hd]
            qkv_ref[rows, h * hd : (h + 1) * hd] = (part * cosine + turn(part) * sine).astype(bf16)
        qkv_ref[rows, 2 * PAIR * hd :] = joined[:, 2 * PAIR * hd :].astype(bf16)
        return carry

    lax.fori_loop(0, 4, project, 0)

    lane = lax.broadcasted_iota(jnp.int32, (block, hd), 1)

    def sequence(s, carry):
        base = s * seq_len
        for r in range(2):
            extent = (r + 1) * block
            rows = at(base + r * block, block)
            cols = pl.ds(pl.multiple_of(base, block), extent)
            allowed = allowed_block(
                segc_ref[s, r * block : (r + 1) * block, :],
                segr_ref[s, :, :extent],
                r * block,
                block,
                extent,
            )
            logs = jnp.zeros((block, hd), f32)
            for h in range(PAIR):
                query = qkv_ref[rows, h * hd : (h + 1) * hd]
                key = qkv_ref[cols, (PAIR + h) * hd : (PAIR + h + 1) * hd]
                value = qkv_ref[cols, (2 * PAIR + h) * hd : (2 * PAIR + h + 1) * hd]
                scores = lax.dot_general(query, key, contract_cols, preferred_element_type=f32)
                scores = jnp.where(allowed, scores * score_scale, -1000000000.0)
                top = jnp.max(scores, axis=-1, keepdims=True)
                weight = jnp.exp(scores - top)
                total = jnp.sum(weight, axis=-1, keepdims=True)
                probs = (weight * (1.0 / total)).astype(bf16)
                ctx_ref[s, r * block : (r + 1) * block, h * hd : (h + 1) * hd] = jnp.dot(
                    probs, value, preferred_element_type=f32
                ).astype(bf16)
                logs = jnp.where(lane == h, top + jnp.log(total), logs)
            lse_ref[rows, :] = logs
        return carry

    lax.fori_loop(0, 2, sequence, 0)


def out_kernel(chunks, place, x_ref, *refs):
    mine, got = refs[:chunks], refs[chunks : 2 * chunks]
    w_mine, w_got, gain, bias, hidden, norm, ctx = refs[2 * chunks :]
    core = place[0]
    seq_len, width = x_ref.shape
    half = width // 2
    own_cols, got_cols = lanes(core * half, half), lanes((1 - core) * half, half)
    for p in range(chunks):
        here = lanes(core * half + p * LANES, LANES)
        there = lanes((1 - core) * half + p * LANES, LANES)
        ctx[:, here] = mine[p][...]
        ctx[:, there] = got[p][...]
    block = 128

    def step(i, carry):
        rows = at(i * block, block)
        hidden[rows, own_cols] = jnp.dot(ctx[rows, :], w_mine[...], preferred_element_type=f32)
        hidden[rows, got_cols] = jnp.dot(ctx[rows, :], w_got[...], preferred_element_type=f32)
        values = hidden[rows, :] + x_ref[rows, :].astype(f32)
        hidden[rows, :] = values
        normal, _ = normal_of(values)
        norm[rows, :] = (normal * gain[...] + bias[...]).astype(bf16)
        return carry

    lax.fori_loop(0, seq_len // block, step, 0)


def out_back_kernel(place, grad, w_mine, w_got, keep, send, grad_send):
    core = place[0]
    seq_len, width = grad.shape
    half = width // 2
    own_cols, got_cols = lanes(core * half, half), lanes((1 - core) * half, half)
    grad_send[...] = grad[:, got_cols]
    for out, part in ((send, 1 - core), (keep, core)):
        rows = at(part * half, half)

        def step(i, carry):
            here = at(i * 256, 256)
            out[here, :] = (
                lax.dot_general(grad[here, own_cols], w_mine[rows, :], contract_cols, preferred_element_type=f32)
                + lax.dot_general(grad[here, got_cols], w_got[rows, :], contract_cols, preferred_element_type=f32)
            ).astype(bf16)
            return carry

        lax.fori_loop(0, seq_len // 256, step, 0)


def spread(place, outs, product):
    if len(outs) > 1:
        span = outs[0].shape[0]
        for j, out in enumerate(outs[:3]):
            out[...] = product(lanes(place[1 + j], span)).astype(bf16)
        corner = product(lanes(place[4], span)).astype(bf16)
        outs[3][...] = corner[: span // 2, :]
        outs[4][...] = corner[span // 2 :, :]
    else:
        for start in range(0, outs[0].shape[0], 256):
            here = slice(start, start + 256)
            outs[0][here, :] = product(here).astype(bf16)


def out_weight_kernel(chunks, place, ctx, grad, grad_got, *refs):
    mine, got, outs, other = refs[:chunks], refs[chunks : 2 * chunks], refs[2 * chunks : -1], refs[-1]
    core = place[0]
    seq_len, width = grad.shape
    half = width // 2
    cols = lanes(core * half, half)
    for p in range(chunks):
        other[:, lanes(core * half + p * LANES, LANES)] = mine[p][...]
        other[:, lanes((1 - core) * half + p * LANES, LANES)] = got[p][...]

    def product(here):
        return lax.dot_general(
            ctx[:, here], grad[:, cols], contract_rows, preferred_element_type=f32
        ) + lax.dot_general(other[:, here], grad_got[...], contract_rows, preferred_element_type=f32)

    spread(place, outs, product)


def attend_back_kernel(
    chunk, place, qkv_ref, lse_ref, keep, got, norm, cos_ref, sin_ref, segc_ref, segr_ref, out_ref, *refs
):
    *pieces, gq, gk, gv = refs
    hd = HEAD_DIM
    seq_len = keep.shape[0]
    block = seq_len // 2
    for s, grad_ref in enumerate((keep, got)):
        base = s * seq_len
        for h in range(PAIR):
            lane = slice(chunk * LANES + h * hd, chunk * LANES + (h + 1) * hd)
            for r in (1, 0):
                extent = (r + 1) * block
                rows = slice(base + r * block, base + (r + 1) * block)
                cols = slice(base, base + extent)
                allowed = allowed_block(
                    segc_ref[s, r * block : (r + 1) * block, :],
                    segr_ref[s, :, :extent],
                    r * block,
                    block,
                    extent,
                )
                query = qkv_ref[rows, h * hd : (h + 1) * hd]
                key = qkv_ref[cols, (PAIR + h) * hd : (PAIR + h + 1) * hd]
                value = qkv_ref[cols, (2 * PAIR + h) * hd : (2 * PAIR + h + 1) * hd]
                grad = grad_ref[r * block : (r + 1) * block, lane]
                scores = lax.dot_general(query, key, contract_cols, preferred_element_type=f32)
                scores = jnp.where(allowed, scores * score_scale, -1000000000.0)
                probs = jnp.exp(scores - lse_ref[rows, h : h + 1])
                grad_probs = lax.dot_general(grad, value, contract_cols, preferred_element_type=f32)
                weighted = jnp.sum(probs * grad_probs, axis=-1, keepdims=True)
                grad_scores = (probs * (grad_probs - weighted) * score_scale).astype(bf16)
                probs = probs.astype(bf16)
                gq[r * block : (r + 1) * block, :] = jnp.dot(grad_scores, key, preferred_element_type=f32)
                grad_key = lax.dot_general(grad_scores, query, contract_rows, preferred_element_type=f32)
                grad_value = lax.dot_general(probs, grad, contract_rows, preferred_element_type=f32)
                if r == 1:
                    gk[...] = grad_key
                    gv[...] = grad_value
                else:
                    gk[:block, :] = gk[:block, :] + grad_key
                    gv[:block, :] = gv[:block, :] + grad_value
            sine, cosine = sin_ref[...], cos_ref[...]
            rows = slice(base, base + seq_len)
            grad_query, grad_key = gq[...], gk[...]
            out_ref[rows, h * hd : (h + 1) * hd] = (
                grad_query * cosine + turn_back(grad_query * sine)
            ).astype(bf16)
            out_ref[rows, (PAIR + h) * hd : (PAIR + h + 1) * hd] = (
                grad_key * cosine + turn_back(grad_key * sine)
            ).astype(bf16)
            out_ref[rows, (2 * PAIR + h) * hd : (2 * PAIR + h + 1) * hd] = gv[...].astype(bf16)

    def product(here):
        return lax.dot_general(norm[:, here], out_ref[...], contract_rows, preferred_element_type=f32)

    spread(place, pieces, product)


def ff_act_kernel(chips, index, place, limits, *refs):
    if chips:
        norm_a, norm_b, cot_a, cot_b, *pieces, act_a, act_b, grad_a, grad_b, up, down = refs
        join(place, chips, pieces, [up, down])
        norms = ([norm_a], [norm_b])
        first = 0
    else:
        norm_a, norm_low, norm_high, cot_a, cot_b, up, down, act_a, act_b, grad_a, grad_b = refs
        norms = ([norm_a], [norm_low, norm_high])
        first = 2
    sides = zip(norms, (cot_a, cot_b), (act_a, act_b), (grad_a, grad_b))
    units = up.shape[1]
    block, tile = 256, 256 if units % 256 == 0 else 128
    for s, (norm_parts, cot, act, grad) in enumerate(sides):
        limit = limits[index, first + s]
        for k, norm in enumerate(norm_parts):
            length = norm.shape[0]

            def step(i, carry):
                here = at(i * block, block)
                rows = at(k * length + i * block, block)
                for n in range(0, units, tile):
                    cols = slice(n, n + tile)
                    preact = jnp.dot(norm[here, :], up[:, cols], preferred_element_type=f32)
                    grad_active = jnp.dot(cot[rows, :], down[:, cols], preferred_element_type=f32)
                    mask = n + lax.broadcasted_iota(jnp.int32, (block, tile), 1) < limit
                    cdf = 0.5 * (1.0 + lax.erf(preact * 0.7071067811865476))
                    slope = cdf + preact * jnp.exp(-0.5 * preact * preact) * 0.3989422804014327
                    act[rows, cols] = jnp.where(mask, preact * cdf, 0.0).astype(bf16)
                    grad[rows, cols] = jnp.where(mask, grad_active * slope, 0.0).astype(bf16)
                return carry

            lax.fori_loop(0, length // block, step, 0)


def rows_back_kernel(count, base, *refs):
    grads, weights, outs = refs[:count], refs[count : 2 * count], refs[2 * count :]
    total = outs[0].shape[0]
    for k, out in enumerate(outs):

        def step(i, carry):
            rows = at(base + k * total + i * 256, 256)
            acc = 0.0
            for g, w in zip(grads, weights):
                acc = acc + lax.dot_general(g[rows, :], w[...], contract_cols, preferred_element_type=f32)
            out[at(i * 256, 256), :] = acc.astype(out.dtype)
            return carry

        lax.fori_loop(0, total // 256, step, 0)


def ff_weight_kernel(count, place, *refs):
    norms, cots = refs[:count], refs[count : 2 * count]
    acts, grads, outs = refs[2 * count : 3 * count], refs[3 * count : 4 * count], refs[4 * count :]
    span = norms[0].shape[1]
    corner = len(outs) == 5
    for j in range(4 if corner else len(outs)):

        @pl.when(pl.program_id(0) == j)
        def _():
            for i, (lefts, rights) in enumerate(((norms, grads), (cots, acts))):
                acc = 0.0
                for left, right in zip(lefts, rights):
                    acc = acc + lax.dot_general(
                        left[...], right[...], contract_rows, preferred_element_type=f32
                    )
                if corner and j == 3:
                    outs[3 + i][...] = acc.astype(bf16)
                else:
                    outs[j][i * span : (i + 1) * span, :] = acc.astype(bf16)


def ff_weight(order, chips, norms, cots, acts, grads):
    seq_len, width = norms[0].shape
    units = acts[0].shape[1]
    span = width // chips
    count = len(norms)
    outs = [(2 * span, units)] * chips
    if chips == 4:
        outs = [(2 * span, units)] * 3 + [(span, units)] * 2
    wide = pl.BlockSpec((seq_len, span), lambda j, order: (0, order[j]))
    whole = pl.BlockSpec((seq_len, units), lambda j, order: (0, 0))
    return pl.pallas_call(
        functools.partial(ff_weight_kernel, count),
        out_shape=[shape(v) for v in outs],
        grid_spec=pltpu.PrefetchScalarGridSpec(
            num_scalar_prefetch=1,
            grid=(chips,),
            in_specs=[wide] * (2 * count) + [whole] * (2 * count),
            out_specs=[pl.BlockSpec(v, lambda j, order: (0, 0)) for v in outs],
        ),
        cost_estimate=COST,
        compiler_params=pltpu.CompilerParams(vmem_limit_bytes=40 * 1024 * 1024),
        name="ff_weight",
    )(order, *norms, *cots, *acts, *grads)


def second_back_kernel(own, beside_a, beside_b, near, hidden, cot, gain, grad_hidden, grad_low, sums):
    seq_len, width = own.shape
    block = 64
    sums[...] = jnp.zeros_like(sums)

    def step(i, carry, first, beside):
        rows = at(first + i * block, block)
        grad = own[rows, :] + beside[at(i * block, block), :].astype(f32) + near[rows, :].astype(f32)
        normal, inverse = normal_of(hidden[rows, :])
        sums[0:1, :] += jnp.sum(grad * normal, axis=0, keepdims=True)
        sums[1:2, :] += jnp.sum(grad, axis=0, keepdims=True)
        back = cot[rows, :].astype(f32) + norm_back(grad, normal, inverse, gain[...])
        grad_hidden[rows, :] = back
        grad_low[rows, :] = back.astype(bf16)
        return carry

    for k, ref in enumerate((beside_a, beside_b)):
        part = functools.partial(step, first=k * seq_len // 2, beside=ref)
        lax.fori_loop(0, seq_len // 2 // block, part, 0)


def first_back_kernel(own, beside, x_ref, grad_hidden, gain, out, sums):
    seq_len, width = own.shape
    block = 64
    sums[...] = jnp.zeros_like(sums)

    def step(i, carry):
        rows = at(i * block, block)
        grad = own[rows, :] + beside[rows, :].astype(f32)
        normal, inverse = normal_of(x_ref[rows, :].astype(f32))
        sums[0:1, :] += jnp.sum(grad * normal, axis=0, keepdims=True)
        sums[1:2, :] += jnp.sum(grad, axis=0, keepdims=True)
        out[rows, :] = grad_hidden[rows, :] + norm_back(grad, normal, inverse, gain[...])
        return carry

    lax.fori_loop(0, seq_len // block, step, 0)


def place_attention_kernel(count, place, *refs):
    mine, got, out = refs[:count], refs[count : 2 * count], refs[2 * count]
    core = place[0]
    rows = out.shape[0]
    width = out.shape[1] // 3
    half = width // 2
    here = at(core * rows, rows)
    for p in range(count):
        for part in range(3):
            cols = slice(part * LANES, (part + 1) * LANES)
            base = part * width + p * LANES
            out[:, lanes(core * half + base, LANES)] = mine[p][here, cols].astype(f32)
            out[:, lanes((1 - core) * half + base, LANES)] = got[p][here, cols].astype(f32)


def place_halves_kernel(place, *refs):
    mine, got, outs = refs[0], refs[1], refs[2:]
    core = place[0]
    rows = outs[0].shape[0]
    half = outs[0].shape[1] // 2
    for i, out in enumerate(outs):
        here = at(core * rows + i * 2 * rows, rows)
        out[:, lanes(core * half, half)] = mine[here, :].astype(f32)
        out[:, lanes((1 - core) * half, half)] = got[here, :].astype(f32)


def tie(value, *others):
    return lax.optimization_barrier((value, *others))[0]


def build(dp_size, mp_size):
    total = dp_size * mp_size
    chip_bits = []
    bit = 2 * mp_size
    while bit < total:
        chip_bits.append(bit)
        bit *= 2
    core_bit = mp_size
    near_bit = 1
    far_bits = []
    bit = 2
    while bit < mp_size:
        far_bits.append(bit)
        bit *= 2
    chips = dp_size // 2

    def flip(value, bit):
        return lax.ppermute(value, AXES, [(i, i ^ bit) for i in range(total)])

    def add(a, b):
        return a.astype(f32) + b.astype(f32)

    def add_low(a, b):
        return add(a, b).astype(bf16)

    class Line:
        def __init__(self):
            self.last = []
            self.open = {}

        def end(self, *values):
            for v in values:
                self.open.pop(id(v), None)

        def after(self, value, *waits):
            self.end(value, *waits)
            waits = list(waits) + self.last
            return tie(value, *waits) if waits else value

        def wait(self, *transfers):
            self.end(*transfers)
            self.last = self.last + list(transfers)

        def send(self, value, bit):
            result = flip(self.after(value), bit)
            self.open[id(result)] = (result, bit)
            return result

        def kernel(self, name, kernel, outs, scalars, *args, wait=(), scratch=()):
            self.end(*args)
            args = (self.after(args[0], *wait),) + args[1:]
            result = run(name, kernel, outs, scalars, *args, scratch=scratch)
            self.last = [result[0] if isinstance(result, (tuple, list)) else result]
            return result

        def op(self, function, *args):
            self.end(*args)
            result = function(self.after(args[0]), *args[1:])
            self.last = [result[0] if isinstance(result, (tuple, list)) else result]
            return result

    two = len(chip_bits) == 2

    class Gather:
        def __init__(self, line, piece):
            self.line, self.piece = line, piece
            if two:
                self.x = line.send(piece, chip_bits[0])
                self.y = line.send(piece, chip_bits[1])
            else:
                held = [line.after(piece)]
                for bit in chip_bits:
                    held = held + [flip(value, bit) for value in held]
                self.all = held

        def turn(self):
            if two:
                half = self.piece.shape[0] // 2
                self.line.wait(self.x, self.y)
                low = self.line.op(lambda v: v[:half], self.x)
                self.low = self.line.send(low, chip_bits[1])
                high = self.line.op(lambda v: v[half:], self.y)
                self.high = self.line.send(high, chip_bits[0])

        def wait(self):
            if two:
                self.line.wait(self.low, self.high)

        def send_first(self, bit):
            if two:
                return [self.line.send(v, bit) for v in (self.x, self.y)]
            return [flip(v, bit) for v in self.all[1:]]

        def send_last(self, bit):
            if two:
                corner = self.line.op(lambda a, b: jnp.concatenate([a, b]), self.low, self.high)
                return [self.line.send(corner, bit)]
            return []

        def pieces(self):
            return [self.piece, self.x, self.y, self.low, self.high] if two else self.all

    class Scatter:
        def __init__(self, line, parts):
            self.line, self.parts = line, parts
            if two:
                self.low = line.send(parts[3], chip_bits[0])
                self.high = line.send(parts[4], chip_bits[1])

        def turn(self):
            if two:
                _, to_x, to_y, low, high = self.parts
                half = low.shape[0]
                self.line.wait(self.low, self.high)
                to_y = self.line.op(lambda v, g: v.at[:half].set(add_low(v[:half], g)), to_y, self.low)
                self.y = self.line.send(to_y, chip_bits[1])
                to_x = self.line.op(lambda v, g: v.at[half:].set(add_low(v[half:], g)), to_x, self.high)
                self.x = self.line.send(to_x, chip_bits[0])

        def close(self):
            if two:
                return self.line.op(
                    lambda own, a, b: (add(own, a) + b.astype(f32)).astype(bf16),
                    self.parts[0],
                    self.x,
                    self.y,
                )
            held = list(self.parts)
            for bit in reversed(chip_bits):
                middle = len(held) // 2
                held = [add_low(a, flip(b, bit)) for a, b in zip(held[:middle], held[middle:])]
            return held[0]

    class OverMp:
        def __init__(self, line, share):
            self.line = line
            size = share.shape[0] // 2
            self.upper = lax.axis_index("mp") % 2
            send = line.op(lambda v: lax.dynamic_slice_in_dim(v, (1 - self.upper) * size, size, axis=0), share)
            self.keep = lax.dynamic_slice_in_dim(share, self.upper * size, size, axis=0)
            self.got = line.send(send, near_bit)

        def turn(self):
            value = self.line.op(add_low, self.keep, self.got)
            for bit in far_bits[:-1]:
                value = add_low(value, flip(value, bit))
            self.keep = value
            self.got = self.line.send(value, far_bits[-1])

        def back(self):
            self.keep = self.line.op(add_low, self.keep, self.got)
            self.got = self.line.send(self.keep, near_bit)

        def close(self):
            def joined(keep, got):
                low = jnp.where(self.upper == 0, keep, got)
                return jnp.concatenate([low, jnp.where(self.upper == 0, got, keep)])

            return self.line.op(joined, self.keep, self.got)

    class SumAll:
        def __init__(self, line, value):
            self.line, self.value, self.bit = line, value, 1
            self.got = line.send(value, 1)

        def turn(self):
            if self.bit < total:
                self.value = self.line.op(jnp.add, self.value, self.got)
                self.bit *= 2
                if self.bit < total:
                    self.got = self.line.send(self.value, self.bit)

        def close(self):
            while self.bit < total:
                self.turn()
            return self.value

    def on_device(
        block_in,
        cotangent,
        segment_ids,
        granularity,
        w_qkv,
        w_out,
        w_up,
        w_down,
        norm1_gain,
        norm1_bias,
        norm2_gain,
        norm2_bias,
    ):
        seq_len, width = block_in.shape
        rows = width // dp_size
        units = w_up.shape[1]
        half_units = units // 2
        half = width // 2
        dp = lax.axis_index("dp")
        mp = lax.axis_index("mp")
        core = dp % 2
        chip = dp // 2
        span = 2 * rows
        order = jnp.stack([chip ^ j for j in range(chips)]).astype(jnp.int32)
        place = jnp.concatenate([core[None].astype(jnp.int32), order * span])
        chunks = HEADS // 2 // PAIR
        chunk_cols = 3 * LANES
        gain1, bias1 = norm1_gain[None], norm1_bias[None]
        gain2, bias2 = norm2_gain[None], norm2_bias[None]
        line = Line()

        def parts_shapes(cols):
            if span % 128 == 0 and chips == 4:
                return [shape((span, cols))] * 3 + [shape((rows, cols))] * 2
            return [shape((width, cols))]

        def by_chip(parts):
            if len(parts) > 1:
                return parts
            return [lax.dynamic_slice_in_dim(parts[0], place[1 + j], span, axis=0) for j in range(chips)]

        def ff_parts(*groups):
            if span % 128 == 0 and chips == 4:
                return ff_weight(order, chips, *groups)
            blocks = width // 256
            parts = ff_weight(jnp.arange(blocks, dtype=jnp.int32), blocks, *groups)
            sides = [
                by_chip([jnp.concatenate([v[i * 256 : (i + 1) * 256] for v in parts])]) for i in range(2)
            ]
            return [jnp.concatenate(v) for v in zip(*sides)]

        w_down_t = w_down.T
        qkv_other = line.send(w_qkv, core_bit)
        small = jnp.concatenate([segment_ids, jnp.broadcast_to(granularity[:, None], (mp_size, seq_len))])
        small_other = line.send(small, core_bit)
        x_other = line.send(block_in, core_bit)
        if units == width:
            rest = jnp.concatenate([w_out, w_up, w_down_t])
        else:
            rest = jnp.concatenate([w_out, jnp.concatenate([w_up, w_down_t], axis=1)])
        rest_other = line.send(rest, core_bit)

        qkv_pieces = line.kernel(
            "cut_attention",
            cut_attention_kernel,
            [shape((span, chunk_cols))] * chunks,
            [place],
            w_qkv,
            qkv_other,
            wait=(small_other,),
        )
        heads = [Gather(line, qkv_pieces[0])]
        cot_near = line.send(cotangent, near_bit)
        normed1 = line.kernel(
            "norm",
            norm_kernel,
            shape((2 * seq_len, width)),
            [],
            block_in,
            x_other,
            gain1,
            bias1,
        )
        out_piece, out_piece_got, ff_piece = line.kernel(
            "cut_rest",
            cut_rest_kernel,
            [shape((span, half))] * 2 + [shape((2 * span, half_units))],
            [place],
            w_out,
            w_up,
            w_down_t,
            rest_other,
        )
        heads.append(Gather(line, qkv_pieces[1]))
        cosine, sine = rotary_tables(seq_len, HEAD_DIM)
        last = mp_size // 2 - 1

        qkv_wide, qkv_low, contexts, logs = [], [], [], []

        def attend(p):
            a, b, c, d = line.kernel(
                "attend",
                functools.partial(attend_kernel, chips, seq_len),
                [
                    shape((width, chunk_cols)),
                    shape((2 * seq_len, chunk_cols)),
                    shape((2, seq_len, LANES)),
                    shape((2 * seq_len, HEAD_DIM), f32),
                ],
                [place],
                normed1,
                cosine,
                sine,
                seg_col,
                seg_row,
                *heads[p].pieces(),
            )
            qkv_wide.append(a)
            qkv_low.append(b)
            contexts.append(c)
            logs.append(d)

        heads[0].turn()

        def from_small(own, other):
            segments = jnp.stack([own[0], other[0]])
            levels = jnp.stack([own[1:, 0], other[1:, 0]])
            ends = BLOCK * jnp.power(2, levels)
            ends = jnp.stack([ends[0, mp], ends[1, mp], ends[0, mp ^ 1], ends[1, mp ^ 1]])
            starts = [(mp ^ (2 * k)) * units + core * half_units for k in range(mp_size // 2)]
            limits = (ends[None, :] - jnp.stack(starts)[:, None]).astype(jnp.int32)
            return limits, segments[:, :, None], segments[:, None, :]

        limits, seg_col, seg_row = line.op(from_small, small, small_other)
        heads[1].turn()
        heads[0].wait()
        line.wait(cot_near)
        slices = [ff_piece]
        for bit in far_bits:
            slices = slices + [line.send(v, bit) for v in slices]
        heads.append(Gather(line, qkv_pieces[2]))
        attend(0)
        heads[1].wait()
        heads[2].turn()
        outs = Gather(line, out_piece)
        attend(1)
        heads[2].wait()
        ctx_near = [line.send(c[1], core_bit) for c in contexts]
        outs.turn()
        line.wait(*ctx_near)
        outs_other = [out_piece_got] + outs.send_first(core_bit)
        attend(2)
        outs.wait()
        line.wait(*outs_other[1:], *slices[1:])
        ffs = {0: Gather(line, slices[0])}
        ctx_near.append(line.send(contexts[2][1], core_bit))
        outs_other += outs.send_last(core_bit)
        out_mine, out_got = line.kernel(
            "join",
            functools.partial(join_kernel, chips, len(outs.pieces())),
            [shape((width, half))] * 2,
            [place],
            *outs.pieces(),
            *outs_other,
            wait=(ctx_near[2],),
        )
        cot_both = line.send(cot_near, core_bit)
        cot_core = line.send(cotangent, core_bit)
        hidden1, normed2, context = line.kernel(
            "out",
            functools.partial(out_kernel, chunks),
            [shape((seq_len, width), f32), shape((seq_len, width)), shape((seq_len, width))],
            [place],
            block_in,
            *[c[0] for c in contexts],
            *ctx_near,
            out_mine,
            out_got,
            gain2,
            bias2,
        )

        line.wait(cot_both, cot_core)
        norm_near = line.send(normed2, near_bit)
        norm_core = line.send(normed2, core_bit)
        ffs[0].turn()
        ffs[0].wait()
        line.wait(norm_core)
        for k in range(1, last + 1):
            ffs[k] = Gather(line, slices[k])
        cot_rows = [cotangent, cot_core, cot_near, cot_both]
        outs_ff = [shape((seq_len, half_units))] * 4
        wide_ff = [shape((width, half_units))] * 2
        acts, grads, ups, downs = {}, {}, {}, {}

        def ff_own(k):
            act_a, act_b, grad_a, grad_b, up, down = line.kernel(
                "ff_own",
                functools.partial(ff_act_kernel, chips, k),
                outs_ff + wide_ff,
                [place, limits],
                normed2,
                norm_core,
                *cot_rows[:2],
                *ffs[k].pieces(),
            )
            acts[k] = [act_a, act_b]
            grads[k] = [grad_a, grad_b]
            ups[k] = up
            downs[k] = down

        def ff_near(k):
            act_a, act_b, grad_a, grad_b = line.kernel(
                "ff_near",
                functools.partial(ff_act_kernel, 0, k),
                outs_ff,
                [place, limits],
                norm_near,
                *norm_both,
                *cot_rows[2:],
                ups[k],
                downs[k],
            )
            acts[k] += [act_a, act_b]
            grads[k] += [grad_a, grad_b]

        def ff_grads(k):
            lefts = [line.after(normed2), norm_core, norm_near, norm_joined]
            parts = ff_parts(lefts, cot_rows, acts[k], grads[k])
            line.last = [parts[0]]
            return parts

        def rows_back(name, lefts, i, weights, kind, count=1):
            outs = [shape((seq_len // count, width), kind)] * count
            result = line.kernel(
                name,
                functools.partial(rows_back_kernel, len(weights), 0),
                outs,
                [],
                *[v[i] for v in lefts.values()],
                *weights.values(),
            )
            return result[0] if count == 1 else result

        def add_halves(a, low, high):
            middle = a.shape[0] // 2
            return jnp.concatenate([add_low(a[:middle], low), add_low(a[middle:], high)])

        ff_own(0)
        line.wait(norm_near)
        arrived = line.after(norm_near)
        middle = seq_len // 2
        norm_both = [line.send(v, core_bit) for v in (arrived[:middle], arrived[middle:])]
        line.wait(*norm_both)
        ff_near(0)
        norm_joined = line.op(lambda a, c: jnp.concatenate([a, c]), *norm_both)
        parts = ff_grads(0)
        for k in range(1, last + 1):
            ffs[k].turn()
        scatters = {0: Scatter(line, parts)}
        ctx_far = []
        for k in range(1, last + 1):
            if k == 1:
                ffs[1].wait()
                ctx_far = [line.send(c[0], core_bit) for c in contexts]
            ff_own(k)
            line.wait(*ctx_far)
            if k == 1:
                scatters[0].turn()
            ff_near(k)
        back_both = rows_back("ff_back", grads, 3, ups, bf16, 2)
        back_both = [line.send(v, core_bit) for v in back_both]
        back_near = rows_back("ff_back", grads, 2, ups, f32)
        fore_both = rows_back("ff_fore", acts, 3, downs, bf16, 2)
        fore_near = rows_back("ff_fore", acts, 2, downs, f32)
        held = {0: scatters[0].close()}
        back_near = line.op(add_halves, back_near, *back_both)
        back_near = line.send(back_near, near_bit)
        for k in range(1, last + 1):
            scatters[k] = Scatter(line, ff_grads(k))
        back_beside = rows_back("ff_back", grads, 1, ups, bf16, 2)
        back_beside = [line.send(v, core_bit) for v in back_beside]
        for k in range(1, last + 1):
            scatters[k].turn()
        back_own = rows_back("ff_back", grads, 0, ups, f32)

        grad_hidden1, grad_attn, sums2 = line.kernel(
            "second_back",
            second_back_kernel,
            [shape((seq_len, width), f32), shape((seq_len, width)), shape((8, width), f32)],
            [],
            back_own,
            *back_beside,
            back_near,
            hidden1,
            cotangent,
            gain2,
        )
        fore_both = [line.send(v, core_bit) for v in fore_both]
        keep, send, grad_send = line.kernel(
            "out_back",
            out_back_kernel,
            [shape((seq_len, half))] * 3,
            [place],
            grad_attn,
            out_mine,
            out_got,
        )
        context_got = line.send(send, core_bit)
        line.wait(context_got, *fore_both)
        fore_near = line.op(add_halves, fore_near, *fore_both)
        fore_near = line.send(fore_near, near_bit)
        grad_got = line.send(grad_send, core_bit)
        grad_low, qkv_scatters = [], []

        def attend_back(p):
            low, *parts = line.kernel(
                "attend_back",
                functools.partial(attend_back_kernel, p),
                [shape((2 * seq_len, chunk_cols))] + parts_shapes(chunk_cols),
                [place],
                qkv_low[p],
                logs[p],
                keep,
                context_got,
                normed1,
                cosine,
                sine,
                seg_col,
                seg_row,
                scratch=[pltpu.VMEM((seq_len, HEAD_DIM), f32)] * 3,
            )
            grad_low.append(low)
            return by_chip(parts)

        parts = attend_back(0)
        line.wait(grad_got)
        qkv_scatters.append(Scatter(line, parts))
        out_parts = line.kernel(
            "out_weight",
            functools.partial(out_weight_kernel, chunks),
            parts_shapes(half),
            [place],
            context,
            grad_attn,
            grad_got,
            *[c[1] for c in contexts],
            *ctx_far,
            scratch=[pltpu.VMEM((seq_len, width), bf16)],
        )
        for k in range(1, last + 1):
            held[k] = scatters[k].close()
        far_got = line.send(held[last], far_bits[0]) if len(far_bits) == 1 else None
        qkv_scatters[0].turn()
        parts = attend_back(1)
        line.wait(fore_near)
        qkv_scatters.append(Scatter(line, parts))
        first, second = qkv_scatters
        first_z = OverMp(line, first.close())
        second.turn()
        parts = attend_back(2)
        if len(far_bits) == 1:
            line.wait(far_got)
        second_share = second.close()
        third = Scatter(line, parts)
        back_other = line.kernel(
            "qkv_back",
            functools.partial(rows_back_kernel, chunks, seq_len),
            [shape((seq_len, width))],
            [],
            *grad_low,
            *qkv_wide,
        )[0]
        back_mine = line.kernel(
            "qkv_back",
            functools.partial(rows_back_kernel, chunks, 0),
            [shape((seq_len, width), f32)],
            [],
            *grad_low,
            *qkv_wide,
        )[0]
        first_z.turn()
        second_z = OverMp(line, second_share)
        third.turn()
        back_other = line.send(back_other, core_bit)
        grad_input, sums1 = line.kernel(
            "first_back",
            first_back_kernel,
            [shape((seq_len, width), f32), shape((8, width), f32)],
            [],
            back_mine,
            back_other,
            block_in,
            grad_hidden1,
            gain1,
        )
        second_z.turn()
        third_share = third.close()
        fourth = Scatter(line, by_chip(out_parts))
        third_z = OverMp(line, third_share)
        first_z.back()
        fourth.turn()
        third_z.turn()
        first_share = first_z.close()
        fourth_z = OverMp(line, fourth.close())
        second_z.back()
        sums = SumAll(line, jnp.concatenate([sums1[:2], sums2[:2]]))
        fore_beside = rows_back("ff_fore", acts, 1, downs, bf16)
        fourth_z.turn()
        third_z.back()
        sums.turn()
        second_share = second_z.close()
        fore_own = rows_back("ff_fore", acts, 0, downs, f32)
        sums.turn()
        third_share = third_z.close()
        if len(far_bits) == 1:
            ff_share = line.op(add_low, held[0], far_got)
        else:
            held = [held[k] for k in range(len(slices))]
            for bit in reversed(far_bits):
                middle = len(held) // 2
                held = [add_low(a, flip(c, bit)) for a, c in zip(held[:middle], held[middle:])]
            ff_share = held[0]
        sums.turn()
        fourth_z.back()
        first_got = line.send(first_share, core_bit)
        second_got = line.send(second_share, core_bit)
        third_got = line.send(third_share, core_bit)
        grad_w_qkv = line.kernel(
            "place_qkv",
            functools.partial(place_attention_kernel, chunks),
            shape((rows, 3 * width), f32),
            [place],
            first_share,
            second_share,
            third_share,
            first_got,
            second_got,
            third_got,
        )
        fore_beside = line.send(fore_beside, core_bit)
        ff_share_got = line.send(ff_share, core_bit)
        sums.turn()

        def finish(base, own, near, beside):
            return (base + own + near.astype(f32) + beside.astype(f32)).astype(bf16)

        block_out = line.op(finish, hidden1, fore_own, fore_near, fore_beside)
        grad_w_up, grad_w_down = line.kernel(
            "place_ff",
            place_halves_kernel,
            [shape((rows, units), f32)] * 2,
            [place],
            ff_share,
            ff_share_got,
        )
        grad_w_down = grad_w_down.T
        sums = sums.close()
        out_share = fourth_z.close()
        out_share_got = line.send(out_share, core_bit)
        grad_w_out = line.kernel(
            "place_out",
            place_halves_kernel,
            [shape((rows, width), f32)],
            [place],
            out_share,
            out_share_got,
        )[0]
        return (
            block_out,
            grad_input,
            grad_w_qkv,
            grad_w_out,
            grad_w_up,
            grad_w_down,
            sums[0],
            sums[1],
            sums[2],
            sums[3],
        )

    return on_device


def solution(mesh):
    return jax.shard_map(
        build(mesh.shape["dp"], mesh.shape["mp"]),
        mesh=mesh,
        in_specs=(
            P(("dp", "mp"), None),
            P(("dp", "mp"), None),
            P(("dp", "mp"), None),
            P("dp"),
            P("dp", None),
            P("dp", None),
            P("dp", "mp"),
            P("mp", "dp"),
            P(),
            P(),
            P(),
            P(),
        ),
        out_specs=(
            P(("dp", "mp"), None),
            P(("dp", "mp"), None),
            P("dp", None),
            P("dp", None),
            P("dp", "mp"),
            P("mp", "dp"),
            P(),
            P(),
            P(),
            P(),
        ),
        check_vma=False,
    )
```

```python
import functools
import math

import jax
import jax.numpy as jnp
import numpy as np
from jax import lax
from jax.experimental import pallas as pl
from jax.experimental.pallas import tpu as pltpu
from jax.sharding import PartitionSpec as P

HEADS = 12
HEAD_DIM = 128
BLOCK = 768
AXES = ("dp", "mp")
PAIR = 2
LANES = PAIR * HEAD_DIM

epsilon = 1e-05
theta_base = 10000.0
score_scale = HEAD_DIM ** (-0.5)
contract_rows = (((0,), (0,)), ((), ()))
contract_cols = (((1,), (1,)), ((), ()))
f32 = jnp.float32
bf16 = jnp.bfloat16
SMEM_SPEC = pl.BlockSpec(memory_space=pltpu.SMEM)
VMEM_SPEC = pl.BlockSpec(memory_space=pltpu.VMEM)


def rotary_tables(length, head_width):
    halfway = head_width // 2
    frequency = np.float32(theta_base) ** (np.float32(-2.0) * np.arange(halfway, dtype=np.float32) / head_width)
    angles = np.arange(length, dtype=np.float32)[:, None] * frequency.astype(np.float32)[None, :]
    angles = np.concatenate([angles, angles], axis=1).astype(np.float64)
    return jnp.asarray(np.cos(angles), f32), jnp.asarray(np.sin(angles), f32)


def turn(values):
    halfway = values.shape[-1] // 2
    return jnp.concatenate([-values[:, halfway:], values[:, :halfway]], axis=-1)


def turn_back(values):
    halfway = values.shape[-1] // 2
    return jnp.concatenate([values[:, halfway:], -values[:, :halfway]], axis=-1)


def at(start, size):
    return pl.ds(pl.multiple_of(start, size), size)


def lanes(start, size):
    return pl.ds(pl.multiple_of(start, 128), size)


def normal_of(values):
    average = jnp.mean(values, axis=-1, keepdims=True)
    centred = values - average
    variance = jnp.mean(centred * centred, axis=-1, keepdims=True)
    inverse = lax.rsqrt(variance + epsilon)
    return centred * inverse, inverse


def norm_back(grad, normal, inverse, gain):
    scaled = grad * gain
    mean = jnp.mean(scaled, axis=-1, keepdims=True)
    mean_normal = jnp.mean(scaled * normal, axis=-1, keepdims=True)
    return (scaled - mean - normal * mean_normal) * inverse


COST = pl.CostEstimate(flops=1000000, bytes_accessed=0, transcendentals=0)


EXTRA = 6 * 1024 * 1024


def room(value):
    return math.prod(value.shape) * jnp.dtype(value.dtype).itemsize


def run(name, kernel, outs, scalars, *args, scratch=()):
    many = isinstance(outs, (tuple, list))
    held = sum(room(v) for v in args) + sum(room(v) for v in (outs if many else [outs]))
    held += sum(room(v) for v in scratch)
    return pl.pallas_call(
        kernel,
        out_shape=outs,
        in_specs=[SMEM_SPEC] * len(scalars) + [VMEM_SPEC] * len(args),
        out_specs=[VMEM_SPEC] * len(outs) if many else VMEM_SPEC,
        scratch_shapes=list(scratch),
        cost_estimate=COST,
        compiler_params=pltpu.CompilerParams(vmem_limit_bytes=held + EXTRA),
        name=name,
    )(*scalars, *args)


def shape(dims, kind=bf16):
    return jax.ShapeDtypeStruct(tuple(dims), kind)


def cut_attention_kernel(place, own_qkv, got_qkv, *outs):
    core = place[0]
    rows, width = own_qkv.shape
    width = width // 3
    half = width // 2
    mine, theirs = at(core * rows, rows), at((1 - core) * rows, rows)
    for p, out in enumerate(outs):
        for part in range(3):
            cols = lanes(core * half + (part * width + p * LANES), LANES)
            here = slice(part * LANES, (part + 1) * LANES)
            out[mine, here] = own_qkv[:, cols]
            out[theirs, here] = got_qkv[:, cols]


def cut_rest_kernel(place, own_out, own_up, own_down, got, out_piece, out_piece_got, ff_piece):
    core = place[0]
    rows, width = own_out.shape
    half = width // 2
    for out, part in ((out_piece, core), (out_piece_got, 1 - core)):
        cols = lanes(part * half, half)
        out[at(core * rows, rows), :] = own_out[:, cols]
        out[at((1 - core) * rows, rows), :] = got[:rows, cols]
    half = own_up.shape[1] // 2
    cols = lanes(core * half, half)
    units = own_up.shape[1]
    for i, own in enumerate((own_up, own_down)):
        ff_piece[at(core * rows + i * 2 * rows, rows), :] = own[:, cols]
        if units == width:
            ff_piece[at((1 - core) * rows + i * 2 * rows, rows), :] = got[(1 + i) * rows : (2 + i) * rows, cols]
        else:
            cols_got = lanes(core * half + i * units, half)
            ff_piece[at((1 - core) * rows + i * 2 * rows, rows), :] = got[rows:, cols_got]


def join(place, chips, pieces, outs):
    parts = len(outs)
    span = pieces[0].shape[0] // parts
    for j in range(min(chips, len(pieces))):
        for i, out in enumerate(outs):
            rows = at(place[1 + j], span)
            if len(pieces) == chips or j < chips - 1:
                out[rows, :] = pieces[j][i * span : (i + 1) * span, :]
            elif parts == 1:
                half = span // 2
                out[pl.ds(pl.multiple_of(place[1 + j], half), half), :] = pieces[j][...]
                out[pl.ds(pl.multiple_of(place[1 + j] + half, half), half), :] = pieces[j + 1][...]
            else:
                out[rows, :] = pieces[j + i][...]


def join_kernel(chips, many, place, *refs):
    *pieces, mine, got = refs
    join(place, chips, pieces[:many], [mine])
    join(place, chips, pieces[many:], [got])


def norm_kernel(own, other, gain, bias, out):
    seq_len = own.shape[0]
    block = 128

    def step(i, carry):
        rows = at(i * block, block)
        for k, ref in enumerate((own, other)):
            normal, _ = normal_of(ref[rows, :].astype(f32))
            out[at(k * seq_len + i * block, block), :] = (normal * gain[...] + bias[...]).astype(bf16)
        return carry

    lax.fori_loop(0, seq_len // block, step, 0)


def allowed_block(seg_col, seg_row, row_start, block, extent):
    row_place = row_start + lax.broadcasted_iota(jnp.int32, (block, extent), 0)
    col_place = lax.broadcasted_iota(jnp.int32, (block, extent), 1)
    return (row_place >= col_place) & (seg_col == seg_row)


def attend_kernel(chips, seq_len, place, norm_ref, cos_ref, sin_ref, segc_ref, segr_ref, *refs):
    *pieces, wide_ref, qkv_ref, ctx_ref, lse_ref = refs
    join(place, chips, pieces, [wide_ref])
    hd = HEAD_DIM
    block = seq_len // 2

    def project(i, carry):
        rows = at(i * block, block)
        joined = jnp.dot(norm_ref[rows, :], wide_ref[...], preferred_element_type=f32)
        table = at((i % 2) * block, block)
        cosine, sine = cos_ref[table, :], sin_ref[table, :]
        for h in range(2 * PAIR):
            part = joined[:, h * hd : (h + 1) * hd]
            qkv_ref[rows, h * hd : (h + 1) * hd] = (part * cosine + turn(part) * sine).astype(bf16)
        qkv_ref[rows, 2 * PAIR * hd :] = joined[:, 2 * PAIR * hd :].astype(bf16)
        return carry

    lax.fori_loop(0, 4, project, 0)

    lane = lax.broadcasted_iota(jnp.int32, (block, hd), 1)

    def sequence(s, carry):
        base = s * seq_len
        for r in range(2):
            extent = (r + 1) * block
            rows = at(base + r * block, block)
            cols = pl.ds(pl.multiple_of(base, block), extent)
            allowed = allowed_block(
                segc_ref[s, r * block : (r + 1) * block, :],
                segr_ref[s, :, :extent],
                r * block,
                block,
                extent,
            )
            logs = jnp.zeros((block, hd), f32)
            for h in range(PAIR):
                query = qkv_ref[rows, h * hd : (h + 1) * hd]
                key = qkv_ref[cols, (PAIR + h) * hd : (PAIR + h + 1) * hd]
                value = qkv_ref[cols, (2 * PAIR + h) * hd : (2 * PAIR + h + 1) * hd]
                scores = lax.dot_general(query, key, contract_cols, preferred_element_type=f32)
                scores = jnp.where(allowed, scores * score_scale, -1000000000.0)
                top = jnp.max(scores, axis=-1, keepdims=True)
                weight = jnp.exp(scores - top)
                total = jnp.sum(weight, axis=-1, keepdims=True)
                probs = (weight * (1.0 / total)).astype(bf16)
                ctx_ref[s, r * block : (r + 1) * block, h * hd : (h + 1) * hd] = jnp.dot(
                    probs, value, preferred_element_type=f32
                ).astype(bf16)
                logs = jnp.where(lane == h, top + jnp.log(total), logs)
            lse_ref[rows, :] = logs
        return carry

    lax.fori_loop(0, 2, sequence, 0)


def out_kernel(chunks, place, x_ref, *refs):
    mine, got = refs[:chunks], refs[chunks : 2 * chunks]
    w_mine, w_got, gain, bias, hidden, norm, ctx = refs[2 * chunks :]
    core = place[0]
    seq_len, width = x_ref.shape
    half = width // 2
    own_cols, got_cols = lanes(core * half, half), lanes((1 - core) * half, half)
    for p in range(chunks):
        here = lanes(core * half + p * LANES, LANES)
        there = lanes((1 - core) * half + p * LANES, LANES)
        ctx[:, here] = mine[p][...]
        ctx[:, there] = got[p][...]
    block = 128

    def step(i, carry):
        rows = at(i * block, block)
        hidden[rows, own_cols] = jnp.dot(ctx[rows, :], w_mine[...], preferred_element_type=f32)
        hidden[rows, got_cols] = jnp.dot(ctx[rows, :], w_got[...], preferred_element_type=f32)
        values = hidden[rows, :] + x_ref[rows, :].astype(f32)
        hidden[rows, :] = values
        normal, _ = normal_of(values)
        norm[rows, :] = (normal * gain[...] + bias[...]).astype(bf16)
        return carry

    lax.fori_loop(0, seq_len // block, step, 0)


def out_back_kernel(place, grad, w_mine, w_got, keep, send, grad_send):
    core = place[0]
    seq_len, width = grad.shape
    half = width // 2
    own_cols, got_cols = lanes(core * half, half), lanes((1 - core) * half, half)
    grad_send[...] = grad[:, got_cols]
    for out, part in ((send, 1 - core), (keep, core)):
        rows = at(part * half, half)

        def step(i, carry):
            here = at(i * 256, 256)
            out[here, :] = (
                lax.dot_general(grad[here, own_cols], w_mine[rows, :], contract_cols, preferred_element_type=f32)
                + lax.dot_general(grad[here, got_cols], w_got[rows, :], contract_cols, preferred_element_type=f32)
            ).astype(bf16)
            return carry

        lax.fori_loop(0, seq_len // 256, step, 0)


def spread(place, outs, product):
    if len(outs) > 1:
        span = outs[0].shape[0]
        for j, out in enumerate(outs[:3]):
            out[...] = product(lanes(place[1 + j], span)).astype(bf16)
        corner = product(lanes(place[4], span)).astype(bf16)
        outs[3][...] = corner[: span // 2, :]
        outs[4][...] = corner[span // 2 :, :]
    else:
        for start in range(0, outs[0].shape[0], 256):
            here = slice(start, start + 256)
            outs[0][here, :] = product(here).astype(bf16)


def out_weight_kernel(chunks, place, ctx, grad, grad_got, *refs):
    mine, got, outs, other = refs[:chunks], refs[chunks : 2 * chunks], refs[2 * chunks : -1], refs[-1]
    core = place[0]
    seq_len, width = grad.shape
    half = width // 2
    cols = lanes(core * half, half)
    for p in range(chunks):
        other[:, lanes(core * half + p * LANES, LANES)] = mine[p][...]
        other[:, lanes((1 - core) * half + p * LANES, LANES)] = got[p][...]

    def product(here):
        return lax.dot_general(
            ctx[:, here], grad[:, cols], contract_rows, preferred_element_type=f32
        ) + lax.dot_general(other[:, here], grad_got[...], contract_rows, preferred_element_type=f32)

    spread(place, outs, product)


def attend_back_kernel(
    chunk, place, qkv_ref, lse_ref, keep, got, norm, cos_ref, sin_ref, segc_ref, segr_ref, out_ref, *refs
):
    *pieces, gq, gk, gv = refs
    hd = HEAD_DIM
    seq_len = keep.shape[0]
    block = seq_len // 2
    for s, grad_ref in enumerate((keep, got)):
        base = s * seq_len
        for h in range(PAIR):
            lane = slice(chunk * LANES + h * hd, chunk * LANES + (h + 1) * hd)
            for r in (1, 0):
                extent = (r + 1) * block
                rows = slice(base + r * block, base + (r + 1) * block)
                cols = slice(base, base + extent)
                allowed = allowed_block(
                    segc_ref[s, r * block : (r + 1) * block, :],
                    segr_ref[s, :, :extent],
                    r * block,
                    block,
                    extent,
                )
                query = qkv_ref[rows, h * hd : (h + 1) * hd]
                key = qkv_ref[cols, (PAIR + h) * hd : (PAIR + h + 1) * hd]
                value = qkv_ref[cols, (2 * PAIR + h) * hd : (2 * PAIR + h + 1) * hd]
                grad = grad_ref[r * block : (r + 1) * block, lane]
                scores = lax.dot_general(query, key, contract_cols, preferred_element_type=f32)
                scores = jnp.where(allowed, scores * score_scale, -1000000000.0)
                probs = jnp.exp(scores - lse_ref[rows, h : h + 1])
                grad_probs = lax.dot_general(grad, value, contract_cols, preferred_element_type=f32)
                weighted = jnp.sum(probs * grad_probs, axis=-1, keepdims=True)
                grad_scores = (probs * (grad_probs - weighted) * score_scale).astype(bf16)
                probs = probs.astype(bf16)
                gq[r * block : (r + 1) * block, :] = jnp.dot(grad_scores, key, preferred_element_type=f32)
                grad_key = lax.dot_general(grad_scores, query, contract_rows, preferred_element_type=f32)
                grad_value = lax.dot_general(probs, grad, contract_rows, preferred_element_type=f32)
                if r == 1:
                    gk[...] = grad_key
                    gv[...] = grad_value
                else:
                    gk[:block, :] = gk[:block, :] + grad_key
                    gv[:block, :] = gv[:block, :] + grad_value
            sine, cosine = sin_ref[...], cos_ref[...]
            rows = slice(base, base + seq_len)
            grad_query, grad_key = gq[...], gk[...]
            out_ref[rows, h * hd : (h + 1) * hd] = (
                grad_query * cosine + turn_back(grad_query * sine)
            ).astype(bf16)
            out_ref[rows, (PAIR + h) * hd : (PAIR + h + 1) * hd] = (
                grad_key * cosine + turn_back(grad_key * sine)
            ).astype(bf16)
            out_ref[rows, (2 * PAIR + h) * hd : (2 * PAIR + h + 1) * hd] = gv[...].astype(bf16)

    def product(here):
        return lax.dot_general(norm[:, here], out_ref[...], contract_rows, preferred_element_type=f32)

    spread(place, pieces, product)


def ff_act_kernel(chips, index, place, limits, *refs):
    if chips:
        norm_a, norm_b, cot_a, cot_b, *pieces, act_a, act_b, grad_a, grad_b, up, down = refs
        join(place, chips, pieces, [up, down])
        norms = ([norm_a], [norm_b])
        first = 0
    else:
        norm_a, norm_low, norm_high, cot_a, cot_b, up, down, act_a, act_b, grad_a, grad_b = refs
        norms = ([norm_a], [norm_low, norm_high])
        first = 2
    sides = zip(norms, (cot_a, cot_b), (act_a, act_b), (grad_a, grad_b))
    units = up.shape[1]
    block, tile = 256, 256 if units % 256 == 0 else 128
    for s, (norm_parts, cot, act, grad) in enumerate(sides):
        limit = limits[index, first + s]
        for k, norm in enumerate(norm_parts):
            length = norm.shape[0]

            def step(i, carry):
                here = at(i * block, block)
                rows = at(k * length + i * block, block)
                for n in range(0, units, tile):
                    cols = slice(n, n + tile)
                    preact = jnp.dot(norm[here, :], up[:, cols], preferred_element_type=f32)
                    grad_active = jnp.dot(cot[rows, :], down[:, cols], preferred_element_type=f32)
                    mask = n + lax.broadcasted_iota(jnp.int32, (block, tile), 1) < limit
                    cdf = 0.5 * (1.0 + lax.erf(preact * 0.7071067811865476))
                    slope = cdf + preact * jnp.exp(-0.5 * preact * preact) * 0.3989422804014327
                    act[rows, cols] = jnp.where(mask, preact * cdf, 0.0).astype(bf16)
                    grad[rows, cols] = jnp.where(mask, grad_active * slope, 0.0).astype(bf16)
                return carry

            lax.fori_loop(0, length // block, step, 0)


def rows_back_kernel(count, base, *refs):
    grads, weights, outs = refs[:count], refs[count : 2 * count], refs[2 * count :]
    total = outs[0].shape[0]
    for k, out in enumerate(outs):

        def step(i, carry):
            rows = at(base + k * total + i * 256, 256)
            acc = 0.0
            for g, w in zip(grads, weights):
                acc = acc + lax.dot_general(g[rows, :], w[...], contract_cols, preferred_element_type=f32)
            out[at(i * 256, 256), :] = acc.astype(out.dtype)
            return carry

        lax.fori_loop(0, total // 256, step, 0)


def ff_weight_kernel(count, place, *refs):
    norms, cots = refs[:count], refs[count : 2 * count]
    acts, grads, outs = refs[2 * count : 3 * count], refs[3 * count : 4 * count], refs[4 * count :]
    span = norms[0].shape[1]
    corner = len(outs) == 5
    for j in range(4 if corner else len(outs)):

        @pl.when(pl.program_id(0) == j)
        def _():
            for i, (lefts, rights) in enumerate(((norms, grads), (cots, acts))):
                acc = 0.0
                for left, right in zip(lefts, rights):
                    acc = acc + lax.dot_general(
                        left[...], right[...], contract_rows, preferred_element_type=f32
                    )
                if corner and j == 3:
                    outs[3 + i][...] = acc.astype(bf16)
                else:
                    outs[j][i * span : (i + 1) * span, :] = acc.astype(bf16)


def ff_weight(order, chips, norms, cots, acts, grads):
    seq_len, width = norms[0].shape
    units = acts[0].shape[1]
    span = width // chips
    count = len(norms)
    outs = [(2 * span, units)] * chips
    if chips == 4:
        outs = [(2 * span, units)] * 3 + [(span, units)] * 2
    wide = pl.BlockSpec((seq_len, span), lambda j, order: (0, order[j]))
    whole = pl.BlockSpec((seq_len, units), lambda j, order: (0, 0))
    return pl.pallas_call(
        functools.partial(ff_weight_kernel, count),
        out_shape=[shape(v) for v in outs],
        grid_spec=pltpu.PrefetchScalarGridSpec(
            num_scalar_prefetch=1,
            grid=(chips,),
            in_specs=[wide] * (2 * count) + [whole] * (2 * count),
            out_specs=[pl.BlockSpec(v, lambda j, order: (0, 0)) for v in outs],
        ),
        cost_estimate=COST,
        compiler_params=pltpu.CompilerParams(vmem_limit_bytes=40 * 1024 * 1024),
        name="ff_weight",
    )(order, *norms, *cots, *acts, *grads)


def second_back_kernel(own, beside_a, beside_b, near, hidden, cot, gain, grad_hidden, grad_low, sums):
    seq_len, width = own.shape
    block = 64
    sums[...] = jnp.zeros_like(sums)

    def step(i, carry, first, beside):
        rows = at(first + i * block, block)
        grad = own[rows, :] + beside[at(i * block, block), :].astype(f32) + near[rows, :].astype(f32)
        normal, inverse = normal_of(hidden[rows, :])
        sums[0:1, :] += jnp.sum(grad * normal, axis=0, keepdims=True)
        sums[1:2, :] += jnp.sum(grad, axis=0, keepdims=True)
        back = cot[rows, :].astype(f32) + norm_back(grad, normal, inverse, gain[...])
        grad_hidden[rows, :] = back
        grad_low[rows, :] = back.astype(bf16)
        return carry

    for k, ref in enumerate((beside_a, beside_b)):
        part = functools.partial(step, first=k * seq_len // 2, beside=ref)
        lax.fori_loop(0, seq_len // 2 // block, part, 0)


def first_back_kernel(own, beside, x_ref, grad_hidden, gain, out, sums):
    seq_len, width = own.shape
    block = 64
    sums[...] = jnp.zeros_like(sums)

    def step(i, carry):
        rows = at(i * block, block)
        grad = own[rows, :] + beside[rows, :].astype(f32)
        normal, inverse = normal_of(x_ref[rows, :].astype(f32))
        sums[0:1, :] += jnp.sum(grad * normal, axis=0, keepdims=True)
        sums[1:2, :] += jnp.sum(grad, axis=0, keepdims=True)
        out[rows, :] = grad_hidden[rows, :] + norm_back(grad, normal, inverse, gain[...])
        return carry

    lax.fori_loop(0, seq_len // block, step, 0)


def place_attention_kernel(count, place, *refs):
    mine, got, out = refs[:count], refs[count : 2 * count], refs[2 * count]
    core = place[0]
    rows = out.shape[0]
    width = out.shape[1] // 3
    half = width // 2
    here = at(core * rows, rows)
    for p in range(count):
        for part in range(3):
            cols = slice(part * LANES, (part + 1) * LANES)
            base = part * width + p * LANES
            out[:, lanes(core * half + base, LANES)] = mine[p][here, cols].astype(f32)
            out[:, lanes((1 - core) * half + base, LANES)] = got[p][here, cols].astype(f32)


def place_halves_kernel(place, *refs):
    mine, got, outs = refs[0], refs[1], refs[2:]
    core = place[0]
    rows = outs[0].shape[0]
    half = outs[0].shape[1] // 2
    for i, out in enumerate(outs):
        here = at(core * rows + i * 2 * rows, rows)
        out[:, lanes(core * half, half)] = mine[here, :].astype(f32)
        out[:, lanes((1 - core) * half, half)] = got[here, :].astype(f32)


def tie(value, *others):
    return lax.optimization_barrier((value, *others))[0]


def build(dp_size, mp_size):
    total = dp_size * mp_size
    chip_bits = []
    bit = 2 * mp_size
    while bit < total:
        chip_bits.append(bit)
        bit *= 2
    core_bit = mp_size
    near_bit = 1
    far_bits = []
    bit = 2
    while bit < mp_size:
        far_bits.append(bit)
        bit *= 2
    chips = dp_size // 2

    def flip(value, bit):
        return lax.ppermute(value, AXES, [(i, i ^ bit) for i in range(total)])

    def add(a, b):
        return a.astype(f32) + b.astype(f32)

    def add_low(a, b):
        return add(a, b).astype(bf16)

    class Line:
        def __init__(self):
            self.last = []
            self.open = {}

        def end(self, *values):
            for v in values:
                self.open.pop(id(v), None)

        def after(self, value, *waits):
            self.end(value, *waits)
            waits = list(waits) + self.last
            return tie(value, *waits) if waits else value

        def wait(self, *transfers):
            self.end(*transfers)
            self.last = self.last + list(transfers)

        def send(self, value, bit):
            result = flip(self.after(value), bit)
            self.open[id(result)] = (result, bit)
            return result

        def kernel(self, name, kernel, outs, scalars, *args, wait=(), scratch=()):
            self.end(*args)
            args = (self.after(args[0], *wait),) + args[1:]
            result = run(name, kernel, outs, scalars, *args, scratch=scratch)
            self.last = [result[0] if isinstance(result, (tuple, list)) else result]
            return result

        def op(self, function, *args):
            self.end(*args)
            result = function(self.after(args[0]), *args[1:])
            self.last = [result[0] if isinstance(result, (tuple, list)) else result]
            return result

    two = len(chip_bits) == 2

    class Gather:
        def __init__(self, line, piece):
            self.line, self.piece = line, piece
            if two:
                self.x = line.send(piece, chip_bits[0])
                self.y = line.send(piece, chip_bits[1])
            else:
                held = [line.after(piece)]
                for bit in chip_bits:
                    held = held + [flip(value, bit) for value in held]
                self.all = held

        def turn(self):
            if two:
                half = self.piece.shape[0] // 2
                self.line.wait(self.x, self.y)
                low = self.line.op(lambda v: v[:half], self.x)
                self.low = self.line.send(low, chip_bits[1])
                high = self.line.op(lambda v: v[half:], self.y)
                self.high = self.line.send(high, chip_bits[0])

        def wait(self):
            if two:
                self.line.wait(self.low, self.high)

        def send_first(self, bit):
            if two:
                return [self.line.send(v, bit) for v in (self.x, self.y)]
            return [flip(v, bit) for v in self.all[1:]]

        def send_last(self, bit):
            if two:
                corner = self.line.op(lambda a, b: jnp.concatenate([a, b]), self.low, self.high)
                return [self.line.send(corner, bit)]
            return []

        def pieces(self):
            return [self.piece, self.x, self.y, self.low, self.high] if two else self.all

    class Scatter:
        def __init__(self, line, parts):
            self.line, self.parts = line, parts
            if two:
                self.low = line.send(parts[3], chip_bits[0])
                self.high = line.send(parts[4], chip_bits[1])

        def turn(self):
            if two:
                _, to_x, to_y, low, high = self.parts
                half = low.shape[0]
                self.line.wait(self.low, self.high)
                to_y = self.line.op(lambda v, g: v.at[:half].set(add_low(v[:half], g)), to_y, self.low)
                self.y = self.line.send(to_y, chip_bits[1])
                to_x = self.line.op(lambda v, g: v.at[half:].set(add_low(v[half:], g)), to_x, self.high)
                self.x = self.line.send(to_x, chip_bits[0])

        def close(self):
            if two:
                return self.line.op(
                    lambda own, a, b: (add(own, a) + b.astype(f32)).astype(bf16),
                    self.parts[0],
                    self.x,
                    self.y,
                )
            held = list(self.parts)
            for bit in reversed(chip_bits):
                middle = len(held) // 2
                held = [add_low(a, flip(b, bit)) for a, b in zip(held[:middle], held[middle:])]
            return held[0]

    class OverMp:
        def __init__(self, line, share):
            self.line = line
            size = share.shape[0] // 2
            self.upper = lax.axis_index("mp") % 2
            send = line.op(lambda v: lax.dynamic_slice_in_dim(v, (1 - self.upper) * size, size, axis=0), share)
            self.keep = lax.dynamic_slice_in_dim(share, self.upper * size, size, axis=0)
            self.got = line.send(send, near_bit)

        def turn(self):
            value = self.line.op(add_low, self.keep, self.got)
            for bit in far_bits[:-1]:
                value = add_low(value, flip(value, bit))
            self.keep = value
            self.got = self.line.send(value, far_bits[-1])

        def back(self):
            self.keep = self.line.op(add_low, self.keep, self.got)
            self.got = self.line.send(self.keep, near_bit)

        def close(self):
            def joined(keep, got):
                low = jnp.where(self.upper == 0, keep, got)
                return jnp.concatenate([low, jnp.where(self.upper == 0, got, keep)])

            return self.line.op(joined, self.keep, self.got)

    class SumAll:
        def __init__(self, line, value):
            self.line, self.value, self.bit = line, value, 1
            self.got = line.send(value, 1)

        def turn(self):
            if self.bit < total:
                self.value = self.line.op(jnp.add, self.value, self.got)
                self.bit *= 2
                if self.bit < total:
                    self.got = self.line.send(self.value, self.bit)

        def close(self):
            while self.bit < total:
                self.turn()
            return self.value

    def on_device(
        block_in,
        cotangent,
        segment_ids,
        granularity,
        w_qkv,
        w_out,
        w_up,
        w_down,
        norm1_gain,
        norm1_bias,
        norm2_gain,
        norm2_bias,
    ):
        seq_len, width = block_in.shape
        rows = width // dp_size
        units = w_up.shape[1]
        half_units = units // 2
        half = width // 2
        dp = lax.axis_index("dp")
        mp = lax.axis_index("mp")
        core = dp % 2
        chip = dp // 2
        span = 2 * rows
        order = jnp.stack([chip ^ j for j in range(chips)]).astype(jnp.int32)
        place = jnp.concatenate([core[None].astype(jnp.int32), order * span])
        chunks = HEADS // 2 // PAIR
        chunk_cols = 3 * LANES
        gain1, bias1 = norm1_gain[None], norm1_bias[None]
        gain2, bias2 = norm2_gain[None], norm2_bias[None]
        line = Line()

        def parts_shapes(cols):
            if span % 128 == 0 and chips == 4:
                return [shape((span, cols))] * 3 + [shape((rows, cols))] * 2
            return [shape((width, cols))]

        def by_chip(parts):
            if len(parts) > 1:
                return parts
            return [lax.dynamic_slice_in_dim(parts[0], place[1 + j], span, axis=0) for j in range(chips)]

        def ff_parts(*groups):
            if span % 128 == 0 and chips == 4:
                return ff_weight(order, chips, *groups)
            blocks = width // 256
            parts = ff_weight(jnp.arange(blocks, dtype=jnp.int32), blocks, *groups)
            sides = [
                by_chip([jnp.concatenate([v[i * 256 : (i + 1) * 256] for v in parts])]) for i in range(2)
            ]
            return [jnp.concatenate(v) for v in zip(*sides)]

        w_down_t = w_down.T
        qkv_other = line.send(w_qkv, core_bit)
        small = jnp.concatenate([segment_ids, jnp.broadcast_to(granularity[:, None], (mp_size, seq_len))])
        small_other = line.send(small, core_bit)
        x_other = line.send(block_in, core_bit)
        if units == width:
            rest = jnp.concatenate([w_out, w_up, w_down_t])
        else:
            rest = jnp.concatenate([w_out, jnp.concatenate([w_up, w_down_t], axis=1)])
        rest_other = line.send(rest, core_bit)

        qkv_pieces = line.kernel(
            "cut_attention",
            cut_attention_kernel,
            [shape((span, chunk_cols))] * chunks,
            [place],
            w_qkv,
            qkv_other,
            wait=(small_other,),
        )
        heads = [Gather(line, qkv_pieces[0])]
        cot_near = line.send(cotangent, near_bit)
        normed1 = line.kernel(
            "norm",
            norm_kernel,
            shape((2 * seq_len, width)),
            [],
            block_in,
            x_other,
            gain1,
            bias1,
        )
        out_piece, out_piece_got, ff_piece = line.kernel(
            "cut_rest",
            cut_rest_kernel,
            [shape((span, half))] * 2 + [shape((2 * span, half_units))],
            [place],
            w_out,
            w_up,
            w_down_t,
            rest_other,
        )
        heads.append(Gather(line, qkv_pieces[1]))
        cosine, sine = rotary_tables(seq_len, HEAD_DIM)
        last = mp_size // 2 - 1

        qkv_wide, qkv_low, contexts, logs = [], [], [], []

        def attend(p):
            a, b, c, d = line.kernel(
                "attend",
                functools.partial(attend_kernel, chips, seq_len),
                [
                    shape((width, chunk_cols)),
                    shape((2 * seq_len, chunk_cols)),
                    shape((2, seq_len, LANES)),
                    shape((2 * seq_len, HEAD_DIM), f32),
                ],
                [place],
                normed1,
                cosine,
                sine,
                seg_col,
                seg_row,
                *heads[p].pieces(),
            )
            qkv_wide.append(a)
            qkv_low.append(b)
            contexts.append(c)
            logs.append(d)

        heads[0].turn()

        def from_small(own, other):
            segments = jnp.stack([own[0], other[0]])
            levels = jnp.stack([own[1:, 0], other[1:, 0]])
            ends = BLOCK * jnp.power(2, levels)
            ends = jnp.stack([ends[0, mp], ends[1, mp], ends[0, mp ^ 1], ends[1, mp ^ 1]])
            starts = [(mp ^ (2 * k)) * units + core * half_units for k in range(mp_size // 2)]
            limits = (ends[None, :] - jnp.stack(starts)[:, None]).astype(jnp.int32)
            return limits, segments[:, :, None], segments[:, None, :]

        limits, seg_col, seg_row = line.op(from_small, small, small_other)
        heads[1].turn()
        heads[0].wait()
        line.wait(cot_near)
        slices = [ff_piece]
        for bit in far_bits:
            slices = slices + [line.send(v, bit) for v in slices]
        heads.append(Gather(line, qkv_pieces[2]))
        attend(0)
        heads[1].wait()
        heads[2].turn()
        outs = Gather(line, out_piece)
        attend(1)
        heads[2].wait()
        ctx_near = [line.send(c[1], core_bit) for c in contexts]
        outs.turn()
        line.wait(*ctx_near)
        outs_other = [out_piece_got] + outs.send_first(core_bit)
        attend(2)
        outs.wait()
        line.wait(*outs_other[1:], *slices[1:])
        ffs = {0: Gather(line, slices[0])}
        ctx_near.append(line.send(contexts[2][1], core_bit))
        outs_other += outs.send_last(core_bit)
        out_mine, out_got = line.kernel(
            "join",
            functools.partial(join_kernel, chips, len(outs.pieces())),
            [shape((width, half))] * 2,
            [place],
            *outs.pieces(),
            *outs_other,
            wait=(ctx_near[2],),
        )
        cot_both = line.send(cot_near, core_bit)
        cot_core = line.send(cotangent, core_bit)
        hidden1, normed2, context = line.kernel(
            "out",
            functools.partial(out_kernel, chunks),
            [shape((seq_len, width), f32), shape((seq_len, width)), shape((seq_len, width))],
            [place],
            block_in,
            *[c[0] for c in contexts],
            *ctx_near,
            out_mine,
            out_got,
            gain2,
            bias2,
        )

        line.wait(cot_both, cot_core)
        norm_near = line.send(normed2, near_bit)
        norm_core = line.send(normed2, core_bit)
        ffs[0].turn()
        ffs[0].wait()
        line.wait(norm_core)
        for k in range(1, last + 1):
            ffs[k] = Gather(line, slices[k])
        cot_rows = [cotangent, cot_core, cot_near, cot_both]
        outs_ff = [shape((seq_len, half_units))] * 4
        wide_ff = [shape((width, half_units))] * 2
        acts, grads, ups, downs = {}, {}, {}, {}

        def ff_own(k):
            act_a, act_b, grad_a, grad_b, up, down = line.kernel(
                "ff_own",
                functools.partial(ff_act_kernel, chips, k),
                outs_ff + wide_ff,
                [place, limits],
                normed2,
                norm_core,
                *cot_rows[:2],
                *ffs[k].pieces(),
            )
            acts[k] = [act_a, act_b]
            grads[k] = [grad_a, grad_b]
            ups[k] = up
            downs[k] = down

        def ff_near(k):
            act_a, act_b, grad_a, grad_b = line.kernel(
                "ff_near",
                functools.partial(ff_act_kernel, 0, k),
                outs_ff,
                [place, limits],
                norm_near,
                *norm_both,
                *cot_rows[2:],
                ups[k],
                downs[k],
            )
            acts[k] += [act_a, act_b]
            grads[k] += [grad_a, grad_b]

        def ff_grads(k):
            lefts = [line.after(normed2), norm_core, norm_near, norm_joined]
            parts = ff_parts(lefts, cot_rows, acts[k], grads[k])
            line.last = [parts[0]]
            return parts

        def rows_back(name, lefts, i, weights, kind, count=1):
            outs = [shape((seq_len // count, width), kind)] * count
            result = line.kernel(
                name,
                functools.partial(rows_back_kernel, len(weights), 0),
                outs,
                [],
                *[v[i] for v in lefts.values()],
                *weights.values(),
            )
            return result[0] if count == 1 else result

        def add_halves(a, low, high):
            middle = a.shape[0] // 2
            return jnp.concatenate([add_low(a[:middle], low), add_low(a[middle:], high)])

        ff_own(0)
        line.wait(norm_near)
        arrived = line.after(norm_near)
        middle = seq_len // 2
        norm_both = [line.send(v, core_bit) for v in (arrived[:middle], arrived[middle:])]
        line.wait(*norm_both)
        ff_near(0)
        norm_joined = line.op(lambda a, c: jnp.concatenate([a, c]), *norm_both)
        parts = ff_grads(0)
        for k in range(1, last + 1):
            ffs[k].turn()
        scatters = {0: Scatter(line, parts)}
        ctx_far = []
        for k in range(1, last + 1):
            if k == 1:
                ffs[1].wait()
                ctx_far = [line.send(c[0], core_bit) for c in contexts]
            ff_own(k)
            line.wait(*ctx_far)
            if k == 1:
                scatters[0].turn()
            ff_near(k)
        back_both = rows_back("ff_back", grads, 3, ups, bf16, 2)
        back_both = [line.send(v, core_bit) for v in back_both]
        back_near = rows_back("ff_back", grads, 2, ups, f32)
        back_near = line.op(add_halves, back_near, *back_both)
        back_near = line.send(back_near, near_bit)
        fore_both = rows_back("ff_fore", acts, 3, downs, bf16, 2)
        fore_near = rows_back("ff_fore", acts, 2, downs, f32)
        held = {}
        for k in range(1, last + 1):
            parts = ff_grads(k)
            if k == 1:
                held[0] = scatters[0].close()
            scatters[k] = Scatter(line, parts)
        back_beside = rows_back("ff_back", grads, 1, ups, bf16, 2)
        back_beside = [line.send(v, core_bit) for v in back_beside]
        back_own = rows_back("ff_back", grads, 0, ups, f32)

        grad_hidden1, grad_attn, sums2 = line.kernel(
            "second_back",
            second_back_kernel,
            [shape((seq_len, width), f32), shape((seq_len, width)), shape((8, width), f32)],
            [],
            back_own,
            *back_beside,
            back_near,
            hidden1,
            cotangent,
            gain2,
        )
        for k in range(1, last + 1):
            scatters[k].turn()
        fore_both = [line.send(v, core_bit) for v in fore_both]
        keep, send, grad_send = line.kernel(
            "out_back",
            out_back_kernel,
            [shape((seq_len, half))] * 3,
            [place],
            grad_attn,
            out_mine,
            out_got,
        )
        context_got = line.send(send, core_bit)
        line.wait(context_got, *fore_both)
        fore_near = line.op(add_halves, fore_near, *fore_both)
        fore_near = line.send(fore_near, near_bit)
        grad_got = line.send(grad_send, core_bit)
        grad_low, qkv_scatters = [], []

        def attend_back(p):
            low, *parts = line.kernel(
                "attend_back",
                functools.partial(attend_back_kernel, p),
                [shape((2 * seq_len, chunk_cols))] + parts_shapes(chunk_cols),
                [place],
                qkv_low[p],
                logs[p],
                keep,
                context_got,
                normed1,
                cosine,
                sine,
                seg_col,
                seg_row,
                scratch=[pltpu.VMEM((seq_len, HEAD_DIM), f32)] * 3,
            )
            grad_low.append(low)
            return by_chip(parts)

        parts = attend_back(0)
        line.wait(grad_got)
        qkv_scatters.append(Scatter(line, parts))
        out_parts = line.kernel(
            "out_weight",
            functools.partial(out_weight_kernel, chunks),
            parts_shapes(half),
            [place],
            context,
            grad_attn,
            grad_got,
            *[c[1] for c in contexts],
            *ctx_far,
            scratch=[pltpu.VMEM((seq_len, width), bf16)],
        )
        for k in range(1, last + 1):
            held[k] = scatters[k].close()
        far_got = line.send(held[last], far_bits[0]) if len(far_bits) == 1 else None
        qkv_scatters[0].turn()
        parts = attend_back(1)
        line.wait(fore_near)
        qkv_scatters.append(Scatter(line, parts))
        first, second = qkv_scatters
        first_z = OverMp(line, first.close())
        second.turn()
        parts = attend_back(2)
        if len(far_bits) == 1:
            line.wait(far_got)
        second_share = second.close()
        third = Scatter(line, parts)
        back_other = line.kernel(
            "qkv_back",
            functools.partial(rows_back_kernel, chunks, seq_len),
            [shape((seq_len, width))],
            [],
            *grad_low,
            *qkv_wide,
        )[0]
        back_mine = line.kernel(
            "qkv_back",
            functools.partial(rows_back_kernel, chunks, 0),
            [shape((seq_len, width), f32)],
            [],
            *grad_low,
            *qkv_wide,
        )[0]
        first_z.turn()
        second_z = OverMp(line, second_share)
        third.turn()
        back_other = line.send(back_other, core_bit)
        grad_input, sums1 = line.kernel(
            "first_back",
            first_back_kernel,
            [shape((seq_len, width), f32), shape((8, width), f32)],
            [],
            back_mine,
            back_other,
            block_in,
            grad_hidden1,
            gain1,
        )
        second_z.turn()
        third_share = third.close()
        fourth = Scatter(line, by_chip(out_parts))
        third_z = OverMp(line, third_share)
        first_z.back()
        fourth.turn()
        third_z.turn()
        first_share = first_z.close()
        fourth_z = OverMp(line, fourth.close())
        second_z.back()
        sums = SumAll(line, jnp.concatenate([sums1[:2], sums2[:2]]))
        fore_beside = rows_back("ff_fore", acts, 1, downs, bf16)
        fourth_z.turn()
        third_z.back()
        sums.turn()
        second_share = second_z.close()
        fore_own = rows_back("ff_fore", acts, 0, downs, f32)
        sums.turn()
        third_share = third_z.close()
        if len(far_bits) == 1:
            ff_share = line.op(add_low, held[0], far_got)
        else:
            held = [held[k] for k in range(len(slices))]
            for bit in reversed(far_bits):
                middle = len(held) // 2
                held = [add_low(a, flip(c, bit)) for a, c in zip(held[:middle], held[middle:])]
            ff_share = held[0]
        sums.turn()
        fourth_z.back()
        first_got = line.send(first_share, core_bit)
        second_got = line.send(second_share, core_bit)
        third_got = line.send(third_share, core_bit)
        grad_w_qkv = line.kernel(
            "place_qkv",
            functools.partial(place_attention_kernel, chunks),
            shape((rows, 3 * width), f32),
            [place],
            first_share,
            second_share,
            third_share,
            first_got,
            second_got,
            third_got,
        )
        fore_beside = line.send(fore_beside, core_bit)
        ff_share_got = line.send(ff_share, core_bit)
        sums.turn()

        def finish(base, own, near, beside):
            return (base + own + near.astype(f32) + beside.astype(f32)).astype(bf16)

        block_out = line.op(finish, hidden1, fore_own, fore_near, fore_beside)
        grad_w_up, grad_w_down = line.kernel(
            "place_ff",
            place_halves_kernel,
            [shape((rows, units), f32)] * 2,
            [place],
            ff_share,
            ff_share_got,
        )
        grad_w_down = grad_w_down.T
        sums = sums.close()
        out_share = fourth_z.close()
        out_share_got = line.send(out_share, core_bit)
        grad_w_out = line.kernel(
            "place_out",
            place_halves_kernel,
            [shape((rows, width), f32)],
            [place],
            out_share,
            out_share_got,
        )[0]
        return (
            block_out,
            grad_input,
            grad_w_qkv,
            grad_w_out,
            grad_w_up,
            grad_w_down,
            sums[0],
            sums[1],
            sums[2],
            sums[3],
        )

    return on_device


def solution(mesh):
    return jax.shard_map(
        build(mesh.shape["dp"], mesh.shape["mp"]),
        mesh=mesh,
        in_specs=(
            P(("dp", "mp"), None),
            P(("dp", "mp"), None),
            P(("dp", "mp"), None),
            P("dp"),
            P("dp", None),
            P("dp", None),
            P("dp", "mp"),
            P("mp", "dp"),
            P(),
            P(),
            P(),
            P(),
        ),
        out_specs=(
            P(("dp", "mp"), None),
            P(("dp", "mp"), None),
            P("dp", None),
            P("dp", None),
            P("dp", "mp"),
            P("mp", "dp"),
            P(),
            P(),
            P(),
            P(),
        ),
        check_vma=False,
    )
```

```python
import functools
import math

import jax
import jax.numpy as jnp
import numpy as np
from jax import lax
from jax.experimental import pallas as pl
from jax.experimental.pallas import tpu as pltpu
from jax.sharding import PartitionSpec as P

HEADS = 12
HEAD_DIM = 128
BLOCK = 768
AXES = ("dp", "mp")
PAIR = 2
LANES = PAIR * HEAD_DIM

epsilon = 1e-05
theta_base = 10000.0
score_scale = HEAD_DIM ** (-0.5)
contract_rows = (((0,), (0,)), ((), ()))
contract_cols = (((1,), (1,)), ((), ()))
f32 = jnp.float32
bf16 = jnp.bfloat16
SMEM_SPEC = pl.BlockSpec(memory_space=pltpu.SMEM)
VMEM_SPEC = pl.BlockSpec(memory_space=pltpu.VMEM)


def rotary_tables(length, head_width):
    halfway = head_width // 2
    frequency = np.float32(theta_base) ** (np.float32(-2.0) * np.arange(halfway, dtype=np.float32) / head_width)
    angles = np.arange(length, dtype=np.float32)[:, None] * frequency.astype(np.float32)[None, :]
    angles = np.concatenate([angles, angles], axis=1).astype(np.float64)
    return jnp.asarray(np.cos(angles), f32), jnp.asarray(np.sin(angles), f32)


def turn(values):
    halfway = values.shape[-1] // 2
    return jnp.concatenate([-values[:, halfway:], values[:, :halfway]], axis=-1)


def turn_back(values):
    halfway = values.shape[-1] // 2
    return jnp.concatenate([values[:, halfway:], -values[:, :halfway]], axis=-1)


def at(start, size):
    return pl.ds(pl.multiple_of(start, size), size)


def lanes(start, size):
    return pl.ds(pl.multiple_of(start, 128), size)


def normal_of(values):
    average = jnp.mean(values, axis=-1, keepdims=True)
    centred = values - average
    variance = jnp.mean(centred * centred, axis=-1, keepdims=True)
    inverse = lax.rsqrt(variance + epsilon)
    return centred * inverse, inverse


def norm_back(grad, normal, inverse, gain):
    scaled = grad * gain
    mean = jnp.mean(scaled, axis=-1, keepdims=True)
    mean_normal = jnp.mean(scaled * normal, axis=-1, keepdims=True)
    return (scaled - mean - normal * mean_normal) * inverse


COST = pl.CostEstimate(flops=1000000, bytes_accessed=0, transcendentals=0)


EXTRA = 6 * 1024 * 1024


def room(value):
    return math.prod(value.shape) * jnp.dtype(value.dtype).itemsize


def run(name, kernel, outs, scalars, *args, scratch=()):
    many = isinstance(outs, (tuple, list))
    held = sum(room(v) for v in args) + sum(room(v) for v in (outs if many else [outs]))
    held += sum(room(v) for v in scratch)
    return pl.pallas_call(
        kernel,
        out_shape=outs,
        in_specs=[SMEM_SPEC] * len(scalars) + [VMEM_SPEC] * len(args),
        out_specs=[VMEM_SPEC] * len(outs) if many else VMEM_SPEC,
        scratch_shapes=list(scratch),
        cost_estimate=COST,
        compiler_params=pltpu.CompilerParams(vmem_limit_bytes=held + EXTRA),
        name=name,
    )(*scalars, *args)


def shape(dims, kind=bf16):
    return jax.ShapeDtypeStruct(tuple(dims), kind)


def cut_attention_kernel(place, own_qkv, got_qkv, *outs):
    core = place[0]
    rows, width = own_qkv.shape
    width = width // 3
    half = width // 2
    mine, theirs = at(core * rows, rows), at((1 - core) * rows, rows)
    for p, out in enumerate(outs):
        for part in range(3):
            cols = lanes(core * half + (part * width + p * LANES), LANES)
            here = slice(part * LANES, (part + 1) * LANES)
            out[mine, here] = own_qkv[:, cols]
            out[theirs, here] = got_qkv[:, cols]


def cut_rest_kernel(place, own_out, own_up, own_down, got, out_piece, out_piece_got, ff_piece):
    core = place[0]
    rows, width = own_out.shape
    half = width // 2
    for out, part in ((out_piece, core), (out_piece_got, 1 - core)):
        cols = lanes(part * half, half)
        out[at(core * rows, rows), :] = own_out[:, cols]
        out[at((1 - core) * rows, rows), :] = got[:rows, cols]
    half = own_up.shape[1] // 2
    cols = lanes(core * half, half)
    units = own_up.shape[1]
    for i, own in enumerate((own_up, own_down)):
        ff_piece[at(core * rows + i * 2 * rows, rows), :] = own[:, cols]
        if units == width:
            ff_piece[at((1 - core) * rows + i * 2 * rows, rows), :] = got[(1 + i) * rows : (2 + i) * rows, cols]
        else:
            cols_got = lanes(core * half + i * units, half)
            ff_piece[at((1 - core) * rows + i * 2 * rows, rows), :] = got[rows:, cols_got]


def join(place, chips, pieces, outs):
    parts = len(outs)
    span = pieces[0].shape[0] // parts
    for j in range(min(chips, len(pieces))):
        for i, out in enumerate(outs):
            rows = at(place[1 + j], span)
            if len(pieces) == chips or j < chips - 1:
                out[rows, :] = pieces[j][i * span : (i + 1) * span, :]
            elif parts == 1:
                half = span // 2
                out[pl.ds(pl.multiple_of(place[1 + j], half), half), :] = pieces[j][...]
                out[pl.ds(pl.multiple_of(place[1 + j] + half, half), half), :] = pieces[j + 1][...]
            else:
                out[rows, :] = pieces[j + i][...]


def join_kernel(chips, many, place, *refs):
    *pieces, mine, got = refs
    join(place, chips, pieces[:many], [mine])
    join(place, chips, pieces[many:], [got])


def norm_kernel(own, other, gain, bias, out):
    seq_len = own.shape[0]
    block = 128

    def step(i, carry):
        rows = at(i * block, block)
        for k, ref in enumerate((own, other)):
            normal, _ = normal_of(ref[rows, :].astype(f32))
            out[at(k * seq_len + i * block, block), :] = (normal * gain[...] + bias[...]).astype(bf16)
        return carry

    lax.fori_loop(0, seq_len // block, step, 0)


def allowed_block(seg_col, seg_row, row_start, block, extent):
    row_place = row_start + lax.broadcasted_iota(jnp.int32, (block, extent), 0)
    col_place = lax.broadcasted_iota(jnp.int32, (block, extent), 1)
    return (row_place >= col_place) & (seg_col == seg_row)


def attend_kernel(chips, seq_len, place, norm_ref, cos_ref, sin_ref, segc_ref, segr_ref, *refs):
    *pieces, wide_ref, qkv_ref, ctx_ref, lse_ref = refs
    join(place, chips, pieces, [wide_ref])
    hd = HEAD_DIM
    block = seq_len // 2

    def project(i, carry):
        rows = at(i * block, block)
        joined = jnp.dot(norm_ref[rows, :], wide_ref[...], preferred_element_type=f32)
        table = at((i % 2) * block, block)
        cosine, sine = cos_ref[table, :], sin_ref[table, :]
        for h in range(2 * PAIR):
            part = joined[:, h * hd : (h + 1) * hd]
            qkv_ref[rows, h * hd : (h + 1) * hd] = (part * cosine + turn(part) * sine).astype(bf16)
        qkv_ref[rows, 2 * PAIR * hd :] = joined[:, 2 * PAIR * hd :].astype(bf16)
        return carry

    lax.fori_loop(0, 4, project, 0)

    lane = lax.broadcasted_iota(jnp.int32, (block, hd), 1)

    def sequence(s, carry):
        base = s * seq_len
        for r in range(2):
            extent = (r + 1) * block
            rows = at(base + r * block, block)
            cols = pl.ds(pl.multiple_of(base, block), extent)
            allowed = allowed_block(
                segc_ref[s, r * block : (r + 1) * block, :],
                segr_ref[s, :, :extent],
                r * block,
                block,
                extent,
            )
            logs = jnp.zeros((block, hd), f32)
            for h in range(PAIR):
                query = qkv_ref[rows, h * hd : (h + 1) * hd]
                key = qkv_ref[cols, (PAIR + h) * hd : (PAIR + h + 1) * hd]
                value = qkv_ref[cols, (2 * PAIR + h) * hd : (2 * PAIR + h + 1) * hd]
                scores = lax.dot_general(query, key, contract_cols, preferred_element_type=f32)
                scores = jnp.where(allowed, scores * score_scale, -1000000000.0)
                top = jnp.max(scores, axis=-1, keepdims=True)
                weight = jnp.exp(scores - top)
                total = jnp.sum(weight, axis=-1, keepdims=True)
                probs = (weight * (1.0 / total)).astype(bf16)
                ctx_ref[s, r * block : (r + 1) * block, h * hd : (h + 1) * hd] = jnp.dot(
                    probs, value, preferred_element_type=f32
                ).astype(bf16)
                logs = jnp.where(lane == h, top + jnp.log(total), logs)
            lse_ref[rows, :] = logs
        return carry

    lax.fori_loop(0, 2, sequence, 0)


def out_kernel(chunks, place, x_ref, *refs):
    mine, got = refs[:chunks], refs[chunks : 2 * chunks]
    w_mine, w_got, gain, bias, hidden, norm, ctx = refs[2 * chunks :]
    core = place[0]
    seq_len, width = x_ref.shape
    half = width // 2
    own_cols, got_cols = lanes(core * half, half), lanes((1 - core) * half, half)
    for p in range(chunks):
        here = lanes(core * half + p * LANES, LANES)
        there = lanes((1 - core) * half + p * LANES, LANES)
        ctx[:, here] = mine[p][...]
        ctx[:, there] = got[p][...]
    block = 128

    def step(i, carry):
        rows = at(i * block, block)
        hidden[rows, own_cols] = jnp.dot(ctx[rows, :], w_mine[...], preferred_element_type=f32)
        hidden[rows, got_cols] = jnp.dot(ctx[rows, :], w_got[...], preferred_element_type=f32)
        values = hidden[rows, :] + x_ref[rows, :].astype(f32)
        hidden[rows, :] = values
        normal, _ = normal_of(values)
        norm[rows, :] = (normal * gain[...] + bias[...]).astype(bf16)
        return carry

    lax.fori_loop(0, seq_len // block, step, 0)


def out_back_kernel(place, grad, w_mine, w_got, keep, send, grad_send):
    core = place[0]
    seq_len, width = grad.shape
    half = width // 2
    own_cols, got_cols = lanes(core * half, half), lanes((1 - core) * half, half)
    grad_send[...] = grad[:, got_cols]
    for out, part in ((send, 1 - core), (keep, core)):
        rows = at(part * half, half)

        def step(i, carry):
            here = at(i * 256, 256)
            out[here, :] = (
                lax.dot_general(grad[here, own_cols], w_mine[rows, :], contract_cols, preferred_element_type=f32)
                + lax.dot_general(grad[here, got_cols], w_got[rows, :], contract_cols, preferred_element_type=f32)
            ).astype(bf16)
            return carry

        lax.fori_loop(0, seq_len // 256, step, 0)


def spread(place, outs, product):
    if len(outs) > 1:
        span = outs[0].shape[0]
        for j, out in enumerate(outs[:3]):
            out[...] = product(lanes(place[1 + j], span)).astype(bf16)
        corner = product(lanes(place[4], span)).astype(bf16)
        outs[3][...] = corner[: span // 2, :]
        outs[4][...] = corner[span // 2 :, :]
    else:
        for start in range(0, outs[0].shape[0], 256):
            here = slice(start, start + 256)
            outs[0][here, :] = product(here).astype(bf16)


def out_weight_kernel(chunks, place, ctx, grad, grad_got, *refs):
    mine, got, outs, other = refs[:chunks], refs[chunks : 2 * chunks], refs[2 * chunks : -1], refs[-1]
    core = place[0]
    seq_len, width = grad.shape
    half = width // 2
    cols = lanes(core * half, half)
    for p in range(chunks):
        other[:, lanes(core * half + p * LANES, LANES)] = mine[p][...]
        other[:, lanes((1 - core) * half + p * LANES, LANES)] = got[p][...]

    def product(here):
        return lax.dot_general(
            ctx[:, here], grad[:, cols], contract_rows, preferred_element_type=f32
        ) + lax.dot_general(other[:, here], grad_got[...], contract_rows, preferred_element_type=f32)

    spread(place, outs, product)


def attend_back_kernel(
    chunk, place, qkv_ref, lse_ref, keep, got, norm, cos_ref, sin_ref, segc_ref, segr_ref, out_ref, *refs
):
    *pieces, gq, gk, gv = refs
    hd = HEAD_DIM
    seq_len = keep.shape[0]
    block = seq_len // 2
    for s, grad_ref in enumerate((keep, got)):
        base = s * seq_len
        for h in range(PAIR):
            lane = slice(chunk * LANES + h * hd, chunk * LANES + (h + 1) * hd)
            for r in (1, 0):
                extent = (r + 1) * block
                rows = slice(base + r * block, base + (r + 1) * block)
                cols = slice(base, base + extent)
                allowed = allowed_block(
                    segc_ref[s, r * block : (r + 1) * block, :],
                    segr_ref[s, :, :extent],
                    r * block,
                    block,
                    extent,
                )
                query = qkv_ref[rows, h * hd : (h + 1) * hd]
                key = qkv_ref[cols, (PAIR + h) * hd : (PAIR + h + 1) * hd]
                value = qkv_ref[cols, (2 * PAIR + h) * hd : (2 * PAIR + h + 1) * hd]
                grad = grad_ref[r * block : (r + 1) * block, lane]
                scores = lax.dot_general(query, key, contract_cols, preferred_element_type=f32)
                scores = jnp.where(allowed, scores * score_scale, -1000000000.0)
                probs = jnp.exp(scores - lse_ref[rows, h : h + 1])
                grad_probs = lax.dot_general(grad, value, contract_cols, preferred_element_type=f32)
                weighted = jnp.sum(probs * grad_probs, axis=-1, keepdims=True)
                grad_scores = (probs * (grad_probs - weighted) * score_scale).astype(bf16)
                probs = probs.astype(bf16)
                gq[r * block : (r + 1) * block, :] = jnp.dot(grad_scores, key, preferred_element_type=f32)
                grad_key = lax.dot_general(grad_scores, query, contract_rows, preferred_element_type=f32)
                grad_value = lax.dot_general(probs, grad, contract_rows, preferred_element_type=f32)
                if r == 1:
                    gk[...] = grad_key
                    gv[...] = grad_value
                else:
                    gk[:block, :] = gk[:block, :] + grad_key
                    gv[:block, :] = gv[:block, :] + grad_value
            sine, cosine = sin_ref[...], cos_ref[...]
            rows = slice(base, base + seq_len)
            grad_query, grad_key = gq[...], gk[...]
            out_ref[rows, h * hd : (h + 1) * hd] = (
                grad_query * cosine + turn_back(grad_query * sine)
            ).astype(bf16)
            out_ref[rows, (PAIR + h) * hd : (PAIR + h + 1) * hd] = (
                grad_key * cosine + turn_back(grad_key * sine)
            ).astype(bf16)
            out_ref[rows, (2 * PAIR + h) * hd : (2 * PAIR + h + 1) * hd] = gv[...].astype(bf16)

    def product(here):
        return lax.dot_general(norm[:, here], out_ref[...], contract_rows, preferred_element_type=f32)

    spread(place, pieces, product)


def ff_act_kernel(chips, index, place, limits, *refs):
    if chips:
        norm_a, norm_b, cot_a, cot_b, *pieces, act_a, act_b, grad_a, grad_b, up, down = refs
        join(place, chips, pieces, [up, down])
        norms = ([norm_a], [norm_b])
        first = 0
    else:
        norm_a, norm_low, norm_high, cot_a, cot_b, up, down, act_a, act_b, grad_a, grad_b = refs
        norms = ([norm_a], [norm_low, norm_high])
        first = 2
    sides = zip(norms, (cot_a, cot_b), (act_a, act_b), (grad_a, grad_b))
    units = up.shape[1]
    block, tile = 256, 256 if units % 256 == 0 else 128
    for s, (norm_parts, cot, act, grad) in enumerate(sides):
        limit = limits[index, first + s]
        for k, norm in enumerate(norm_parts):
            length = norm.shape[0]

            def step(i, carry):
                here = at(i * block, block)
                rows = at(k * length + i * block, block)
                for n in range(0, units, tile):
                    cols = slice(n, n + tile)
                    preact = jnp.dot(norm[here, :], up[:, cols], preferred_element_type=f32)
                    grad_active = jnp.dot(cot[rows, :], down[:, cols], preferred_element_type=f32)
                    mask = n + lax.broadcasted_iota(jnp.int32, (block, tile), 1) < limit
                    cdf = 0.5 * (1.0 + lax.erf(preact * 0.7071067811865476))
                    slope = cdf + preact * jnp.exp(-0.5 * preact * preact) * 0.3989422804014327
                    act[rows, cols] = jnp.where(mask, preact * cdf, 0.0).astype(bf16)
                    grad[rows, cols] = jnp.where(mask, grad_active * slope, 0.0).astype(bf16)
                return carry

            lax.fori_loop(0, length // block, step, 0)


def rows_back_kernel(count, base, *refs):
    grads, weights, outs = refs[:count], refs[count : 2 * count], refs[2 * count :]
    total = outs[0].shape[0]
    for k, out in enumerate(outs):

        def step(i, carry):
            rows = at(base + k * total + i * 256, 256)
            acc = 0.0
            for g, w in zip(grads, weights):
                acc = acc + lax.dot_general(g[rows, :], w[...], contract_cols, preferred_element_type=f32)
            out[at(i * 256, 256), :] = acc.astype(out.dtype)
            return carry

        lax.fori_loop(0, total // 256, step, 0)


def ff_weight_kernel(count, place, *refs):
    norms, cots = refs[:count], refs[count : 2 * count]
    acts, grads, outs = refs[2 * count : 3 * count], refs[3 * count : 4 * count], refs[4 * count :]
    span = norms[0].shape[1]
    corner = len(outs) == 5
    for j in range(4 if corner else len(outs)):

        @pl.when(pl.program_id(0) == j)
        def _():
            for i, (lefts, rights) in enumerate(((norms, grads), (cots, acts))):
                acc = 0.0
                for left, right in zip(lefts, rights):
                    acc = acc + lax.dot_general(
                        left[...], right[...], contract_rows, preferred_element_type=f32
                    )
                if corner and j == 3:
                    outs[3 + i][...] = acc.astype(bf16)
                else:
                    outs[j][i * span : (i + 1) * span, :] = acc.astype(bf16)


def ff_weight(order, chips, norms, cots, acts, grads):
    seq_len, width = norms[0].shape
    units = acts[0].shape[1]
    span = width // chips
    count = len(norms)
    outs = [(2 * span, units)] * chips
    if chips == 4:
        outs = [(2 * span, units)] * 3 + [(span, units)] * 2
    wide = pl.BlockSpec((seq_len, span), lambda j, order: (0, order[j]))
    whole = pl.BlockSpec((seq_len, units), lambda j, order: (0, 0))
    return pl.pallas_call(
        functools.partial(ff_weight_kernel, count),
        out_shape=[shape(v) for v in outs],
        grid_spec=pltpu.PrefetchScalarGridSpec(
            num_scalar_prefetch=1,
            grid=(chips,),
            in_specs=[wide] * (2 * count) + [whole] * (2 * count),
            out_specs=[pl.BlockSpec(v, lambda j, order: (0, 0)) for v in outs],
        ),
        cost_estimate=COST,
        compiler_params=pltpu.CompilerParams(vmem_limit_bytes=30 * 1024 * 1024),
        name="ff_weight",
    )(order, *norms, *cots, *acts, *grads)


def second_back_kernel(own, beside_a, beside_b, near, hidden, cot, gain, grad_hidden, grad_low, sums):
    seq_len, width = own.shape
    block = 64
    sums[...] = jnp.zeros_like(sums)

    def step(i, carry, first, beside):
        rows = at(first + i * block, block)
        grad = own[rows, :] + beside[at(i * block, block), :].astype(f32) + near[rows, :].astype(f32)
        normal, inverse = normal_of(hidden[rows, :])
        sums[0:1, :] += jnp.sum(grad * normal, axis=0, keepdims=True)
        sums[1:2, :] += jnp.sum(grad, axis=0, keepdims=True)
        back = cot[rows, :].astype(f32) + norm_back(grad, normal, inverse, gain[...])
        grad_hidden[rows, :] = back
        grad_low[rows, :] = back.astype(bf16)
        return carry

    for k, ref in enumerate((beside_a, beside_b)):
        part = functools.partial(step, first=k * seq_len // 2, beside=ref)
        lax.fori_loop(0, seq_len // 2 // block, part, 0)


def first_back_kernel(own, beside, x_ref, grad_hidden, gain, out, sums):
    seq_len, width = own.shape
    block = 64
    sums[...] = jnp.zeros_like(sums)

    def step(i, carry):
        rows = at(i * block, block)
        grad = own[rows, :] + beside[rows, :].astype(f32)
        normal, inverse = normal_of(x_ref[rows, :].astype(f32))
        sums[0:1, :] += jnp.sum(grad * normal, axis=0, keepdims=True)
        sums[1:2, :] += jnp.sum(grad, axis=0, keepdims=True)
        out[rows, :] = grad_hidden[rows, :] + norm_back(grad, normal, inverse, gain[...])
        return carry

    lax.fori_loop(0, seq_len // block, step, 0)


def place_attention_kernel(count, place, *refs):
    mine, got, out = refs[:count], refs[count : 2 * count], refs[2 * count]
    core = place[0]
    rows = out.shape[0]
    width = out.shape[1] // 3
    half = width // 2
    here = at(core * rows, rows)
    for p in range(count):
        for part in range(3):
            cols = slice(part * LANES, (part + 1) * LANES)
            base = part * width + p * LANES
            out[:, lanes(core * half + base, LANES)] = mine[p][here, cols].astype(f32)
            out[:, lanes((1 - core) * half + base, LANES)] = got[p][here, cols].astype(f32)


def place_halves_kernel(place, *refs):
    mine, got, outs = refs[0], refs[1], refs[2:]
    core = place[0]
    rows = outs[0].shape[0]
    half = outs[0].shape[1] // 2
    for i, out in enumerate(outs):
        here = at(core * rows + i * 2 * rows, rows)
        out[:, lanes(core * half, half)] = mine[here, :].astype(f32)
        out[:, lanes((1 - core) * half, half)] = got[here, :].astype(f32)


def tie(value, *others):
    return lax.optimization_barrier((value, *others))[0]


def build(dp_size, mp_size):
    total = dp_size * mp_size
    chip_bits = []
    bit = 2 * mp_size
    while bit < total:
        chip_bits.append(bit)
        bit *= 2
    core_bit = mp_size
    near_bit = 1
    far_bits = []
    bit = 2
    while bit < mp_size:
        far_bits.append(bit)
        bit *= 2
    chips = dp_size // 2

    def flip(value, bit):
        return lax.ppermute(value, AXES, [(i, i ^ bit) for i in range(total)])

    def add(a, b):
        return a.astype(f32) + b.astype(f32)

    def add_low(a, b):
        return add(a, b).astype(bf16)

    class Line:
        def __init__(self):
            self.last = []
            self.open = {}

        def end(self, *values):
            for v in values:
                self.open.pop(id(v), None)

        def after(self, value, *waits):
            self.end(value, *waits)
            waits = list(waits) + self.last
            return tie(value, *waits) if waits else value

        def wait(self, *transfers):
            self.end(*transfers)
            self.last = self.last + list(transfers)

        def send(self, value, bit):
            result = flip(self.after(value), bit)
            self.open[id(result)] = (result, bit)
            return result

        def kernel(self, name, kernel, outs, scalars, *args, wait=(), scratch=()):
            self.end(*args)
            args = (self.after(args[0], *wait),) + args[1:]
            result = run(name, kernel, outs, scalars, *args, scratch=scratch)
            self.last = [result[0] if isinstance(result, (tuple, list)) else result]
            return result

        def op(self, function, *args):
            self.end(*args)
            result = function(self.after(args[0]), *args[1:])
            self.last = [result[0] if isinstance(result, (tuple, list)) else result]
            return result

    two = len(chip_bits) == 2

    class Gather:
        def __init__(self, line, piece):
            self.line, self.piece = line, piece
            if two:
                self.x = line.send(piece, chip_bits[0])
                self.y = line.send(piece, chip_bits[1])
            else:
                held = [line.after(piece)]
                for bit in chip_bits:
                    held = held + [flip(value, bit) for value in held]
                self.all = held

        def turn(self):
            if two:
                half = self.piece.shape[0] // 2
                self.line.wait(self.x, self.y)
                low = self.line.op(lambda v: v[:half], self.x)
                self.low = self.line.send(low, chip_bits[1])
                high = self.line.op(lambda v: v[half:], self.y)
                self.high = self.line.send(high, chip_bits[0])

        def wait(self):
            if two:
                self.line.wait(self.low, self.high)

        def send_first(self, bit):
            if two:
                return [self.line.send(v, bit) for v in (self.x, self.y)]
            return [flip(v, bit) for v in self.all[1:]]

        def send_last(self, bit):
            if two:
                corner = self.line.op(lambda a, b: jnp.concatenate([a, b]), self.low, self.high)
                return [self.line.send(corner, bit)]
            return []

        def pieces(self):
            return [self.piece, self.x, self.y, self.low, self.high] if two else self.all

    class Scatter:
        def __init__(self, line, parts):
            self.line, self.parts = line, parts
            if two:
                self.low = line.send(parts[3], chip_bits[0])
                self.high = line.send(parts[4], chip_bits[1])

        def turn(self):
            if two:
                _, to_x, to_y, low, high = self.parts
                half = low.shape[0]
                self.line.wait(self.low, self.high)
                to_y = self.line.op(lambda v, g: v.at[:half].set(add_low(v[:half], g)), to_y, self.low)
                self.y = self.line.send(to_y, chip_bits[1])
                to_x = self.line.op(lambda v, g: v.at[half:].set(add_low(v[half:], g)), to_x, self.high)
                self.x = self.line.send(to_x, chip_bits[0])

        def close(self):
            if two:
                return self.line.op(
                    lambda own, a, b: (add(own, a) + b.astype(f32)).astype(bf16),
                    self.parts[0],
                    self.x,
                    self.y,
                )
            held = list(self.parts)
            for bit in reversed(chip_bits):
                middle = len(held) // 2
                held = [add_low(a, flip(b, bit)) for a, b in zip(held[:middle], held[middle:])]
            return held[0]

    class OverMp:
        def __init__(self, line, share):
            self.line = line
            size = share.shape[0] // 2
            self.upper = lax.axis_index("mp") % 2
            send = line.op(lambda v: lax.dynamic_slice_in_dim(v, (1 - self.upper) * size, size, axis=0), share)
            self.keep = lax.dynamic_slice_in_dim(share, self.upper * size, size, axis=0)
            self.got = line.send(send, near_bit)

        def turn(self):
            value = self.line.op(add_low, self.keep, self.got)
            for bit in far_bits[:-1]:
                value = add_low(value, flip(value, bit))
            self.keep = value
            self.got = self.line.send(value, far_bits[-1])

        def back(self):
            self.keep = self.line.op(add_low, self.keep, self.got)
            self.got = self.line.send(self.keep, near_bit)

        def close(self):
            def joined(keep, got):
                low = jnp.where(self.upper == 0, keep, got)
                return jnp.concatenate([low, jnp.where(self.upper == 0, got, keep)])

            return self.line.op(joined, self.keep, self.got)

    class SumAll:
        def __init__(self, line, value):
            self.line, self.value, self.bit = line, value, 1
            self.got = line.send(value, 1)

        def turn(self):
            if self.bit < total:
                self.value = self.line.op(jnp.add, self.value, self.got)
                self.bit *= 2
                if self.bit < total:
                    self.got = self.line.send(self.value, self.bit)

        def close(self):
            while self.bit < total:
                self.turn()
            return self.value

    def on_device(
        block_in,
        cotangent,
        segment_ids,
        granularity,
        w_qkv,
        w_out,
        w_up,
        w_down,
        norm1_gain,
        norm1_bias,
        norm2_gain,
        norm2_bias,
    ):
        seq_len, width = block_in.shape
        rows = width // dp_size
        units = w_up.shape[1]
        half_units = units // 2
        half = width // 2
        dp = lax.axis_index("dp")
        mp = lax.axis_index("mp")
        core = dp % 2
        chip = dp // 2
        span = 2 * rows
        order = jnp.stack([chip ^ j for j in range(chips)]).astype(jnp.int32)
        place = jnp.concatenate([core[None].astype(jnp.int32), order * span])
        chunks = HEADS // 2 // PAIR
        chunk_cols = 3 * LANES
        gain1, bias1 = norm1_gain[None], norm1_bias[None]
        gain2, bias2 = norm2_gain[None], norm2_bias[None]
        line = Line()

        def parts_shapes(cols):
            if span % 128 == 0 and chips == 4:
                return [shape((span, cols))] * 3 + [shape((rows, cols))] * 2
            return [shape((width, cols))]

        def by_chip(parts):
            if len(parts) > 1:
                return parts
            return [lax.dynamic_slice_in_dim(parts[0], place[1 + j], span, axis=0) for j in range(chips)]

        def ff_parts(*groups):
            if span % 128 == 0 and chips == 4:
                return ff_weight(order, chips, *groups)
            blocks = width // 256
            parts = ff_weight(jnp.arange(blocks, dtype=jnp.int32), blocks, *groups)
            sides = [
                by_chip([jnp.concatenate([v[i * 256 : (i + 1) * 256] for v in parts])]) for i in range(2)
            ]
            return [jnp.concatenate(v) for v in zip(*sides)]

        w_down_t = w_down.T
        qkv_other = line.send(w_qkv, core_bit)
        small = jnp.concatenate([segment_ids, jnp.broadcast_to(granularity[:, None], (mp_size, seq_len))])
        small_other = line.send(small, core_bit)
        x_other = line.send(block_in, core_bit)
        if units == width:
            rest = jnp.concatenate([w_out, w_up, w_down_t])
        else:
            rest = jnp.concatenate([w_out, jnp.concatenate([w_up, w_down_t], axis=1)])
        rest_other = line.send(rest, core_bit)

        qkv_pieces = line.kernel(
            "cut_attention",
            cut_attention_kernel,
            [shape((span, chunk_cols))] * chunks,
            [place],
            w_qkv,
            qkv_other,
            wait=(small_other,),
        )
        heads = [Gather(line, qkv_pieces[0])]
        cot_near = line.send(cotangent, near_bit)
        normed1 = line.kernel(
            "norm",
            norm_kernel,
            shape((2 * seq_len, width)),
            [],
            block_in,
            x_other,
            gain1,
            bias1,
        )
        out_piece, out_piece_got, ff_piece = line.kernel(
            "cut_rest",
            cut_rest_kernel,
            [shape((span, half))] * 2 + [shape((2 * span, half_units))],
            [place],
            w_out,
            w_up,
            w_down_t,
            rest_other,
        )
        heads.append(Gather(line, qkv_pieces[1]))
        cosine, sine = rotary_tables(seq_len, HEAD_DIM)
        last = mp_size // 2 - 1

        qkv_wide, qkv_low, contexts, logs = [], [], [], []

        def attend(p):
            a, b, c, d = line.kernel(
                "attend",
                functools.partial(attend_kernel, chips, seq_len),
                [
                    shape((width, chunk_cols)),
                    shape((2 * seq_len, chunk_cols)),
                    shape((2, seq_len, LANES)),
                    shape((2 * seq_len, HEAD_DIM), f32),
                ],
                [place],
                normed1,
                cosine,
                sine,
                seg_col,
                seg_row,
                *heads[p].pieces(),
            )
            qkv_wide.append(a)
            qkv_low.append(b)
            contexts.append(c)
            logs.append(d)

        heads[0].turn()

        def from_small(own, other):
            segments = jnp.stack([own[0], other[0]])
            levels = jnp.stack([own[1:, 0], other[1:, 0]])
            ends = BLOCK * jnp.power(2, levels)
            ends = jnp.stack([ends[0, mp], ends[1, mp], ends[0, mp ^ 1], ends[1, mp ^ 1]])
            starts = [(mp ^ (2 * k)) * units + core * half_units for k in range(mp_size // 2)]
            limits = (ends[None, :] - jnp.stack(starts)[:, None]).astype(jnp.int32)
            return limits, segments[:, :, None], segments[:, None, :]

        limits, seg_col, seg_row = line.op(from_small, small, small_other)
        heads[1].turn()
        heads[0].wait()
        line.wait(cot_near)
        slices = [ff_piece]
        for bit in far_bits:
            slices = slices + [line.send(v, bit) for v in slices]
        heads.append(Gather(line, qkv_pieces[2]))
        attend(0)
        heads[1].wait()
        heads[2].turn()
        outs = Gather(line, out_piece)
        attend(1)
        heads[2].wait()
        ctx_near = [line.send(c[1], core_bit) for c in contexts]
        outs.turn()
        line.wait(*ctx_near)
        outs_other = [out_piece_got] + outs.send_first(core_bit)
        attend(2)
        outs.wait()
        line.wait(*outs_other[1:], *slices[1:])
        ffs = {0: Gather(line, slices[0])}
        ctx_near.append(line.send(contexts[2][1], core_bit))
        outs_other += outs.send_last(core_bit)
        out_mine, out_got = line.kernel(
            "join",
            functools.partial(join_kernel, chips, len(outs.pieces())),
            [shape((width, half))] * 2,
            [place],
            *outs.pieces(),
            *outs_other,
            wait=(ctx_near[2],),
        )
        cot_both = line.send(cot_near, core_bit)
        cot_core = line.send(cotangent, core_bit)
        hidden1, normed2, context = line.kernel(
            "out",
            functools.partial(out_kernel, chunks),
            [shape((seq_len, width), f32), shape((seq_len, width)), shape((seq_len, width))],
            [place],
            block_in,
            *[c[0] for c in contexts],
            *ctx_near,
            out_mine,
            out_got,
            gain2,
            bias2,
        )

        line.wait(cot_both, cot_core)
        norm_near = line.send(normed2, near_bit)
        norm_core = line.send(normed2, core_bit)
        ffs[0].turn()
        ffs[0].wait()
        line.wait(norm_core)
        for k in range(1, last + 1):
            ffs[k] = Gather(line, slices[k])
        cot_rows = [cotangent, cot_core, cot_near, cot_both]
        outs_ff = [shape((seq_len, half_units))] * 4
        wide_ff = [shape((width, half_units))] * 2
        acts, grads, ups, downs = {}, {}, {}, {}

        def ff_own(k):
            act_a, act_b, grad_a, grad_b, up, down = line.kernel(
                "ff_own",
                functools.partial(ff_act_kernel, chips, k),
                outs_ff + wide_ff,
                [place, limits],
                normed2,
                norm_core,
                *cot_rows[:2],
                *ffs[k].pieces(),
            )
            acts[k] = [act_a, act_b]
            grads[k] = [grad_a, grad_b]
            ups[k] = up
            downs[k] = down

        def ff_near(k):
            act_a, act_b, grad_a, grad_b = line.kernel(
                "ff_near",
                functools.partial(ff_act_kernel, 0, k),
                outs_ff,
                [place, limits],
                norm_near,
                *norm_both,
                *cot_rows[2:],
                ups[k],
                downs[k],
            )
            acts[k] += [act_a, act_b]
            grads[k] += [grad_a, grad_b]

        def ff_grads(k):
            lefts = [line.after(normed2), norm_core, norm_near, norm_joined]
            parts = ff_parts(lefts, cot_rows, acts[k], grads[k])
            line.last = [parts[0]]
            return parts

        def rows_back(name, lefts, i, weights, kind, count=1):
            outs = [shape((seq_len // count, width), kind)] * count
            result = line.kernel(
                name,
                functools.partial(rows_back_kernel, len(weights), 0),
                outs,
                [],
                *[v[i] for v in lefts.values()],
                *weights.values(),
            )
            return result[0] if count == 1 else result

        def add_halves(a, low, high):
            middle = a.shape[0] // 2
            return jnp.concatenate([add_low(a[:middle], low), add_low(a[middle:], high)])

        ff_own(0)
        line.wait(norm_near)
        arrived = line.after(norm_near)
        middle = seq_len // 2
        norm_both = [line.send(v, core_bit) for v in (arrived[:middle], arrived[middle:])]
        line.wait(*norm_both)
        ff_near(0)
        norm_joined = line.op(lambda a, c: jnp.concatenate([a, c]), *norm_both)
        parts = ff_grads(0)
        for k in range(1, last + 1):
            ffs[k].turn()
        scatters = {0: Scatter(line, parts)}
        ctx_far = []
        for k in range(1, last + 1):
            if k == 1:
                ffs[1].wait()
                ctx_far = [line.send(c[0], core_bit) for c in contexts]
            ff_own(k)
            line.wait(*ctx_far)
            if k == 1:
                scatters[0].turn()
            ff_near(k)
        back_both = rows_back("ff_back", grads, 3, ups, bf16, 2)
        back_both = [line.send(v, core_bit) for v in back_both]
        back_near = rows_back("ff_back", grads, 2, ups, f32)
        back_near = line.op(add_halves, back_near, *back_both)
        back_near = line.send(back_near, near_bit)
        fore_both = rows_back("ff_fore", acts, 3, downs, bf16, 2)
        fore_near = rows_back("ff_fore", acts, 2, downs, f32)
        held = {}
        for k in range(1, last + 1):
            parts = ff_grads(k)
            if k == 1:
                held[0] = scatters[0].close()
            scatters[k] = Scatter(line, parts)
        back_beside = rows_back("ff_back", grads, 1, ups, bf16, 2)
        back_beside = [line.send(v, core_bit) for v in back_beside]
        back_own = rows_back("ff_back", grads, 0, ups, f32)

        grad_hidden1, grad_attn, sums2 = line.kernel(
            "second_back",
            second_back_kernel,
            [shape((seq_len, width), f32), shape((seq_len, width)), shape((8, width), f32)],
            [],
            back_own,
            *back_beside,
            back_near,
            hidden1,
            cotangent,
            gain2,
        )
        for k in range(1, last + 1):
            scatters[k].turn()
        fore_both = [line.send(v, core_bit) for v in fore_both]
        keep, send, grad_send = line.kernel(
            "out_back",
            out_back_kernel,
            [shape((seq_len, half))] * 3,
            [place],
            grad_attn,
            out_mine,
            out_got,
        )
        context_got = line.send(send, core_bit)
        line.wait(context_got, *fore_both)
        fore_near = line.op(add_halves, fore_near, *fore_both)
        fore_near = line.send(fore_near, near_bit)
        grad_got = line.send(grad_send, core_bit)
        grad_low, qkv_scatters = [], []

        def attend_back(p):
            low, *parts = line.kernel(
                "attend_back",
                functools.partial(attend_back_kernel, p),
                [shape((2 * seq_len, chunk_cols))] + parts_shapes(chunk_cols),
                [place],
                qkv_low[p],
                logs[p],
                keep,
                context_got,
                normed1,
                cosine,
                sine,
                seg_col,
                seg_row,
                scratch=[pltpu.VMEM((seq_len, HEAD_DIM), f32)] * 3,
            )
            grad_low.append(low)
            return by_chip(parts)

        parts = attend_back(0)
        line.wait(grad_got)
        qkv_scatters.append(Scatter(line, parts))
        out_parts = line.kernel(
            "out_weight",
            functools.partial(out_weight_kernel, chunks),
            parts_shapes(half),
            [place],
            context,
            grad_attn,
            grad_got,
            *[c[1] for c in contexts],
            *ctx_far,
            scratch=[pltpu.VMEM((seq_len, width), bf16)],
        )
        for k in range(1, last + 1):
            held[k] = scatters[k].close()
        far_got = line.send(held[last], far_bits[0]) if len(far_bits) == 1 else None
        qkv_scatters[0].turn()
        parts = attend_back(1)
        line.wait(fore_near)
        qkv_scatters.append(Scatter(line, parts))
        first, second = qkv_scatters
        first_z = OverMp(line, first.close())
        second.turn()
        parts = attend_back(2)
        if len(far_bits) == 1:
            line.wait(far_got)
        second_share = second.close()
        third = Scatter(line, parts)
        back_other = line.kernel(
            "qkv_back",
            functools.partial(rows_back_kernel, chunks, seq_len),
            [shape((seq_len, width))],
            [],
            *grad_low,
            *qkv_wide,
        )[0]
        back_mine = line.kernel(
            "qkv_back",
            functools.partial(rows_back_kernel, chunks, 0),
            [shape((seq_len, width), f32)],
            [],
            *grad_low,
            *qkv_wide,
        )[0]
        first_z.turn()
        second_z = OverMp(line, second_share)
        third.turn()
        back_other = line.send(back_other, core_bit)
        grad_input, sums1 = line.kernel(
            "first_back",
            first_back_kernel,
            [shape((seq_len, width), f32), shape((8, width), f32)],
            [],
            back_mine,
            back_other,
            block_in,
            grad_hidden1,
            gain1,
        )
        second_z.turn()
        third_share = third.close()
        fourth = Scatter(line, by_chip(out_parts))
        third_z = OverMp(line, third_share)
        first_z.back()
        fourth.turn()
        third_z.turn()
        first_share = first_z.close()
        fourth_z = OverMp(line, fourth.close())
        second_z.back()
        sums = SumAll(line, jnp.concatenate([sums1[:2], sums2[:2]]))
        fore_beside = rows_back("ff_fore", acts, 1, downs, bf16)
        fourth_z.turn()
        third_z.back()
        sums.turn()
        second_share = second_z.close()
        fore_own = rows_back("ff_fore", acts, 0, downs, f32)
        sums.turn()
        third_share = third_z.close()
        if len(far_bits) == 1:
            ff_share = line.op(add_low, held[0], far_got)
        else:
            held = [held[k] for k in range(len(slices))]
            for bit in reversed(far_bits):
                middle = len(held) // 2
                held = [add_low(a, flip(c, bit)) for a, c in zip(held[:middle], held[middle:])]
            ff_share = held[0]
        sums.turn()
        fourth_z.back()
        first_got = line.send(first_share, core_bit)
        second_got = line.send(second_share, core_bit)
        third_got = line.send(third_share, core_bit)
        grad_w_qkv = line.kernel(
            "place_qkv",
            functools.partial(place_attention_kernel, chunks),
            shape((rows, 3 * width), f32),
            [place],
            first_share,
            second_share,
            third_share,
            first_got,
            second_got,
            third_got,
        )
        fore_beside = line.send(fore_beside, core_bit)
        ff_share_got = line.send(ff_share, core_bit)
        sums.turn()

        def finish(base, own, near, beside):
            return (base + own + near.astype(f32) + beside.astype(f32)).astype(bf16)

        block_out = line.op(finish, hidden1, fore_own, fore_near, fore_beside)
        grad_w_up, grad_w_down = line.kernel(
            "place_ff",
            place_halves_kernel,
            [shape((rows, units), f32)] * 2,
            [place],
            ff_share,
            ff_share_got,
        )
        grad_w_down = grad_w_down.T
        sums = sums.close()
        out_share = fourth_z.close()
        out_share_got = line.send(out_share, core_bit)
        grad_w_out = line.kernel(
            "place_out",
            place_halves_kernel,
            [shape((rows, width), f32)],
            [place],
            out_share,
            out_share_got,
        )[0]
        return (
            block_out,
            grad_input,
            grad_w_qkv,
            grad_w_out,
            grad_w_up,
            grad_w_down,
            sums[0],
            sums[1],
            sums[2],
            sums[3],
        )

    return on_device


def solution(mesh):
    return jax.shard_map(
        build(mesh.shape["dp"], mesh.shape["mp"]),
        mesh=mesh,
        in_specs=(
            P(("dp", "mp"), None),
            P(("dp", "mp"), None),
            P(("dp", "mp"), None),
            P("dp"),
            P("dp", None),
            P("dp", None),
            P("dp", "mp"),
            P("mp", "dp"),
            P(),
            P(),
            P(),
            P(),
        ),
        out_specs=(
            P(("dp", "mp"), None),
            P(("dp", "mp"), None),
            P("dp", None),
            P("dp", None),
            P("dp", "mp"),
            P("mp", "dp"),
            P(),
            P(),
            P(),
            P(),
        ),
        check_vma=False,
    )
```
